256 devices in a mesh: dp: 16 (over y, z_lo, core), tensor: 16 (over x, z_hi).
Axes of the slice: x: 4, y: 4, z: 8 (z_hi: 4, z_lo: 2; z = z_hi * 2 + z_lo), core: 2. Of those that a mesh axis runs over, the one named last changes fastest.
Arguments:
- inputs: bfloat16 [32768, 1664], P(('dp', 'tensor')), may hold values from -24 to 24
- gain: bfloat16 [1664], replicated, may hold values from 0.099609375 to 1.8984375
- w_up: bfloat16 [1664, 6400], P(None, 'tensor'), may hold values from -0.15625 to 0.15625
- w_down: bfloat16 [6400, 1664], P('tensor'), may hold values from -0.078125 to 0.078125
- upstream: bfloat16 [32768, 1664], P(('dp', 'tensor')), may hold values from -24 to 24
Outputs:
- input_grad: bfloat16 [32768, 1664], P(('dp', 'tensor'))
- up_grad: float32 [1664, 6400], P('dp', 'tensor')
- down_grad: float32 [6400, 1664], P('tensor', 'dp')
The draws below stay inside these ranges and needn't reach their ends.
All inputs are finite; a program needn't handle non-finite values.
Results may differ from the reference program's by a relative error of at most 0.022.
Values may be sent and summed in bfloat16 or wider, within the bound.
A program may use at most 64 MiB of HBM per device.

```python
import jax
import jax.numpy as jnp
from jax import lax

D = 1664
FF = 6400
TOK_DEV = 128
TOKENS = 32768
N_DP = 16
N_TENSOR = 16


def strengthened(entries, rng, source, target, blocks, factor):
    owner, partner = [(jnp.arange(entries.shape[axis_at]) // (entries.shape[axis_at] // blocks)).reshape([-1 if axis == axis_at else 1 for axis in range(entries.ndim)]) for axis_at in (source, target)]
    chosen = jax.random.permutation(rng, blocks)[partner]
    strong = (owner == chosen) | (owner == (partner + blocks // 2) % blocks)
    return jnp.where(strong, factor * entries, entries)


def levels(key, shape, shards, least, high):
    level, own = 1.0, jax.random.fold_in(key, 6)
    for dim, parts in shards:
        steps = jnp.exp(jax.random.uniform(jax.random.fold_in(own, dim), (parts,), jnp.float32, least / len(shards), high / len(shards)))
        level = level * jnp.repeat(steps, shape[dim] // parts).reshape([-1 if axis == dim else 1 for axis in range(len(shape))])
    return level


def centred(stream_key, shape, deviation, bound, cuts=(), dtype=jnp.bfloat16):
    array = deviation * jax.random.normal(stream_key, shape, jnp.float32)
    if cuts:
        array = array * levels(stream_key, shape, cuts, -0.22, 0.18)
    return jnp.clip(array, -bound, bound).astype(dtype)


def bell_draw_with(rng, shape, width, bound, shards, heavy, dtype=jnp.bfloat16):
    values = width * jax.random.normal(rng, shape, jnp.float32)
    if shards:
        values = values * levels(rng, shape, shards, -0.22, 0.18)
    return jnp.clip(strengthened(values, jax.random.fold_in(rng, 3), *heavy), -bound, bound).astype(dtype)


def setup_inputs(seed: int = 0) -> dict:
    splits = jax.random.split(jax.random.key(seed), 6)
    inputs = bell_draw_with(splits[0], (TOKENS, D), 1.0, 24.0, ((0, 256),), (0, 1, 128, 5.5))
    gain = jnp.clip(1.0 + 0.18 * jax.random.normal(splits[1], (D,), jnp.float32), 0.099609375, 1.8984375).astype(jnp.bfloat16)
    w_up = centred(splits[2], (D, FF), D ** -0.5, 0.15625, ((1, 16),))
    w_down = centred(splits[3], (FF, D), FF ** -0.5, 0.078125, ((0, 16),))
    upstream = bell_draw_with(splits[4], (TOKENS, D), 1.0, 24.0, ((0, 256),), (0, 1, 128, 5.5))
    return dict(inputs=inputs, gain=gain, w_up=w_up, w_down=w_down, upstream=upstream)


norm_eps = 1e-06

def gelu_parts(pre):
    cdf = 0.5 * (1.0 + lax.erf(pre * 0.7071067811865476))
    pdf = jnp.exp(-0.5 * pre * pre) * 0.3989422804014327
    return (pre * cdf, cdf + pre * pdf)

def round_keep(value):
    return lax.optimization_barrier(value.astype(jnp.bfloat16)).astype(jnp.float32)

def reference(inputs, gain, w_up, w_down, upstream):
    group = TOK_DEV * N_TENSOR
    slice_width = FF // N_TENSOR
    grad_scale = float(TOKENS) ** (-0.5)
    clips_in = inputs.reshape(N_DP, group, D)
    clips_up = upstream.reshape(N_DP, group, D)
    gain_wide = gain.astype(jnp.float32)
    up_blocks = jnp.transpose(w_up.reshape(D, N_TENSOR, slice_width), (1, 0, 2))

    def one_clip(carry, pair):
        clip_in, clip_up = pair
        inputs_wide = clip_in.astype(jnp.float32)
        inv_rms = lax.rsqrt(lax.optimization_barrier(jnp.mean(inputs_wide * inputs_wide, axis=-1, keepdims=True)) + norm_eps)
        unit_rows = inputs_wide * inv_rms
        normed = (unit_rows * gain_wide).astype(jnp.bfloat16)
        pre = jnp.dot(normed, w_up, preferred_element_type=jnp.float32)
        hidden_full, slope = gelu_parts(pre)
        hidden = hidden_full.astype(jnp.bfloat16)
        dhidden = jnp.dot(clip_up, w_down.T, preferred_element_type=jnp.float32)
        dpre = (dhidden * slope).astype(jnp.bfloat16)
        down_part = round_keep(jnp.dot(hidden.T, clip_up, preferred_element_type=jnp.float32) * grad_scale)
        up_part = round_keep(jnp.dot(normed.T, dpre, preferred_element_type=jnp.float32) * grad_scale)
        dpre_blocks = jnp.transpose(dpre.reshape(group, N_TENSOR, slice_width), (1, 0, 2))

        def add_block(total, block_pair):
            dpre_block, weight_block = block_pair
            term = jnp.dot(dpre_block, weight_block.T, preferred_element_type=jnp.float32)
            return (total + round_keep(term), None)
        dnormed, unused = lax.scan(add_block, jnp.zeros((group, D), jnp.float32), (dpre_blocks, up_blocks))
        dunit = dnormed * gain_wide
        project = lax.optimization_barrier(jnp.mean(dunit * unit_rows, axis=-1, keepdims=True))
        grad_rows = clip_up.astype(jnp.float32) + inv_rms * (dunit - unit_rows * project)
        return ((carry[0] + up_part, carry[1] + down_part), grad_rows.astype(jnp.bfloat16))
    start = (jnp.zeros((D, FF), jnp.float32), jnp.zeros((FF, D), jnp.float32))
    sums, grads = lax.scan(one_clip, start, (clips_in, clips_up))
    return (grads.reshape(TOKENS, D), sums[0], sums[1])
```

```python
import jax
import jax.numpy as jnp
from jax import lax
from jax.experimental import pallas as pl
from jax.experimental.pallas import tpu as pltpu
from jax.sharding import PartitionSpec as P

MESH = pl.DeviceIdType.MESH
F32, BF16 = jnp.float32, jnp.bfloat16

norm_eps = 1e-06
D = 1664
TOK = 128
GROUP = 2 * TOK
T = 4 * GROUP
HALF = 208
HID = 4 * HALF
WIN = 512
CHUNKS = ((0, 64), (64, 48), (112, 48), (160, 48))
N_SEM = 80
GRAD_SCALE = float(32768) ** (-0.5)

MIRROR = {0: 0, 1: 3, 2: 2, 3: 1}


def gelu_parts(pre):
    cdf = 0.5 * (1.0 + lax.erf(pre * 0.7071067811865476))
    pdf = jnp.exp(-0.5 * pre * pre) * 0.3989422804014327
    return (pre * cdf, cdf + pre * pdf)


def place(x, y, z, c):
    x, y, z = (x + 8) % 4, (y + 8) % 4, (z + 16) % 8
    return (y * 4 + (z % 2) * 2 + c, x * 4 + z // 2)


def kernel(
    x_ref, up_ref, gain_ref, w_ref, grad_ref, out_ref,
    tok_n, tok_u, w, hid, dpre, g, yo_in, ya_st, nb_in, ysum, z1_in, z2_st, z2_in, total, fin_st, fin_in,
    dn, dn_sib, dn_st, dn_in, ss, rs, local_sem,
):
    dp, tensor = lax.axis_index("dp"), lax.axis_index("tensor")
    y, zl, c = dp // 4, (dp // 2) % 2, dp % 2
    x, z = tensor // 4, (tensor % 4) * 2 + zl
    step_out = 2 * zl - 1
    sib = place(x, y, z, 1 - c)
    xr, xl = place(x + 1, y, z, c), place(x - 1, y, z, c)
    x_far = place(x + 2, y, z, c)
    yr, yl = place(x, y + 1, z, c), place(x, y - 1, z, c)
    z_out, z_in = place(x, y, z + step_out, c), place(x, y, z - step_out, c)
    z_cross = place(x, y, z - step_out, 1 - c)
    z_far = {1: place(x, y, z + 2 * step_out, c), 2: place(x, y, z + 4, c), 3: place(x, y, z - 2 * step_out, c)}
    kind_out, kind_in = zl, 1 - zl
    mine = zl

    own_w = pltpu.make_async_copy(w_ref, w.at[:, pl.ds(0, HALF)], local_sem)
    own_w.start()
    barrier = pltpu.get_barrier_semaphore()
    peers = [sib, xr, xl, x_far, yr, yl, z_out, z_in, z_cross, z_far[1], z_far[2], z_far[3]]
    for peer in peers:
        pl.semaphore_signal(barrier, inc=1, device_id=peer, device_id_type=MESH)

    copies = {}

    def send(key, src, dst, device):
        i = len(copies)
        copies[key] = pltpu.make_async_remote_copy(
            src_ref=src, dst_ref=dst, send_sem=ss.at[i], recv_sem=rs.at[i], device_id=device, device_id_type=MESH
        )
        copies[key].start()

    def recv(*keys):
        for key in keys:
            copies[key].wait_recv()

    def tok_rows(group, core, first=0, rows=TOK):
        return pl.ds(pl.multiple_of(group * GROUP + core * TOK + first, 16), rows)

    def norm(i, _):
        r = pl.ds(pl.multiple_of(i * 16, 16), 16)
        wide = x_ref[r].astype(F32)
        inv = lax.rsqrt(jnp.mean(wide * wide, axis=-1, keepdims=True) + norm_eps)
        to = pl.ds(pl.multiple_of(c * TOK + i * 16, 16), 16)
        tok_n[to] = (wide * inv * gain_ref[...]).astype(BF16)
        tok_u[to] = up_ref[r]
        return 0

    lax.fori_loop(0, TOK // 16, norm, 0)
    pl.semaphore_wait(barrier, len(peers))

    toks = {"u": tok_u, "n": tok_n}
    own = tok_rows(0, c)
    for a in ("u", "n"):
        send((a, "r"), toks[a].at[own], toks[a].at[tok_rows(3, c)], xr)
        send((a, "l"), toks[a].at[own], toks[a].at[tok_rows(1, c)], xl)
        send((a, "s0"), toks[a].at[own], toks[a].at[own], sib)
    own_w.wait()

    def chunk(slot, i):
        first, rows = CHUNKS[i]
        return pl.ds(slot * HALF + first, rows)

    for i in range(4):
        send(("w0", i), w.at[:, chunk(0, i)], w.at[:, chunk(1, i)], z_out)

    def pass_neighbours(a):
        recv((a, "r"))
        send((a, "fr"), toks[a].at[tok_rows(3, c, 0, 64)], toks[a].at[tok_rows(2, c, 0, 64)], xr)
        send((a, "s3"), toks[a].at[tok_rows(3, c)], toks[a].at[tok_rows(3, c)], sib)
        recv((a, "l"))
        send((a, "fl"), toks[a].at[tok_rows(1, c, 64, 64)], toks[a].at[tok_rows(2, c, 64, 64)], xl)
        send((a, "s1"), toks[a].at[tok_rows(1, c)], toks[a].at[tok_rows(1, c)], sib)

    def pass_opposite(a):
        recv((a, "fr"), (a, "fl"))
        send((a, "s2"), toks[a].at[tok_rows(2, c)], toks[a].at[tok_rows(2, c)], sib)

    def pass_w1(i):
        recv(("w0", i))
        send(("w1", i), w.at[:, chunk(1, i)], w.at[:, chunk(3, i)], z_in)

    def pass_w3(i):
        recv(("w1", i))
        send(("w3", i), w.at[kind_in, chunk(3, i)], w.at[kind_in, chunk(2, i)], z_out)

    def pass_w2(i):
        recv(("w3", i))
        send(("w2", i), w.at[kind_out, chunk(2, i)], w.at[kind_out, chunk(2, i)], z_in)

    def forward(slot, group):
        r = pl.ds(slot * HALF, HALF)
        t = pl.ds(pl.multiple_of(group * GROUP, GROUP), GROUP)
        nt = (((1,), (1,)), ((), ()))
        pre = lax.dot_general(w[0, r], tok_n[t], nt, preferred_element_type=F32)
        dhidden = lax.dot_general(w[1, r], tok_u[t], nt, preferred_element_type=F32)
        hidden, slope = gelu_parts(pre)
        hid[r, t] = hidden.astype(BF16)
        dpre[r, t] = (dhidden * slope).astype(BF16)

    def forward_all(slot):
        def one(group, _):
            forward(slot, group)
            return 0

        lax.fori_loop(0, 4, one, 0)

    def grads(slot):
        r = pl.ds(slot * HALF, HALF)

        def columns(cols):
            up = jnp.dot(dpre[r], tok_n[:, cols], preferred_element_type=F32)
            g[0, r, cols] = (up * GRAD_SCALE).astype(BF16)
            down = jnp.dot(hid[r], tok_u[:, cols], preferred_element_type=F32)
            g[1, r, cols] = (down * GRAD_SCALE).astype(BF16)

        def tile(n, _):
            columns(pl.ds(pl.multiple_of(n * 256, 256), 256))
            return 0

        lax.fori_loop(0, 6, tile, 0)
        columns(pl.ds(1536, 128))

    def window(owner, first=0, cols=WIN):
        return pl.ds(pl.multiple_of(((owner + 8) % 4) * 384 + first, 128), cols)

    def y1(slot):
        r = pl.ds(slot * HALF, HALF)
        send(("yo", slot, 0), g.at[:, r, window(y + 2, 0, 256)], yo_in.at[slot, 0], yr)
        send(("yo", slot, 1), g.at[:, r, window(y + 2, 256, 256)], yo_in.at[slot, 1], yl)
        send(("yd", slot, 0), g.at[:, r, window(y + 1, 256, 256)], nb_in.at[slot, 0, :, :, pl.ds(256, 256)], yr)
        send(("yd", slot, 1), g.at[:, r, window(y - 1, 0, 256)], nb_in.at[slot, 1, :, :, pl.ds(0, 256)], yl)

    def rows16(i):
        return pl.ds(pl.multiple_of(i * 16, 16), 16)

    def y2(slot):
        for way, owner, first, peer in ((0, y + 1, 0, yr), (1, y - 1, 256, yl)):
            recv(("yo", slot, way))
            cols = window(owner, first, 256)

            def add(i, _):
                part = pl.ds(pl.multiple_of(slot * HALF + i * 16, 16), 16)
                here = rows16(i)
                ya_st[slot, way, :, here] = (
                    g[:, part, cols].astype(F32) + yo_in[slot, way, :, here].astype(F32)
                ).astype(BF16)
                return 0

            lax.fori_loop(0, HALF // 16, add, 0)
            send(("ya", slot, way), ya_st.at[slot, way], nb_in.at[slot, way, :, :, pl.ds(first, 256)], peer)

    def y3(slot):
        recv(("yd", slot, 0), ("yd", slot, 1), ("ya", slot, 0), ("ya", slot, 1))
        cols = window(y)

        def add(i, _):
            part = pl.ds(pl.multiple_of(slot * HALF + i * 16, 16), 16)
            here = rows16(i)
            ysum[slot, :, here] = (
                g[:, part, cols].astype(F32)
                + nb_in[slot, 0, :, here].astype(F32)
                + nb_in[slot, 1, :, here].astype(F32)
            ).astype(BF16)
            return 0

        lax.fori_loop(0, HALF // 16, add, 0)
        there = MIRROR[slot]
        send(("z1", there), ysum.at[slot, 1 - mine], z1_in.at[there], z_in)

    def z2(slot):
        recv(("z1", slot))

        def add(i, _):
            here = rows16(i)
            z2_st[slot - 1, here] = (
                ysum[slot, mine, here].astype(F32) + z1_in[slot, here].astype(F32)
            ).astype(BF16)
            return 0

        lax.fori_loop(0, HALF // 16, add, 0)
        send(("z2", slot), z2_st.at[slot - 1], z2_in.at[slot - 1], z_far[slot])

    def back(group):
        t = pl.ds(group * GROUP, GROUP)
        rows = dpre[:, t].T

        def columns(cols):
            part = jnp.dot(rows, w[0, :, cols], preferred_element_type=F32).astype(BF16)
            dn[group, 0, :, cols] = part[:TOK]
            dn[group, 1, :, cols] = part[TOK:]

        def tile(n, _):
            columns(pl.ds(pl.multiple_of(n * 256, 256), 256))
            return 0

        lax.fori_loop(0, 6, tile, 0)
        columns(pl.ds(1536, 128))
        send(("dn", group), dn.at[group, 1 - c], dn_sib.at[group], sib)

    def dn_pass(group, peer):
        recv(("dn", group))

        def add(i, _):
            here = rows16(i)
            dn_st[group - 1, here] = (dn[group, c, here].astype(F32) + dn_sib[group, here].astype(F32)).astype(BF16)
            return 0

        lax.fori_loop(0, TOK // 16, add, 0)
        send(("dx", group), dn_st.at[group - 1], dn_in.at[group - 1], peer)

    pass_neighbours("u")
    pass_w1(0)
    recv(("u", "s0"), ("n", "s0"))
    forward(0, 0)
    pass_neighbours("n")
    pass_w1(1)
    recv(("u", "s1"), ("n", "s1"))
    forward(0, 1)
    pass_w3(0)
    recv(("u", "s3"), ("n", "s3"))
    forward(0, 3)
    pass_w1(2)
    pass_opposite("u")
    pass_w2(0)
    pass_opposite("n")
    pass_w3(1)
    recv(("u", "s2"), ("n", "s2"))
    forward(0, 2)
    pass_w1(3)
    pass_w2(1)
    grads(0)
    y1(0)
    pass_w3(2)
    forward_all(1)
    pass_w2(2)
    pass_w3(3)
    grads(1)
    y1(1)
    y2(0)
    pass_w2(3)
    forward_all(3)
    grads(3)
    y1(3)
    y2(1)
    recv(("w2", 0), ("w2", 1), ("w2", 2), ("w2", 3))
    forward_all(2)
    grads(2)
    y1(2)
    y2(3)
    y3(0)
    back(2)
    back(1)
    y2(2)
    back(3)
    back(0)
    dn_pass(2, x_far)
    dn_pass(1, xr)
    dn_pass(3, xl)
    y3(1)
    y3(3)
    z2(1)
    z2(3)
    y3(2)
    z2(2)

    recv(("dn", 0), ("dx", 1), ("dx", 2), ("dx", 3))

    def finish(i, _):
        here = rows16(i)
        gain = gain_ref[...]
        wide = x_ref[here].astype(F32)
        inv = lax.rsqrt(jnp.mean(wide * wide, axis=-1, keepdims=True) + norm_eps)
        unit = wide * inv
        dnormed = dn[0, c, here].astype(F32) + dn_sib[0, here].astype(F32)
        for k in range(3):
            dnormed += dn_in[k, here].astype(F32)
        dunit = dnormed * gain
        project = jnp.mean(dunit * unit, axis=-1, keepdims=True)
        grad_ref[here] = (up_ref[here].astype(F32) + inv * (dunit - unit * project)).astype(BF16)
        return 0

    lax.fori_loop(0, TOK // 16, finish, 0)

    recv(("z1", 0), ("z2", 1), ("z2", 2), ("z2", 3))
    total[:, pl.ds(WIN, 128)] = jnp.zeros((16, 128), F32)

    def split(i, _):
        here = rows16(i)
        rows = ysum[0, mine, here].astype(F32) + z1_in[0, here].astype(F32)
        for k in range(3):
            rows += z2_in[k, here].astype(F32)
        total[:, pl.ds(0, WIN)] = rows
        for q in range(4):
            turned = pltpu.roll(total[...], (WIN + 128 - 104 * q) - 32 * y, 1)
            fin_st[q, here] = turned[:, :128].astype(BF16)
        return 0

    lax.fori_loop(0, HALF // 16, split, 0)
    me = 2 * zl + c
    for key, device, to in (("sib", sib, 2 * zl + 1 - c), ("in", z_in, 2 * (1 - zl) + c), ("cross", z_cross, 2 * (1 - zl) + 1 - c)):
        send(("f", key), fin_st.at[to], fin_in.at[me], device)

    def keep(i, _):
        fin_in[me, rows16(i)] = fin_st[me, rows16(i)]
        return 0

    lax.fori_loop(0, HALF // 16, keep, 0)
    recv(("f", "sib"), ("f", "in"), ("f", "cross"))

    def store(i, _):
        here = rows16(i)
        for q in range(4):
            out_ref[q, here] = fin_in[q, here].astype(F32)
        return 0

    lax.fori_loop(0, HALF // 16, store, 0)
    for copy in copies.values():
        copy.wait_send()


def body(inputs, gain, w_up, w_down, upstream):
    core = lax.axis_index("dp") % 2
    up_rows = jnp.pad(w_up, ((0, 0), (0, 16)))
    down_rows = jnp.pad(w_down, ((0, 16), (0, 0)))
    w_own = jnp.stack([
        lax.dynamic_slice_in_dim(up_rows, core * HALF, HALF, 1).T,
        lax.dynamic_slice_in_dim(down_rows, core * HALF, HALF, 0),
    ])
    vmem = pl.BlockSpec(memory_space=pltpu.VMEM)
    input_grad, pieces = pl.pallas_call(
        kernel,
        out_shape=(jax.ShapeDtypeStruct((TOK, D), BF16), jax.ShapeDtypeStruct((4, HALF, 128), F32)),
        in_specs=[vmem, vmem, vmem, pl.BlockSpec(memory_space=pl.ANY)],
        out_specs=(vmem, vmem),
        scratch_shapes=[
            pltpu.VMEM((T, D), BF16),
            pltpu.VMEM((T, D), BF16),
            pltpu.VMEM((2, HID, D), BF16),
            pltpu.VMEM((HID, T), BF16),
            pltpu.VMEM((HID, T), BF16),
            pltpu.VMEM((2, HID, D), BF16),
            pltpu.VMEM((4, 2, 2, HALF, 256), BF16),
            pltpu.VMEM((4, 2, 2, HALF, 256), BF16),
            pltpu.VMEM((4, 2, 2, HALF, WIN), BF16),
            pltpu.VMEM((4, 2, HALF, WIN), BF16),
            pltpu.VMEM((4, HALF, WIN), BF16),
            pltpu.VMEM((3, HALF, WIN), BF16),
            pltpu.VMEM((3, HALF, WIN), BF16),
            pltpu.VMEM((16, WIN + 128), F32),
            pltpu.VMEM((4, HALF, 128), BF16),
            pltpu.VMEM((4, HALF, 128), BF16),
            pltpu.VMEM((4, 2, TOK, D), BF16),
            pltpu.VMEM((4, TOK, D), BF16),
            pltpu.VMEM((3, TOK, D), BF16),
            pltpu.VMEM((3, TOK, D), BF16),
            pltpu.SemaphoreType.DMA((N_SEM,)),
            pltpu.SemaphoreType.DMA((N_SEM,)),
            pltpu.SemaphoreType.DMA,
        ],
        compiler_params=pltpu.CompilerParams(
            collective_id=1, has_side_effects=True, vmem_limit_bytes=60 * 2**20
        ),
        name="block_backward",
    )(inputs, upstream, gain.astype(F32).reshape(1, D), w_own)
    up_grad = pieces[:2].reshape(2 * HALF, 128)[:400, :104].T
    down_grad = pieces[2:].reshape(2 * HALF, 128)[:400, :104]
    return input_grad, up_grad, down_grad


def solution(mesh):
    in_specs = (
        P(("dp", "tensor"), None),
        P(),
        P(None, "tensor"),
        P("tensor", None),
        P(("dp", "tensor"), None),
    )
    out_specs = (P(("dp", "tensor"), None), P("dp", "tensor"), P("tensor", "dp"))
    return jax.shard_map(body, mesh=mesh, in_specs=in_specs, out_specs=out_specs, check_vma=False)
```

```python
import jax
import jax.numpy as jnp
from jax import lax
from jax.experimental import pallas as pl
from jax.experimental.pallas import tpu as pltpu
from jax.sharding import PartitionSpec as P

MESH = pl.DeviceIdType.MESH
F32, BF16 = jnp.float32, jnp.bfloat16

norm_eps = 1e-06
D = 1664
TOK = 128
GROUP = 2 * TOK
T = 4 * GROUP
HALF = 208
HID = 4 * HALF
WIN = 512
CHUNKS = ((0, 64), (64, 48), (112, 48), (160, 48))
N_SEM = 88
GRAD_SCALE = float(32768) ** (-0.5)


def gelu_parts(pre):
    cdf = 0.5 * (1.0 + lax.erf(pre * 0.7071067811865476))
    pdf = jnp.exp(-0.5 * pre * pre) * 0.3989422804014327
    return (pre * cdf, cdf + pre * pdf)


def place(x, y, z, c):
    x, y, z = (x + 8) % 4, (y + 8) % 4, (z + 16) % 8
    return (y * 4 + (z % 2) * 2 + c, x * 4 + z // 2)


def kernel(
    x_ref, up_ref, gain_ref, wu_ref, wd_ref, grad_ref, up_out, down_out,
    tok_n, tok_u, wt, w, hid, dpre, g, yo_in, ya_st, nb_in, ysum, za_in, zb_in, total, fin_st, fin_in, up_rows,
    dn, dn_sib, dn_st, dn_in, ss, rs,
):
    dp, tensor = lax.axis_index("dp"), lax.axis_index("tensor")
    y, zl, c = dp // 4, (dp // 2) % 2, dp % 2
    x, z = tensor // 4, (tensor % 4) * 2 + zl
    step_out = 2 * zl - 1
    sib = place(x, y, z, 1 - c)
    xr, xl = place(x + 1, y, z, c), place(x - 1, y, z, c)
    x_far = place(x + 2, y, z, c)
    yr, yl = place(x, y + 1, z, c), place(x, y - 1, z, c)
    z_out, z_in = place(x, y, z + step_out, c), place(x, y, z - step_out, c)
    z_cross = place(x, y, z - step_out, 1 - c)
    z_same = {1: place(x, y, z + 2 * step_out, c), 2: place(x, y, z + 4, c), 3: place(x, y, z - 2 * step_out, c)}
    z_other = {0: z_in, 1: z_out, 2: place(x, y, z + 3 * step_out, c), 3: place(x, y, z - 3 * step_out, c)}
    kind = y % 2
    from_out, from_in = 16 + 96 * zl, 112 - 96 * zl
    mine = zl

    barrier = pltpu.get_barrier_semaphore()
    peers = [sib, xr, xl, x_far, yr, yl, z_cross, *z_same.values(), *z_other.values()]
    for peer in peers:
        pl.semaphore_signal(barrier, inc=1, device_id=peer, device_id_type=MESH)

    copies, only = {}, {}

    def make(key, src, dst, device):
        i = len(copies)
        copies[key] = pltpu.make_async_remote_copy(
            src_ref=src, dst_ref=dst, send_sem=ss.at[i], recv_sem=rs.at[i], device_id=device, device_id_type=MESH
        )

    def start(key, when=None):
        if when is None:
            copies[key].start()
        else:
            only[key] = when
            pl.when(when)(copies[key].start)

    def send(key, src, dst, device, when=None):
        make(key, src, dst, device)
        start(key, when)

    def recv(*keys, when=None):
        for key in keys:
            if when is None:
                copies[key].wait_recv()
            else:
                pl.when(when)(copies[key].wait_recv)

    def tok_rows(group, core, first=0, rows=TOK):
        return pl.ds(pl.multiple_of(group * GROUP + core * TOK + first, 16), rows)

    own = tok_rows(0, c)
    tok_u[own] = up_ref[...]
    toks = {"u": tok_u, "n": tok_n}

    def send_own(a):
        send((a, "r"), toks[a].at[own], toks[a].at[tok_rows(3, c)], xr)
        send((a, "l"), toks[a].at[own], toks[a].at[tok_rows(1, c)], xl)
        send((a, "s0"), toks[a].at[own], toks[a].at[own], sib)

    pl.semaphore_wait(barrier, len(peers))
    send_own("u")

    for n in range(13):
        cols = pl.ds(n * 128, 128)
        wt[pl.ds(0, 400), cols] = wu_ref[cols, :].T
    wt[pl.ds(400, 16)] = jnp.zeros((16, D), BF16)
    w[0, pl.ds(0, HALF)] = wt[pl.ds(pl.multiple_of(c * HALF, 16), HALF)]

    @pl.when(c == 0)
    def _():
        w[1, pl.ds(0, HALF)] = wd_ref[pl.ds(0, HALF)]

    @pl.when(c == 1)
    def _():
        w[1, pl.ds(0, 192)] = wd_ref[pl.ds(HALF, 192)]
        w[1, pl.ds(192, 16)] = jnp.zeros((16, D), BF16)

    def rows_of(slot, first, rows):
        return pl.ds(pl.multiple_of(slot * HALF + first, 16), rows)

    def chunk(slot, i):
        return rows_of(slot, *CHUNKS[i])

    for i in range(4):
        send(("w0", i), w.at[kind, chunk(0, i)], w.at[kind, chunk(1, i)], z_out)

    def norm(i, _):
        r = pl.ds(pl.multiple_of(i * 16, 16), 16)
        wide = x_ref[r].astype(F32)
        inv = lax.rsqrt(jnp.mean(wide * wide, axis=-1, keepdims=True) + norm_eps)
        tok_n[tok_rows(0, c, i * 16, 16)] = (wide * inv * gain_ref[...]).astype(BF16)
        return 0

    lax.fori_loop(0, TOK // 16, norm, 0)
    send_own("n")

    def pass_neighbours(a):
        recv((a, "r"))
        send((a, "fr"), toks[a].at[tok_rows(3, c, 0, 64)], toks[a].at[tok_rows(2, c, 0, 64)], xr)
        send((a, "s3"), toks[a].at[tok_rows(3, c)], toks[a].at[tok_rows(3, c)], sib)
        recv((a, "l"))
        send((a, "fl"), toks[a].at[tok_rows(1, c, 64, 64)], toks[a].at[tok_rows(2, c, 64, 64)], xl)
        send((a, "s1"), toks[a].at[tok_rows(1, c)], toks[a].at[tok_rows(1, c)], sib)

    def pass_opposite(a):
        recv((a, "fr"), (a, "fl"))
        send((a, "s2"), toks[a].at[tok_rows(2, c)], toks[a].at[tok_rows(2, c)], sib)

    def share(key, rows, peer):
        send(("wy", key), w.at[kind, rows], w.at[kind, rows], peer)

    def pass_w1(i):
        recv(("w0", i))
        send(("w1", i), w.at[kind, chunk(1, i)], w.at[kind, chunk(3, i)], z_in)
        share((1, i), chunk(1, i), (yr, yr, yl, yl)[i])

    def pass_w3(i):
        recv(("w1", i))
        if i == 0:
            extra = rows_of(3, 0, 16), rows_of(2, 0, 16)
            send(("w3", "x"), w.at[kind, extra[0]], w.at[kind, extra[1]], z_out, zl == 1)
            for n in range(2):
                there = rows_of(2, from_in + 48 * n, 48)
                make(("w3", n), w.at[kind, rows_of(3, from_in + 48 * n, 48)], w.at[kind, there], z_out)
        pl.when(zl == 1 - i // 2)(copies["w3", i % 2].start)
        share((3, i), chunk(3, i), (yl, yl, yr, yr)[i])

    def pass_w2(n):
        recv(("w3", n))
        rows = rows_of(2, from_out + 48 * n, 48)
        send(("w2", n), w.at[kind, rows], w.at[kind, rows], z_in)
        share((2, "o", n), rows, yr)
        if n == 1:
            recv(("w3", "x"), when=zl == 0)
            rows = rows_of(2, 0, 16)
            send(("w2", "x"), w.at[kind, rows], w.at[kind, rows], z_in, zl == 0)

    def pass_last():
        for n in range(2):
            recv(("w2", n))
            share((2, "i", n), rows_of(2, from_in + 48 * n, 48), yl)
        recv(("w2", "x"), when=zl == 1)
        share((2, "x"), rows_of(2, 0, 16), yl)

    def all_w(slot):
        recv(*[key for key in copies if key[0] == "wy" and key[1][0] == slot])

    def forward(slot, group):
        r = pl.ds(slot * HALF, HALF)
        t = pl.ds(pl.multiple_of(group * GROUP, GROUP), GROUP)
        nt = (((1,), (1,)), ((), ()))
        pre = lax.dot_general(w[0, r], tok_n[t], nt, preferred_element_type=F32)
        dhidden = lax.dot_general(w[1, r], tok_u[t], nt, preferred_element_type=F32)
        hidden, slope = gelu_parts(pre)
        hid[r, t] = hidden.astype(BF16)
        dpre[r, t] = (dhidden * slope).astype(BF16)

    def forward_all(slot):
        def one(group, _):
            forward(slot, group)
            return 0

        lax.fori_loop(0, 4, one, 0)

    def grads(slot):
        r = pl.ds(slot * HALF, HALF)

        def columns(cols):
            up = jnp.dot(dpre[r], tok_n[:, cols], preferred_element_type=F32)
            g[0, r, cols] = (up * GRAD_SCALE).astype(BF16)
            down = jnp.dot(hid[r], tok_u[:, cols], preferred_element_type=F32)
            g[1, r, cols] = (down * GRAD_SCALE).astype(BF16)

        def tile(n, _):
            columns(pl.ds(pl.multiple_of(n * 256, 256), 256))
            return 0

        lax.fori_loop(0, 6, tile, 0)
        columns(pl.ds(1536, 128))

    def window(owner, first=0, cols=WIN):
        return pl.ds(pl.multiple_of(((owner + 8) % 4) * 384 + first, 128), cols)

    def y1(slot):
        r = pl.ds(slot * HALF, HALF)
        send(("yo", slot, 0), g.at[:, r, window(y + 2, 0, 256)], yo_in.at[slot, 0], yr)
        send(("yo", slot, 1), g.at[:, r, window(y + 2, 256, 256)], yo_in.at[slot, 1], yl)
        send(("yd", slot, 0), g.at[:, r, window(y + 1, 256, 256)], nb_in.at[slot, 0, :, :, pl.ds(256, 256)], yr)
        send(("yd", slot, 1), g.at[:, r, window(y - 1, 0, 256)], nb_in.at[slot, 1, :, :, pl.ds(0, 256)], yl)

    def rows16(i):
        return pl.ds(pl.multiple_of(i * 16, 16), 16)

    def y2(slot):
        for way, owner, first, peer in ((0, y + 1, 0, yr), (1, y - 1, 256, yl)):
            recv(("yo", slot, way))
            cols = window(owner, first, 256)

            def add(i, _):
                part = pl.ds(pl.multiple_of(slot * HALF + i * 16, 16), 16)
                here = rows16(i)
                ya_st[slot, way, :, here] = (
                    g[:, part, cols].astype(F32) + yo_in[slot, way, :, here].astype(F32)
                ).astype(BF16)
                return 0

            lax.fori_loop(0, HALF // 16, add, 0)
            send(("ya", slot, way), ya_st.at[slot, way], nb_in.at[slot, way, :, :, pl.ds(first, 256)], peer)

    def y3(slot):
        recv(("yd", slot, 0), ("yd", slot, 1), ("ya", slot, 0), ("ya", slot, 1))
        cols = window(y)

        def add(i, _):
            part = pl.ds(pl.multiple_of(slot * HALF + i * 16, 16), 16)
            here = rows16(i)
            ysum[slot, :, here] = (
                g[:, part, cols].astype(F32)
                + nb_in[slot, 0, :, here].astype(F32)
                + nb_in[slot, 1, :, here].astype(F32)
            ).astype(BF16)
            return 0

        lax.fori_loop(0, HALF // 16, add, 0)
        send(("zb", slot), ysum.at[slot, 1 - mine], zb_in.at[slot], z_other[slot])
        if slot:
            send(("za", slot), ysum.at[slot, mine], za_in.at[slot - 1], z_same[slot])

    def back(group):
        t = pl.ds(group * GROUP, GROUP)
        rows = dpre[:, t].T

        def columns(cols):
            part = jnp.dot(rows, w[0, :, cols], preferred_element_type=F32).astype(BF16)
            dn[group, 0, :, cols] = part[:TOK]
            dn[group, 1, :, cols] = part[TOK:]

        def tile(n, _):
            columns(pl.ds(pl.multiple_of(n * 256, 256), 256))
            return 0

        lax.fori_loop(0, 6, tile, 0)
        columns(pl.ds(1536, 128))
        send(("dn", group), dn.at[group, 1 - c], dn_sib.at[group], sib)

    def dn_pass(group, peer):
        recv(("dn", group))

        def add(i, _):
            here = rows16(i)
            dn_st[group - 1, here] = (dn[group, c, here].astype(F32) + dn_sib[group, here].astype(F32)).astype(BF16)
            return 0

        lax.fori_loop(0, TOK // 16, add, 0)
        send(("dx", group), dn_st.at[group - 1], dn_in.at[group - 1], peer)

    pass_w1(0)
    pass_neighbours("u")
    pass_w1(1)
    recv(("u", "s0"), ("n", "s0"))
    forward(0, 0)
    pass_w1(2)
    pass_w3(0)
    pass_w1(3)
    pass_neighbours("n")
    pass_w3(1)
    recv(("u", "s1"), ("n", "s1"))
    forward(0, 1)
    pass_w3(2)
    recv(("u", "s3"), ("n", "s3"))
    forward(0, 3)
    pass_opposite("u")
    pass_w3(3)
    pass_opposite("n")
    pass_w2(0)
    recv(("u", "s2"), ("n", "s2"))
    forward(0, 2)
    pass_w2(1)
    grads(0)
    y1(0)
    all_w(1)
    forward_all(1)
    pass_last()
    grads(1)
    y1(1)
    all_w(3)
    forward_all(3)
    grads(3)
    y1(3)
    y2(1)
    all_w(2)
    forward_all(2)
    grads(2)
    y1(2)
    y2(3)
    back(2)
    y2(2)
    y2(0)
    y3(1)
    back(1)
    back(3)
    back(0)
    dn_pass(2, x_far)
    dn_pass(1, xr)
    dn_pass(3, xl)
    y3(3)
    y3(2)
    y3(0)

    recv(("dn", 0), ("dx", 1), ("dx", 2), ("dx", 3))

    def finish(i, _):
        here = rows16(i)
        gain = gain_ref[...]
        wide = x_ref[here].astype(F32)
        inv = lax.rsqrt(jnp.mean(wide * wide, axis=-1, keepdims=True) + norm_eps)
        unit = wide * inv
        dnormed = dn[0, c, here].astype(F32) + dn_sib[0, here].astype(F32)
        for k in range(3):
            dnormed += dn_in[k, here].astype(F32)
        dunit = dnormed * gain
        project = jnp.mean(dunit * unit, axis=-1, keepdims=True)
        grad_ref[here] = (up_ref[here].astype(F32) + inv * (dunit - unit * project)).astype(BF16)
        return 0

    lax.fori_loop(0, TOK // 16, finish, 0)

    recv(*[("za", k) for k in (1, 2, 3)], *[("zb", k) for k in range(4)])
    total[:, pl.ds(WIN, 128)] = jnp.zeros((16, 128), F32)

    def split(i, _):
        here = rows16(i)
        rows = ysum[0, mine, here].astype(F32) + zb_in[0, here].astype(F32)
        for k in range(3):
            rows += za_in[k, here].astype(F32) + zb_in[k + 1, here].astype(F32)
        total[:, pl.ds(0, WIN)] = rows
        for q in range(4):
            turned = pltpu.roll(total[...], (WIN + 128 - 104 * q) - 32 * y, 1)
            fin_st[q, here] = turned[:, :128].astype(BF16)
        return 0

    lax.fori_loop(0, HALF // 16, split, 0)
    me = 2 * zl + c
    for key, device, to in (("sib", sib, 2 * zl + 1 - c), ("in", z_in, 2 * (1 - zl) + c), ("cross", z_cross, 2 * (1 - zl) + 1 - c)):
        send(("f", key), fin_st.at[to], fin_in.at[me], device)

    def keep(i, _):
        fin_in[me, rows16(i)] = fin_st[me, rows16(i)]
        return 0

    lax.fori_loop(0, HALF // 16, keep, 0)
    recv(("f", "sib"), ("f", "in"), ("f", "cross"))

    for q in range(2):
        up_rows[pl.ds(q * HALF, HALF)] = fin_in[q].astype(F32)
        rows = (HALF, 400 - HALF)[q]
        down_out[pl.ds(q * HALF, rows), :] = fin_in[2 + q, pl.ds(0, rows)].astype(F32)[:, :104]
    up_rows[pl.ds(2 * HALF, 96)] = jnp.zeros((96, 128), F32)
    up_out[...] = up_rows[...].T[:104, :400]
    for key, copy in copies.items():
        if key in only:
            pl.when(only[key])(copy.wait_send)
        else:
            copy.wait_send()


def body(inputs, gain, w_up, w_down, upstream):
    vmem = pl.BlockSpec(memory_space=pltpu.VMEM)
    return pl.pallas_call(
        kernel,
        out_shape=(
            jax.ShapeDtypeStruct((TOK, D), BF16),
            jax.ShapeDtypeStruct((104, 400), F32),
            jax.ShapeDtypeStruct((400, 104), F32),
        ),
        in_specs=[vmem] * 5,
        out_specs=(vmem,) * 3,
        scratch_shapes=[
            pltpu.VMEM((T, D), BF16),
            pltpu.VMEM((T, D), BF16),
            pltpu.VMEM((2 * HALF, D), BF16),
            pltpu.VMEM((2, HID, D), BF16),
            pltpu.VMEM((HID, T), BF16),
            pltpu.VMEM((HID, T), BF16),
            pltpu.VMEM((2, HID, D), BF16),
            pltpu.VMEM((4, 2, 2, HALF, 256), BF16),
            pltpu.VMEM((4, 2, 2, HALF, 256), BF16),
            pltpu.VMEM((4, 2, 2, HALF, WIN), BF16),
            pltpu.VMEM((4, 2, HALF, WIN), BF16),
            pltpu.VMEM((3, HALF, WIN), BF16),
            pltpu.VMEM((4, HALF, WIN), BF16),
            pltpu.VMEM((16, WIN + 128), F32),
            pltpu.VMEM((4, HALF, 128), BF16),
            pltpu.VMEM((4, HALF, 128), BF16),
            pltpu.VMEM((512, 128), F32),
            pltpu.VMEM((4, 2, TOK, D), BF16),
            pltpu.VMEM((4, TOK, D), BF16),
            pltpu.VMEM((3, TOK, D), BF16),
            pltpu.VMEM((3, TOK, D), BF16),
            pltpu.SemaphoreType.DMA((N_SEM,)),
            pltpu.SemaphoreType.DMA((N_SEM,)),
        ],
        compiler_params=pltpu.CompilerParams(
            collective_id=1, has_side_effects=True, vmem_limit_bytes=60 * 2**20
        ),
        name="block_backward",
    )(inputs, upstream, gain.astype(F32).reshape(1, D), w_up, w_down)


def solution(mesh):
    in_specs = (
        P(("dp", "tensor"), None),
        P(),
        P(None, "tensor"),
        P("tensor", None),
        P(("dp", "tensor"), None),
    )
    out_specs = (P(("dp", "tensor"), None), P("dp", "tensor"), P("tensor", "dp"))
    return jax.shard_map(body, mesh=mesh, in_specs=in_specs, out_specs=out_specs, check_vma=False)
```

```python
import jax
import jax.numpy as jnp
from jax import lax
from jax.experimental import pallas as pl
from jax.experimental.pallas import tpu as pltpu
from jax.sharding import PartitionSpec as P

MESH = pl.DeviceIdType.MESH
F32, BF16 = jnp.float32, jnp.bfloat16

norm_eps = 1e-06
D = 1664
TOK = 128
GROUP = 2 * TOK
T = 4 * GROUP
HALF = 208
HID = 4 * HALF
WIN = 512
CHUNKS = ((0, 64), (64, 48), (112, 48), (160, 48))
N_SEM = 88
GRAD_SCALE = float(32768) ** (-0.5)


def gelu_parts(pre):
    cdf = 0.5 * (1.0 + lax.erf(pre * 0.7071067811865476))
    pdf = jnp.exp(-0.5 * pre * pre) * 0.3989422804014327
    return (pre * cdf, cdf + pre * pdf)


def place(x, y, z, c):
    x, y, z = (x + 8) % 4, (y + 8) % 4, (z + 16) % 8
    return (y * 4 + (z % 2) * 2 + c, x * 4 + z // 2)


def kernel(
    x_ref, up_ref, gain_ref, wu_ref, wd_ref, grad_ref, up_out, down_out,
    tok_n, tok_u, w, hid, dpre, g, yo_in, ya_st, nb_in, ysum, za_in, zb_in, pair_in, total, fin_st, fin_in,
    dn, dn_sib, dn_st, dn_in, ss, rs,
):
    dp, tensor = lax.axis_index("dp"), lax.axis_index("tensor")
    y, zl, c = dp // 4, (dp // 2) % 2, dp % 2
    x, z = tensor // 4, (tensor % 4) * 2 + zl
    step_out = 2 * zl - 1
    sib = place(x, y, z, 1 - c)
    xr, xl = place(x + 1, y, z, c), place(x - 1, y, z, c)
    x_far = place(x + 2, y, z, c)
    yr, yl = place(x, y + 1, z, c), place(x, y - 1, z, c)
    z_out, z_in = place(x, y, z + step_out, c), place(x, y, z - step_out, c)
    z_cross = place(x, y, z - step_out, 1 - c)
    z_same = {1: place(x, y, z + 2 * step_out, c), 2: place(x, y, z + 4, c)}
    z_other = {0: z_in, 1: z_out, 2: place(x, y, z + 3 * step_out, c)}
    kind = y % 2
    from_out, from_in = 16 + 96 * zl, 112 - 96 * zl
    mine = zl

    barrier = pltpu.get_barrier_semaphore()
    peers = [sib, xr, xl, x_far, yr, yl, z_cross, place(x, y, z - 2 * step_out, c), *z_same.values(), *z_other.values()]
    for peer in peers:
        pl.semaphore_signal(barrier, inc=1, device_id=peer, device_id_type=MESH)

    copies, only = {}, {}

    def make(key, src, dst, device):
        i = len(copies)
        copies[key] = pltpu.make_async_remote_copy(
            src_ref=src, dst_ref=dst, send_sem=ss.at[i], recv_sem=rs.at[i], device_id=device, device_id_type=MESH
        )

    def start(key, when=None):
        if when is None:
            copies[key].start()
        else:
            only[key] = when
            pl.when(when)(copies[key].start)

    def send(key, src, dst, device, when=None):
        make(key, src, dst, device)
        start(key, when)

    def recv(*keys, when=None):
        for key in keys:
            if when is None:
                copies[key].wait_recv()
            else:
                pl.when(when)(copies[key].wait_recv)

    def tok_rows(group, core, first=0, rows=TOK):
        return pl.ds(pl.multiple_of(group * GROUP + core * TOK + first, 16), rows)

    own = tok_rows(0, c)
    tok_u[own] = up_ref[...]
    toks = {"u": tok_u, "n": tok_n}

    def send_own(a):
        send((a, "r"), toks[a].at[own], toks[a].at[tok_rows(3, c)], xr)
        send((a, "l"), toks[a].at[own], toks[a].at[tok_rows(1, c)], xl)
        send((a, "s0"), toks[a].at[own], toks[a].at[own], sib)

    pl.semaphore_wait(barrier, len(peers))
    send_own("u")

    for k, ref in enumerate((wu_ref, wd_ref)):
        w[k, pl.ds(0, 192)] = ref[pl.ds(pl.multiple_of(c * HALF, 16), 192)]

        @pl.when(c == 0)
        def _():
            w[k, pl.ds(192, 16)] = ref[pl.ds(192, 16)]

        @pl.when(c == 1)
        def _():
            w[k, pl.ds(192, 16)] = jnp.zeros((16, D), BF16)

    def rows_of(slot, first, rows):
        return pl.ds(pl.multiple_of(slot * HALF + first, 16), rows)

    def chunk(slot, i):
        return rows_of(slot, *CHUNKS[i])

    for i in range(4):
        send(("w0", i), w.at[kind, chunk(0, i)], w.at[kind, chunk(1, i)], z_out)

    def norm(i, _):
        r = pl.ds(pl.multiple_of(i * 16, 16), 16)
        wide = x_ref[r].astype(F32)
        inv = lax.rsqrt(jnp.mean(wide * wide, axis=-1, keepdims=True) + norm_eps)
        tok_n[tok_rows(0, c, i * 16, 16)] = (wide * inv * gain_ref[...]).astype(BF16)
        return 0

    lax.fori_loop(0, TOK // 16, norm, 0)
    send_own("n")

    def pass_neighbours(a):
        recv((a, "r"))
        send((a, "fr"), toks[a].at[tok_rows(3, c, 0, 64)], toks[a].at[tok_rows(2, c, 0, 64)], xr)
        send((a, "s3"), toks[a].at[tok_rows(3, c)], toks[a].at[tok_rows(3, c)], sib)
        recv((a, "l"))
        send((a, "fl"), toks[a].at[tok_rows(1, c, 64, 64)], toks[a].at[tok_rows(2, c, 64, 64)], xl)
        send((a, "s1"), toks[a].at[tok_rows(1, c)], toks[a].at[tok_rows(1, c)], sib)

    def pass_opposite(a):
        recv((a, "fr"), (a, "fl"))
        send((a, "s2"), toks[a].at[tok_rows(2, c)], toks[a].at[tok_rows(2, c)], sib)

    def share(key, rows, peer):
        send(("wy", key), w.at[kind, rows], w.at[kind, rows], peer)

    def pass_w1(i):
        recv(("w0", i))
        send(("w1", i), w.at[kind, chunk(1, i)], w.at[kind, chunk(3, i)], z_in)
        share((1, i), chunk(1, i), (yr, yr, yl, yl)[i])

    def pass_w3(i):
        recv(("w1", i))
        if i == 0:
            extra = rows_of(3, 0, 16), rows_of(2, 0, 16)
            send(("w3", "x"), w.at[kind, extra[0]], w.at[kind, extra[1]], z_out, zl == 1)
            for n in range(2):
                there = rows_of(2, from_in + 48 * n, 48)
                make(("w3", n), w.at[kind, rows_of(3, from_in + 48 * n, 48)], w.at[kind, there], z_out)
        pl.when(zl == 1 - i // 2)(copies["w3", i % 2].start)
        share((3, i), chunk(3, i), (yl, yl, yr, yr)[i])

    def pass_w2(n):
        recv(("w3", n))
        rows = rows_of(2, from_out + 48 * n, 48)
        send(("w2", n), w.at[kind, rows], w.at[kind, rows], z_in)
        share((2, "o", n), rows, yr)
        if n == 1:
            recv(("w3", "x"), when=zl == 0)
            rows = rows_of(2, 0, 16)
            send(("w2", "x"), w.at[kind, rows], w.at[kind, rows], z_in, zl == 0)

    def pass_last():
        for n in range(2):
            recv(("w2", n))
            share((2, "i", n), rows_of(2, from_in + 48 * n, 48), yl)
        recv(("w2", "x"), when=zl == 1)
        share((2, "x"), rows_of(2, 0, 16), yl)

    def all_w(slot):
        recv(*[key for key in copies if key[0] == "wy" and key[1][0] == slot])

    def forward(slot, group):
        r = pl.ds(slot * HALF, HALF)
        t = pl.ds(pl.multiple_of(group * GROUP, GROUP), GROUP)
        nt = (((1,), (1,)), ((), ()))
        pre = lax.dot_general(w[0, r], tok_n[t], nt, preferred_element_type=F32)
        dhidden = lax.dot_general(w[1, r], tok_u[t], nt, preferred_element_type=F32)
        hidden, slope = gelu_parts(pre)
        hid[r, t] = hidden.astype(BF16)
        dpre[r, t] = (dhidden * slope).astype(BF16)

    def forward_all(slot):
        def one(group, _):
            forward(slot, group)
            return 0

        lax.fori_loop(0, 4, one, 0)

    def grads(slot):
        r = pl.ds(slot * HALF, HALF)

        def columns(cols):
            up = jnp.dot(dpre[r], tok_n[:, cols], preferred_element_type=F32)
            g[0, r, cols] = (up * GRAD_SCALE).astype(BF16)
            down = jnp.dot(hid[r], tok_u[:, cols], preferred_element_type=F32)
            g[1, r, cols] = (down * GRAD_SCALE).astype(BF16)

        def tile(n, _):
            columns(pl.ds(pl.multiple_of(n * 256, 256), 256))
            return 0

        lax.fori_loop(0, 6, tile, 0)
        columns(pl.ds(1536, 128))

    def window(owner, first=0, cols=WIN):
        return pl.ds(pl.multiple_of(((owner + 8) % 4) * 384 + first, 128), cols)

    def rows16(i):
        return pl.ds(pl.multiple_of(i * 16, 16), 16)

    def slot16(slot, i):
        return pl.ds(pl.multiple_of(slot * HALF + i * 16, 16), 16)

    def kinds(part):
        return pl.ds(0, 2) if part[1] is None else pl.ds(part[1], 1)

    def y1(*part):
        r, k = pl.ds(part[0] * HALF, HALF), kinds(part)
        left, right = pl.ds(0, 256), pl.ds(256, 256)
        send(("yo", part, 0), g.at[k, r, window(y + 2, 0, 256)], yo_in.at[part[0], 0, k], yr)
        send(("yo", part, 1), g.at[k, r, window(y + 2, 256, 256)], yo_in.at[part[0], 1, k], yl)
        send(("yd", part, 0), g.at[k, r, window(y + 1, 256, 256)], nb_in.at[part[0], 0, k, :, right], yr)
        send(("yd", part, 1), g.at[k, r, window(y - 1, 0, 256)], nb_in.at[part[0], 1, k, :, left], yl)

    def y2(*part):
        slot, k = part[0], kinds(part)
        for way, owner, first, peer in ((0, y + 1, 0, yr), (1, y - 1, 256, yl)):
            recv(("yo", part, way))
            cols = window(owner, first, 256)

            def add(i, _):
                here = rows16(i)
                ya_st[slot, way, k, here] = (
                    g[k, slot16(slot, i), cols].astype(F32) + yo_in[slot, way, k, here].astype(F32)
                ).astype(BF16)
                return 0

            lax.fori_loop(0, HALF // 16, add, 0)
            send(("ya", part, way), ya_st.at[slot, way, k], nb_in.at[slot, way, k, :, pl.ds(first, 256)], peer)

    def y3(*part):
        slot, k = part[0], kinds(part)
        recv(("yd", part, 0), ("yd", part, 1), ("ya", part, 0), ("ya", part, 1))
        cols = window(y)

        def add(i, _):
            here = rows16(i)
            ysum[slot, k, here] = (
                g[k, slot16(slot, i), cols].astype(F32)
                + nb_in[slot, 0, k, here].astype(F32)
                + nb_in[slot, 1, k, here].astype(F32)
            ).astype(BF16)
            return 0

        lax.fori_loop(0, HALF // 16, add, 0)
        if part[1] in (None, 0):
            make(("zb", slot), ysum.at[slot, 1 - mine], zb_in.at[slot], z_other[slot])
            if slot:
                make(("za", slot), ysum.at[slot, mine], za_in.at[slot - 1], z_same[slot])
        if part[1] is None:
            for key in ("zb", "za")[: 1 + (slot > 0)]:
                start((key, slot))
        else:
            pl.when(mine == part[1])(copies["za", slot].start)
            pl.when(mine != part[1])(copies["zb", slot].start)

    def pair_send():
        for k in range(2):
            send(("pair", k), g.at[k, pl.ds(3 * HALF, HALF)], pair_in.at[k], z_in)

    def pair_add(k):
        recv(("pair", k))

        def add(i, _):
            here = slot16(1, i)
            g[k, here] = (g[k, here].astype(F32) + pair_in[k, rows16(i)].astype(F32)).astype(BF16)
            return 0

        lax.fori_loop(0, HALF // 16, add, 0)

    def back(group):
        t = pl.ds(group * GROUP, GROUP)
        rows = dpre[:, t].T

        def columns(cols):
            part = jnp.dot(rows, w[0, :, cols], preferred_element_type=F32).astype(BF16)
            dn[group, 0, :, cols] = part[:TOK]
            dn[group, 1, :, cols] = part[TOK:]

        def tile(n, _):
            columns(pl.ds(pl.multiple_of(n * 256, 256), 256))
            return 0

        lax.fori_loop(0, 6, tile, 0)
        columns(pl.ds(1536, 128))
        send(("dn", group), dn.at[group, 1 - c], dn_sib.at[group], sib)

    def dn_pass(group, peer):
        recv(("dn", group))

        def add(i, _):
            here = rows16(i)
            dn_st[group - 1, here] = (dn[group, c, here].astype(F32) + dn_sib[group, here].astype(F32)).astype(BF16)
            return 0

        lax.fori_loop(0, TOK // 16, add, 0)
        send(("dx", group), dn_st.at[group - 1], dn_in.at[group - 1], peer)

    pass_w1(0)
    pass_neighbours("u")
    pass_w1(1)
    recv(("u", "s0"), ("n", "s0"))
    forward(0, 0)
    pass_w1(2)
    pass_w3(0)
    pass_w1(3)
    pass_neighbours("n")
    pass_w3(1)
    recv(("u", "s1"), ("n", "s1"))
    forward(0, 1)
    pass_w3(2)
    recv(("u", "s3"), ("n", "s3"))
    forward(0, 3)
    pass_w3(3)
    pass_opposite("u")
    pass_opposite("n")
    pass_w2(0)
    recv(("u", "s2"), ("n", "s2"))
    forward(0, 2)
    grads(0)
    y1(0, None)
    pass_w2(1)
    all_w(3)
    forward_all(3)
    pass_last()
    grads(3)
    pair_send()
    y2(0, None)
    all_w(2)
    forward_all(2)
    grads(2)
    y1(2, None)
    all_w(1)
    forward_all(1)
    grads(1)
    y2(2, None)
    y3(0, None)
    back(2)
    pair_add(0)
    y1(1, 0)
    back(1)
    y2(1, 0)
    back(3)
    pair_add(1)
    y1(1, 1)
    y3(2, None)
    back(0)
    y2(1, 1)
    dn_pass(2, x_far)
    dn_pass(1, xr)
    dn_pass(3, xl)
    y3(1, 0)
    y3(1, 1)

    recv(("dn", 0), ("dx", 1), ("dx", 2), ("dx", 3))

    def finish(i, _):
        here = rows16(i)
        gain = gain_ref[...]
        wide = x_ref[here].astype(F32)
        inv = lax.rsqrt(jnp.mean(wide * wide, axis=-1, keepdims=True) + norm_eps)
        unit = wide * inv
        dnormed = dn[0, c, here].astype(F32) + dn_sib[0, here].astype(F32)
        for k in range(3):
            dnormed += dn_in[k, here].astype(F32)
        dunit = dnormed * gain
        project = jnp.mean(dunit * unit, axis=-1, keepdims=True)
        grad_ref[here] = (up_ref[here].astype(F32) + inv * (dunit - unit * project)).astype(BF16)
        return 0

    lax.fori_loop(0, TOK // 16, finish, 0)

    recv(*[("za", k) for k in (1, 2)], *[("zb", k) for k in range(3)])
    total[:, pl.ds(WIN, 128)] = jnp.zeros((16, 128), F32)

    def split(i, _):
        here = rows16(i)
        rows = ysum[0, mine, here].astype(F32) + zb_in[0, here].astype(F32)
        for k in range(2):
            rows += za_in[k, here].astype(F32) + zb_in[k + 1, here].astype(F32)
        total[:, pl.ds(0, WIN)] = rows
        for q in range(4):
            turned = pltpu.roll(total[...], (WIN + 128 - 104 * q) - 32 * y, 1)
            fin_st[q, here] = turned[:, :128].astype(BF16)
        return 0

    lax.fori_loop(0, HALF // 16, split, 0)
    me = 2 * zl + c
    for key, device, to in (("sib", sib, 2 * zl + 1 - c), ("in", z_in, 2 * (1 - zl) + c), ("cross", z_cross, 2 * (1 - zl) + 1 - c)):
        send(("f", key), fin_st.at[to], fin_in.at[me], device)

    def keep(i, _):
        fin_in[me, rows16(i)] = fin_st[me, rows16(i)]
        return 0

    lax.fori_loop(0, HALF // 16, keep, 0)
    recv(("f", "sib"), ("f", "in"), ("f", "cross"))

    for q in range(2):
        rows = (HALF, 400 - HALF)[q]
        up_out[pl.ds(q * HALF, rows), :] = fin_in[q, pl.ds(0, rows)].astype(F32)[:, :104]
        down_out[pl.ds(q * HALF, rows), :] = fin_in[2 + q, pl.ds(0, rows)].astype(F32)[:, :104]
    for key, copy in copies.items():
        if key in only:
            pl.when(only[key])(copy.wait_send)
        else:
            copy.wait_send()


def body(inputs, gain, w_up, w_down, upstream):
    vmem = pl.BlockSpec(memory_space=pltpu.VMEM)
    input_grad, up_grad, down_grad = pl.pallas_call(
        kernel,
        out_shape=(
            jax.ShapeDtypeStruct((TOK, D), BF16),
            jax.ShapeDtypeStruct((400, 104), F32),
            jax.ShapeDtypeStruct((400, 104), F32),
        ),
        in_specs=[vmem] * 5,
        out_specs=(vmem,) * 3,
        scratch_shapes=[
            pltpu.VMEM((T, D), BF16),
            pltpu.VMEM((T, D), BF16),
            pltpu.VMEM((2, HID, D), BF16),
            pltpu.VMEM((HID, T), BF16),
            pltpu.VMEM((HID, T), BF16),
            pltpu.VMEM((2, HID, D), BF16),
            pltpu.VMEM((3, 2, 2, HALF, 256), BF16),
            pltpu.VMEM((3, 2, 2, HALF, 256), BF16),
            pltpu.VMEM((3, 2, 2, HALF, WIN), BF16),
            pltpu.VMEM((3, 2, HALF, WIN), BF16),
            pltpu.VMEM((2, HALF, WIN), BF16),
            pltpu.VMEM((3, HALF, WIN), BF16),
            pltpu.VMEM((2, HALF, D), BF16),
            pltpu.VMEM((16, WIN + 128), F32),
            pltpu.VMEM((4, HALF, 128), BF16),
            pltpu.VMEM((4, HALF, 128), BF16),
            pltpu.VMEM((4, 2, TOK, D), BF16),
            pltpu.VMEM((4, TOK, D), BF16),
            pltpu.VMEM((3, TOK, D), BF16),
            pltpu.VMEM((3, TOK, D), BF16),
            pltpu.SemaphoreType.DMA((N_SEM,)),
            pltpu.SemaphoreType.DMA((N_SEM,)),
        ],
        compiler_params=pltpu.CompilerParams(
            collective_id=1, has_side_effects=True, vmem_limit_bytes=60 * 2**20
        ),
        name="block_backward",
    )(inputs, upstream, gain.astype(F32).reshape(1, D), w_up.T, w_down)
    return input_grad, up_grad.T, down_grad


def solution(mesh):
    in_specs = (
        P(("dp", "tensor"), None),
        P(),
        P(None, "tensor"),
        P("tensor", None),
        P(("dp", "tensor"), None),
    )
    out_specs = (P(("dp", "tensor"), None), P("dp", "tensor"), P("tensor", "dp"))
    return jax.shard_map(body, mesh=mesh, in_specs=in_specs, out_specs=out_specs, check_vma=False)
```

```python
import jax
import jax.numpy as jnp
from jax import lax
from jax.experimental import pallas as pl
from jax.experimental.pallas import tpu as pltpu
from jax.sharding import PartitionSpec as P

MESH = pl.DeviceIdType.MESH
F32, BF16 = jnp.float32, jnp.bfloat16

norm_eps = 1e-06
D = 1664
TOK = 128
GROUP = 2 * TOK
T = 4 * GROUP
HALF = 208
HID = 4 * HALF
WIN = 512
CHUNKS = ((0, 64), (64, 48), (112, 48), (160, 48))
N_SEM = 96
GRAD_SCALE = float(32768) ** (-0.5)


def gelu_parts(pre):
    cdf = 0.5 * (1.0 + lax.erf(pre * 0.7071067811865476))
    pdf = jnp.exp(-0.5 * pre * pre) * 0.3989422804014327
    return (pre * cdf, cdf + pre * pdf)


def place(x, y, z, c):
    x, y, z = (x + 8) % 4, (y + 8) % 4, (z + 16) % 8
    return (y * 4 + (z % 2) * 2 + c, x * 4 + z // 2)


def kernel(
    x_ref, up_ref, gain_ref, wu_ref, wd_ref, grad_ref, up_out, down_out,
    tok_n, tok_u, w, hid, dpre, g, yo_in, ya_st, nb_in, ysum, z_sum, pair_in, total, fin_st, fin_in,
    dn, dn_sib, dn_st, dn_in, ss, rs,
):
    dp, tensor = lax.axis_index("dp"), lax.axis_index("tensor")
    y, zl, c = dp // 4, (dp // 2) % 2, dp % 2
    x, z = tensor // 4, (tensor % 4) * 2 + zl
    step_out = 2 * zl - 1
    sib = place(x, y, z, 1 - c)
    xr, xl = place(x + 1, y, z, c), place(x - 1, y, z, c)
    x_far = place(x + 2, y, z, c)
    yr, yl = place(x, y + 1, z, c), place(x, y - 1, z, c)
    z_out, z_in = place(x, y, z + step_out, c), place(x, y, z - step_out, c)
    z_cross = place(x, y, z - step_out, 1 - c)
    z_same = {1: place(x, y, z + 2 * step_out, c), 2: place(x, y, z + 4, c), 3: place(x, y, z - 2 * step_out, c)}
    z_other = {0: z_in, 1: z_out, 2: place(x, y, z + 3 * step_out, c), 3: place(x, y, z - 3 * step_out, c)}
    kind = y % 2
    from_out, from_in = 16 + 96 * zl, 112 - 96 * zl
    mine = zl

    barrier = pltpu.get_barrier_semaphore()
    peers = [sib, xr, xl, x_far, yr, yl, z_cross, *z_same.values(), *z_other.values()]
    for peer in peers:
        pl.semaphore_signal(barrier, inc=1, device_id=peer, device_id_type=MESH)

    copies, only = {}, {}

    def make(key, src, dst, device):
        i = len(copies)
        copies[key] = pltpu.make_async_remote_copy(
            src_ref=src, dst_ref=dst, send_sem=ss.at[i], recv_sem=rs.at[i], device_id=device, device_id_type=MESH
        )

    def start(key, when=None):
        if when is None:
            copies[key].start()
        else:
            only[key] = when
            pl.when(when)(copies[key].start)

    def send(key, src, dst, device, when=None):
        make(key, src, dst, device)
        start(key, when)

    def recv(*keys, when=None):
        for key in keys:
            if when is None:
                copies[key].wait_recv()
            else:
                pl.when(when)(copies[key].wait_recv)

    def tok_rows(group, core, first=0, rows=TOK):
        return pl.ds(pl.multiple_of(group * GROUP + core * TOK + first, 16), rows)

    own = tok_rows(0, c)
    tok_u[own] = up_ref[...]
    toks = {"u": tok_u, "n": tok_n}

    def send_own(a):
        send((a, "r"), toks[a].at[own], toks[a].at[tok_rows(3, c)], xr)
        send((a, "l"), toks[a].at[own], toks[a].at[tok_rows(1, c)], xl)
        send((a, "s0"), toks[a].at[own], toks[a].at[own], sib)

    pl.semaphore_wait(barrier, len(peers))
    send_own("u")

    for k, ref in enumerate((wu_ref, wd_ref)):
        w[k, pl.ds(0, 192)] = ref[pl.ds(pl.multiple_of(c * HALF, 16), 192)]

        @pl.when(c == 0)
        def _():
            w[k, pl.ds(192, 16)] = ref[pl.ds(192, 16)]

        @pl.when(c == 1)
        def _():
            w[k, pl.ds(192, 16)] = jnp.zeros((16, D), BF16)

    def rows_of(slot, first, rows):
        return pl.ds(pl.multiple_of(slot * HALF + first, 16), rows)

    def chunk(slot, i):
        return rows_of(slot, *CHUNKS[i])

    for i in range(4):
        send(("w0", i), w.at[kind, chunk(0, i)], w.at[kind, chunk(1, i)], z_out)

    def norm(i, _):
        r = pl.ds(pl.multiple_of(i * 16, 16), 16)
        wide = x_ref[r].astype(F32)
        inv = lax.rsqrt(jnp.mean(wide * wide, axis=-1, keepdims=True) + norm_eps)
        tok_n[tok_rows(0, c, i * 16, 16)] = (wide * inv * gain_ref[...]).astype(BF16)
        return 0

    lax.fori_loop(0, TOK // 16, norm, 0)
    send_own("n")

    def pass_neighbours(a):
        recv((a, "r"))
        send((a, "fr"), toks[a].at[tok_rows(3, c, 0, 64)], toks[a].at[tok_rows(2, c, 0, 64)], xr)
        send((a, "s3"), toks[a].at[tok_rows(3, c)], toks[a].at[tok_rows(3, c)], sib)
        recv((a, "l"))
        send((a, "fl"), toks[a].at[tok_rows(1, c, 64, 64)], toks[a].at[tok_rows(2, c, 64, 64)], xl)
        send((a, "s1"), toks[a].at[tok_rows(1, c)], toks[a].at[tok_rows(1, c)], sib)

    def pass_opposite(a):
        recv((a, "fr"), (a, "fl"))
        send((a, "s2"), toks[a].at[tok_rows(2, c)], toks[a].at[tok_rows(2, c)], sib)

    def share(key, rows, peer):
        send(("wy", key), w.at[kind, rows], w.at[kind, rows], peer)

    def pass_w1(i):
        recv(("w0", i))
        send(("w1", i), w.at[kind, chunk(1, i)], w.at[kind, chunk(3, i)], z_in)
        share((1, i), chunk(1, i), (yr, yr, yl, yl)[i])

    def pass_w3(i):
        recv(("w1", i))
        if i == 0:
            extra = rows_of(3, 0, 16), rows_of(2, 0, 16)
            send(("w3", "x"), w.at[kind, extra[0]], w.at[kind, extra[1]], z_out, zl == 1)
            for n in range(2):
                there = rows_of(2, from_in + 48 * n, 48)
                make(("w3", n), w.at[kind, rows_of(3, from_in + 48 * n, 48)], w.at[kind, there], z_out)
        pl.when(zl == 1 - i // 2)(copies["w3", i % 2].start)
        share((3, i), chunk(3, i), (yl, yl, yr, yr)[i])

    def pass_w2(n):
        recv(("w3", n))
        rows = rows_of(2, from_out + 48 * n, 48)
        send(("w2", n), w.at[kind, rows], w.at[kind, rows], z_in)
        share((2, "o", n), rows, yr)
        if n == 1:
            recv(("w3", "x"), when=zl == 0)
            rows = rows_of(2, 0, 16)
            send(("w2", "x"), w.at[kind, rows], w.at[kind, rows], z_in, zl == 0)

    def pass_last():
        for n in range(2):
            recv(("w2", n))
            share((2, "i", n), rows_of(2, from_in + 48 * n, 48), yl)
        recv(("w2", "x"), when=zl == 1)
        share((2, "x"), rows_of(2, 0, 16), yl)

    def all_w(slot):
        recv(*[key for key in copies if key[0] == "wy" and key[1][0] == slot])

    def forward(slot, group):
        r = pl.ds(slot * HALF, HALF)
        t = pl.ds(pl.multiple_of(group * GROUP, GROUP), GROUP)
        nt = (((1,), (1,)), ((), ()))
        pre = lax.dot_general(w[0, r], tok_n[t], nt, preferred_element_type=F32)
        dhidden = lax.dot_general(w[1, r], tok_u[t], nt, preferred_element_type=F32)
        hidden, slope = gelu_parts(pre)
        hid[r, t] = hidden.astype(BF16)
        dpre[r, t] = (dhidden * slope).astype(BF16)

    def forward_all(slot, first=0):
        def one(group, _):
            forward(slot, group)
            return 0

        lax.fori_loop(first, 4, one, 0)

    def grads(slot):
        r = pl.ds(slot * HALF, HALF)

        def columns(cols):
            up = jnp.dot(dpre[r], tok_n[:, cols], preferred_element_type=F32)
            g[0, r, cols] = (up * GRAD_SCALE).astype(BF16)
            down = jnp.dot(hid[r], tok_u[:, cols], preferred_element_type=F32)
            g[1, r, cols] = (down * GRAD_SCALE).astype(BF16)

        def tile(n, _):
            columns(pl.ds(pl.multiple_of(n * 256, 256), 256))
            return 0

        lax.fori_loop(0, 6, tile, 0)
        columns(pl.ds(1536, 128))

    def window(owner, first=0, cols=WIN):
        return pl.ds(pl.multiple_of(((owner + 8) % 4) * 384 + first, 128), cols)

    def rows16(i):
        return pl.ds(pl.multiple_of(i * 16, 16), 16)

    def slot16(slot, i):
        return pl.ds(pl.multiple_of(slot * HALF + i * 16, 16), 16)

    def kinds(part):
        return pl.ds(0, 2) if part[1] is None else pl.ds(part[1], 1)

    def y1(*part):
        r, k = pl.ds(part[0] * HALF, HALF), kinds(part)
        left, right = pl.ds(0, 256), pl.ds(256, 256)
        send(("yo", part, 0), g.at[k, r, window(y + 2, 0, 256)], yo_in.at[part[0], 0, k], yr)
        send(("yo", part, 1), g.at[k, r, window(y + 2, 256, 256)], yo_in.at[part[0], 1, k], yl)
        send(("yd", part, 0), g.at[k, r, window(y + 1, 256, 256)], nb_in.at[part[0], 0, k, :, right], yr)
        send(("yd", part, 1), g.at[k, r, window(y - 1, 0, 256)], nb_in.at[part[0], 1, k, :, left], yl)

    def y2(*part):
        slot, k = part[0], kinds(part)
        for way, owner, first, peer in ((0, y + 1, 0, yr), (1, y - 1, 256, yl)):
            recv(("yo", part, way))
            cols = window(owner, first, 256)

            def add(i, _):
                here = rows16(i)
                ya_st[slot, way, k, here] = (
                    g[k, slot16(slot, i), cols].astype(F32) + yo_in[slot, way, k, here].astype(F32)
                ).astype(BF16)
                return 0

            lax.fori_loop(0, HALF // 16, add, 0)
            send(("ya", part, way), ya_st.at[slot, way, k], nb_in.at[slot, way, k, :, pl.ds(first, 256)], peer)

    def y3(*part):
        slot, k = part[0], kinds(part)
        recv(("yd", part, 0), ("yd", part, 1), ("ya", part, 0), ("ya", part, 1))
        cols = window(y)

        def add(i, _):
            here = rows16(i)
            ysum[slot, k, here] = (
                g[k, slot16(slot, i), cols].astype(F32)
                + nb_in[slot, 0, k, here].astype(F32)
                + nb_in[slot, 1, k, here].astype(F32)
            ).astype(BF16)
            return 0

        lax.fori_loop(0, HALF // 16, add, 0)
        if slot == 2:
            send(("zb", 2), ysum.at[2, 1 - mine], z_sum.at[1], z_other[2])
            send(("za", 2), ysum.at[2, mine], z_sum.at[2], z_same[2])
        elif slot == 0:
            if ("zb", 0) not in copies:
                make(("zb", 0), ysum.at[0, 1 - mine], z_sum.at[0], z_other[0])
            pl.when(mine != part[1])(copies["zb", 0].start)
        else:
            send(("zb", slot), ysum.at[slot, part[1]], z_sum.at[3], z_other[slot], mine != part[1])
            send(("za", slot), ysum.at[slot, part[1]], z_sum.at[4], z_same[slot], mine == part[1])

    def pair_send(k):
        send(("pair", k), g.at[k, pl.ds((3, 1)[k] * HALF, HALF)], pair_in.at[k], (z_in, z_out)[k])

    def pair_add(k):
        recv(("pair", k))

        def add(i, _):
            here = slot16((1, 0)[k], i)
            g[k, here] = (g[k, here].astype(F32) + pair_in[k, rows16(i)].astype(F32)).astype(BF16)
            return 0

        lax.fori_loop(0, HALF // 16, add, 0)

    def back(group):
        t = pl.ds(group * GROUP, GROUP)
        rows = dpre[:, t].T

        def columns(cols):
            part = jnp.dot(rows, w[0, :, cols], preferred_element_type=F32).astype(BF16)
            dn[group, 0, :, cols] = part[:TOK]
            dn[group, 1, :, cols] = part[TOK:]

        def tile(n, _):
            columns(pl.ds(pl.multiple_of(n * 256, 256), 256))
            return 0

        lax.fori_loop(0, 6, tile, 0)
        columns(pl.ds(1536, 128))
        send(("dn", group), dn.at[group, 1 - c], dn_sib.at[group], sib)

    def dn_pass(group, peer):
        recv(("dn", group))

        def add(i, _):
            here = rows16(i)
            dn_st[group - 1, here] = (dn[group, c, here].astype(F32) + dn_sib[group, here].astype(F32)).astype(BF16)
            return 0

        lax.fori_loop(0, TOK // 16, add, 0)
        send(("dx", group), dn_st.at[group - 1], dn_in.at[group - 1], peer)

    pass_w1(0)
    pass_neighbours("u")
    pass_w1(1)
    recv(("u", "s0"), ("n", "s0"))
    forward(0, 0)
    pass_w1(2)
    pass_w3(0)
    pass_w1(3)
    pass_neighbours("n")
    pass_w3(1)
    recv(("u", "s1"), ("n", "s1"))
    forward(0, 1)
    pass_w3(2)
    recv(("u", "s3"), ("n", "s3"))
    forward(0, 3)
    pass_w3(3)
    pass_opposite("u")
    pass_opposite("n")
    all_w(1)
    forward(1, 0)
    recv(("u", "s2"), ("n", "s2"))
    forward(0, 2)
    grads(0)
    y1(0, 0)
    pass_w2(0)
    forward_all(1, 1)
    grads(1)
    pair_send(1)
    pass_w2(1)
    all_w(3)
    forward_all(3)
    grads(3)
    pair_send(0)
    y1(3, 1)
    pass_last()
    y2(0, 0)
    all_w(2)
    forward_all(2)
    grads(2)
    y1(2, None)
    y2(3, 1)
    y3(0, 0)
    back(2)
    pair_add(1)
    y1(0, 1)
    back(1)
    y2(2, None)
    pair_add(0)
    y1(1, 0)
    y3(3, 1)
    back(3)
    y2(0, 1)
    back(0)
    y2(1, 0)
    y3(2, None)
    dn_pass(2, x_far)
    dn_pass(1, xr)
    dn_pass(3, xl)
    y3(0, 1)
    y3(1, 0)

    recv(("dn", 0), ("dx", 1), ("dx", 2), ("dx", 3))

    def finish(i, _):
        here = rows16(i)
        gain = gain_ref[...]
        wide = x_ref[here].astype(F32)
        inv = lax.rsqrt(jnp.mean(wide * wide, axis=-1, keepdims=True) + norm_eps)
        unit = wide * inv
        dnormed = dn[0, c, here].astype(F32) + dn_sib[0, here].astype(F32)
        for k in range(3):
            dnormed += dn_in[k, here].astype(F32)
        dunit = dnormed * gain
        project = jnp.mean(dunit * unit, axis=-1, keepdims=True)
        grad_ref[here] = (up_ref[here].astype(F32) + inv * (dunit - unit * project)).astype(BF16)
        return 0

    lax.fori_loop(0, TOK // 16, finish, 0)

    recv(("zb", 0), ("zb", 2), ("za", 2))
    recv(("zb", 1), ("za", 1), when=mine == 0)
    recv(("zb", 3), ("za", 3), when=mine == 1)
    total[:, pl.ds(WIN, 128)] = jnp.zeros((16, 128), F32)

    def split(i, _):
        here = rows16(i)
        rows = ysum[0, mine, here].astype(F32)
        for k in range(5):
            rows += z_sum[k, here].astype(F32)
        total[:, pl.ds(0, WIN)] = rows
        for q in range(4):
            turned = pltpu.roll(total[...], (WIN + 128 - 104 * q) - 32 * y, 1)
            fin_st[q, here] = turned[:, :128].astype(BF16)
        return 0

    lax.fori_loop(0, HALF // 16, split, 0)
    me = 2 * zl + c
    for key, device, to in (("sib", sib, 2 * zl + 1 - c), ("in", z_in, 2 * (1 - zl) + c), ("cross", z_cross, 2 * (1 - zl) + 1 - c)):
        send(("f", key), fin_st.at[to], fin_in.at[me], device)

    def keep(i, _):
        fin_in[me, rows16(i)] = fin_st[me, rows16(i)]
        return 0

    lax.fori_loop(0, HALF // 16, keep, 0)
    recv(("f", "sib"), ("f", "in"), ("f", "cross"))

    for q in range(2):
        rows = (HALF, 400 - HALF)[q]
        up_out[pl.ds(q * HALF, rows), :] = fin_in[q, pl.ds(0, rows)].astype(F32)[:, :104]
        down_out[pl.ds(q * HALF, rows), :] = fin_in[2 + q, pl.ds(0, rows)].astype(F32)[:, :104]
    for key, copy in copies.items():
        if key in only:
            pl.when(only[key])(copy.wait_send)
        else:
            copy.wait_send()


def body(inputs, gain, w_up, w_down, upstream):
    vmem = pl.BlockSpec(memory_space=pltpu.VMEM)
    input_grad, up_grad, down_grad = pl.pallas_call(
        kernel,
        out_shape=(
            jax.ShapeDtypeStruct((TOK, D), BF16),
            jax.ShapeDtypeStruct((400, 104), F32),
            jax.ShapeDtypeStruct((400, 104), F32),
        ),
        in_specs=[vmem] * 5,
        out_specs=(vmem,) * 3,
        scratch_shapes=[
            pltpu.VMEM((T, D), BF16),
            pltpu.VMEM((T, D), BF16),
            pltpu.VMEM((2, HID, D), BF16),
            pltpu.VMEM((HID, T), BF16),
            pltpu.VMEM((HID, T), BF16),
            pltpu.VMEM((2, HID, D), BF16),
            pltpu.VMEM((4, 2, 2, HALF, 256), BF16),
            pltpu.VMEM((4, 2, 2, HALF, 256), BF16),
            pltpu.VMEM((4, 2, 2, HALF, WIN), BF16),
            pltpu.VMEM((4, 2, HALF, WIN), BF16),
            pltpu.VMEM((5, HALF, WIN), BF16),
            pltpu.VMEM((2, HALF, D), BF16),
            pltpu.VMEM((16, WIN + 128), F32),
            pltpu.VMEM((4, HALF, 128), BF16),
            pltpu.VMEM((4, HALF, 128), BF16),
            pltpu.VMEM((4, 2, TOK, D), BF16),
            pltpu.VMEM((4, TOK, D), BF16),
            pltpu.VMEM((3, TOK, D), BF16),
            pltpu.VMEM((3, TOK, D), BF16),
            pltpu.SemaphoreType.DMA((N_SEM,)),
            pltpu.SemaphoreType.DMA((N_SEM,)),
        ],
        compiler_params=pltpu.CompilerParams(
            collective_id=1, has_side_effects=True, vmem_limit_bytes=60 * 2**20
        ),
        name="block_backward",
    )(inputs, upstream, gain.astype(F32).reshape(1, D), w_up.T, w_down)
    return input_grad, up_grad.T, down_grad


def solution(mesh):
    in_specs = (
        P(("dp", "tensor"), None),
        P(),
        P(None, "tensor"),
        P("tensor", None),
        P(("dp", "tensor"), None),
    )
    out_specs = (P(("dp", "tensor"), None), P("dp", "tensor"), P("tensor", "dp"))
    return jax.shard_map(body, mesh=mesh, in_specs=in_specs, out_specs=out_specs, check_vma=False)
```

```python
import jax
import jax.numpy as jnp
from jax import lax
from jax.experimental import pallas as pl
from jax.experimental.pallas import tpu as pltpu
from jax.sharding import PartitionSpec as P

MESH = pl.DeviceIdType.MESH
F32, BF16 = jnp.float32, jnp.bfloat16

norm_eps = 1e-06
D = 1664
TOK = 128
GROUP = 2 * TOK
T = 4 * GROUP
HALF = 208
HID = 4 * HALF
WIN = 512
CHUNKS = ((0, 64), (64, 48), (112, 48), (160, 48))
N_SEM = 96
GRAD_SCALE = float(32768) ** (-0.5)

FIRST = (0, HALF, 3 * HALF, 2 * HALF)


def gelu_parts(pre):
    cdf = 0.5 * (1.0 + lax.erf(pre * 0.7071067811865476))
    pdf = jnp.exp(-0.5 * pre * pre) * 0.3989422804014327
    return (pre * cdf, cdf + pre * pdf)


def place(x, y, z, c):
    x, y, z = (x + 8) % 4, (y + 8) % 4, (z + 16) % 8
    return (y * 4 + (z % 2) * 2 + c, x * 4 + z // 2)


def kernel(
    x_ref, up_ref, gain_ref, wu_ref, wd_ref, grad_ref, up_out, down_out,
    tok_n, tok_u, w, hid, dpre, g, yo_in, ya_st, nb_in, ysum, z_sum, pair_in, total, fin_st, fin_in,
    dn, dn_sib, dn_st, dn_in, ss, rs,
):
    dp, tensor = lax.axis_index("dp"), lax.axis_index("tensor")
    y, zl, c = dp // 4, (dp // 2) % 2, dp % 2
    x, z = tensor // 4, (tensor % 4) * 2 + zl
    step_out = 2 * zl - 1
    sib = place(x, y, z, 1 - c)
    xr, xl = place(x + 1, y, z, c), place(x - 1, y, z, c)
    x_far = place(x + 2, y, z, c)
    yr, yl = place(x, y + 1, z, c), place(x, y - 1, z, c)
    z_out, z_in = place(x, y, z + step_out, c), place(x, y, z - step_out, c)
    z_cross = place(x, y, z - step_out, 1 - c)
    z_same = {1: place(x, y, z + 2 * step_out, c), 2: place(x, y, z + 4, c), 3: place(x, y, z - 2 * step_out, c)}
    z_other = {0: z_in, 1: z_out, 2: place(x, y, z + 3 * step_out, c), 3: place(x, y, z - 3 * step_out, c)}
    kind = y % 2
    from_out, from_in = 16 + 96 * zl, 112 - 96 * zl
    mine = zl

    barrier = pltpu.get_barrier_semaphore()
    peers = [sib, xr, xl, x_far, yr, yl, z_cross, *z_same.values(), *z_other.values()]
    for peer in peers:
        pl.semaphore_signal(barrier, inc=1, device_id=peer, device_id_type=MESH)

    copies, only = {}, {}

    def make(key, src, dst, device):
        i = len(copies)
        copies[key] = pltpu.make_async_remote_copy(
            src_ref=src, dst_ref=dst, send_sem=ss.at[i], recv_sem=rs.at[i], device_id=device, device_id_type=MESH
        )

    def start(key, when=None):
        if when is None:
            copies[key].start()
        else:
            only[key] = when
            pl.when(when)(copies[key].start)

    def send(key, src, dst, device, when=None):
        make(key, src, dst, device)
        start(key, when)

    def recv(*keys, when=None):
        for key in keys:
            if when is None:
                copies[key].wait_recv()
            else:
                pl.when(when)(copies[key].wait_recv)

    def tok_rows(group, core, first=0, rows=TOK):
        return pl.ds(pl.multiple_of(group * GROUP + core * TOK + first, 16), rows)

    gain = gain_ref[...].astype(F32).reshape(1, D)
    own = tok_rows(0, c)
    tok_u[own] = up_ref[...]
    toks = {"u": tok_u, "n": tok_n}

    def send_own(a):
        send((a, "r"), toks[a].at[own], toks[a].at[tok_rows(3, c)], xr)
        send((a, "l"), toks[a].at[own], toks[a].at[tok_rows(1, c)], xl)
        send((a, "s0"), toks[a].at[own], toks[a].at[own], sib)

    pl.semaphore_wait(barrier, len(peers))
    send_own("u")

    for k, ref in enumerate((wu_ref, wd_ref)):
        w[k, pl.ds(0, 192)] = ref[pl.ds(pl.multiple_of(c * HALF, 16), 192)]

        @pl.when(c == 0)
        def _():
            w[k, pl.ds(192, 16)] = ref[pl.ds(192, 16)]

        @pl.when(c == 1)
        def _():
            w[k, pl.ds(192, 16)] = jnp.zeros((16, D), BF16)

    def rows_of(slot, first, rows):
        return pl.ds(pl.multiple_of(FIRST[slot] + first, 16), rows)

    def chunk(slot, i):
        return rows_of(slot, *CHUNKS[i])

    for i in range(4):
        send(("w0", i), w.at[kind, chunk(0, i)], w.at[kind, chunk(1, i)], z_out)

    def norm(i, _):
        r = pl.ds(pl.multiple_of(i * 16, 16), 16)
        wide = x_ref[r].astype(F32)
        inv = lax.rsqrt(jnp.mean(wide * wide, axis=-1, keepdims=True) + norm_eps)
        tok_n[tok_rows(0, c, i * 16, 16)] = (wide * inv * gain).astype(BF16)
        return 0

    lax.fori_loop(0, TOK // 16, norm, 0)
    send_own("n")

    def pass_neighbours(a):
        recv((a, "r"))
        send((a, "fr"), toks[a].at[tok_rows(3, c, 0, 64)], toks[a].at[tok_rows(2, c, 0, 64)], xr)
        send((a, "s3"), toks[a].at[tok_rows(3, c)], toks[a].at[tok_rows(3, c)], sib)
        recv((a, "l"))
        send((a, "fl"), toks[a].at[tok_rows(1, c, 64, 64)], toks[a].at[tok_rows(2, c, 64, 64)], xl)
        send((a, "s1"), toks[a].at[tok_rows(1, c)], toks[a].at[tok_rows(1, c)], sib)

    def pass_opposite(a):
        recv((a, "fr"), (a, "fl"))
        send((a, "s2"), toks[a].at[tok_rows(2, c)], toks[a].at[tok_rows(2, c)], sib)

    def share(key, rows, peer):
        send(("wy", key), w.at[kind, rows], w.at[kind, rows], peer)

    def pass_w1(i):
        recv(("w0", i))
        send(("w1", i), w.at[kind, chunk(1, i)], w.at[kind, chunk(3, i)], z_in)
        share((1, i), chunk(1, i), (yr, yr, yl, yl)[i])

    def pass_w3(i):
        recv(("w1", i))
        if i == 0:
            extra = rows_of(3, 0, 16), rows_of(2, 0, 16)
            send(("w3", "x"), w.at[kind, extra[0]], w.at[kind, extra[1]], z_out, zl == 1)
            for n in range(2):
                there = rows_of(2, from_in + 48 * n, 48)
                make(("w3", n), w.at[kind, rows_of(3, from_in + 48 * n, 48)], w.at[kind, there], z_out)
        pl.when(zl == 1 - i // 2)(copies["w3", i % 2].start)
        share((3, i), chunk(3, i), (yl, yl, yr, yr)[i])

    def pass_w2(n):
        recv(("w3", n))
        rows = rows_of(2, from_out + 48 * n, 48)
        send(("w2", n), w.at[kind, rows], w.at[kind, rows], z_in)
        share((2, "o", n), rows, yr)
        if n == 1:
            recv(("w3", "x"), when=zl == 0)
            rows = rows_of(2, 0, 16)
            send(("w2", "x"), w.at[kind, rows], w.at[kind, rows], z_in, zl == 0)

    def pass_last():
        for n in range(2):
            recv(("w2", n))
            share((2, "i", n), rows_of(2, from_in + 48 * n, 48), yl)
        recv(("w2", "x"), when=zl == 1)
        share((2, "x"), rows_of(2, 0, 16), yl)

    def all_w(slot):
        recv(*[key for key in copies if key[0] == "wy" and key[1][0] == slot])

    def forward(r, t):
        nt = (((1,), (1,)), ((), ()))
        pre = lax.dot_general(w[0, r], tok_n[t], nt, preferred_element_type=F32)
        dhidden = lax.dot_general(w[1, r], tok_u[t], nt, preferred_element_type=F32)
        hidden, slope = gelu_parts(pre)
        hid[r, t] = hidden.astype(BF16)
        dpre[r, t] = (dhidden * slope).astype(BF16)

    def forward_one(slot, group):
        forward(pl.ds(FIRST[slot], HALF), pl.ds(group * GROUP, GROUP))

    def forward_all(slot, slots=1):
        def one(i, _):
            forward(pl.ds(FIRST[slot], slots * HALF), pl.ds(pl.multiple_of(i * 512, 512), 512))
            return 0

        lax.fori_loop(0, 2, one, 0)

    def grads(slot, slots=1):
        r = pl.ds(FIRST[slot], slots * HALF)

        def columns(cols):
            up = jnp.dot(dpre[r], tok_n[:, cols], preferred_element_type=F32)
            g[0, r, cols] = (up * GRAD_SCALE).astype(BF16)
            down = jnp.dot(hid[r], tok_u[:, cols], preferred_element_type=F32)
            g[1, r, cols] = (down * GRAD_SCALE).astype(BF16)

        def tile(n, _):
            columns(pl.ds(pl.multiple_of(n * 512, 512), 512))
            return 0

        lax.fori_loop(0, 3, tile, 0)
        columns(pl.ds(1536, 128))

    def window(owner, first=0, cols=WIN):
        return pl.ds(pl.multiple_of(((owner + 8) % 4) * 384 + first, 128), cols)

    def rows16(i):
        return pl.ds(pl.multiple_of(i * 16, 16), 16)

    def slot16(slot, i):
        return pl.ds(pl.multiple_of(FIRST[slot] + i * 16, 16), 16)

    def kinds(part):
        return pl.ds(0, 2) if part[1] is None else pl.ds(part[1], 1)

    def y1(*part):
        r, k = pl.ds(FIRST[part[0]], HALF), kinds(part)
        left, right = pl.ds(0, 256), pl.ds(256, 256)
        send(("yo", part, 0), g.at[k, r, window(y + 2, 0, 256)], yo_in.at[part[0], 0, k], yr)
        send(("yo", part, 1), g.at[k, r, window(y + 2, 256, 256)], yo_in.at[part[0], 1, k], yl)
        send(("yd", part, 0), g.at[k, r, window(y + 1, 256, 256)], nb_in.at[part[0], 0, k, :, right], yr)
        send(("yd", part, 1), g.at[k, r, window(y - 1, 0, 256)], nb_in.at[part[0], 1, k, :, left], yl)

    def y2(*part):
        slot, k = part[0], kinds(part)
        for way, owner, first, peer in ((0, y + 1, 0, yr), (1, y - 1, 256, yl)):
            recv(("yo", part, way))
            cols = window(owner, first, 256)

            def add(i, _):
                here = rows16(i)
                ya_st[slot, way, k, here] = (
                    g[k, slot16(slot, i), cols].astype(F32) + yo_in[slot, way, k, here].astype(F32)
                ).astype(BF16)
                return 0

            lax.fori_loop(0, HALF // 16, add, 0)
            send(("ya", part, way), ya_st.at[slot, way, k], nb_in.at[slot, way, k, :, pl.ds(first, 256)], peer)

    def y3(*part):
        slot, k = part[0], kinds(part)
        recv(("yd", part, 0), ("yd", part, 1), ("ya", part, 0), ("ya", part, 1))
        cols = window(y)

        def add(i, _):
            here = rows16(i)
            ysum[slot, k, here] = (
                g[k, slot16(slot, i), cols].astype(F32)
                + nb_in[slot, 0, k, here].astype(F32)
                + nb_in[slot, 1, k, here].astype(F32)
            ).astype(BF16)
            return 0

        lax.fori_loop(0, HALF // 16, add, 0)
        if slot == 2:
            send(("zb", 2), ysum.at[2, 1 - mine], z_sum.at[1], z_other[2])
            send(("za", 2), ysum.at[2, mine], z_sum.at[2], z_same[2])
        elif slot == 0:
            if ("zb", 0) not in copies:
                make(("zb", 0), ysum.at[0, 1 - mine], z_sum.at[0], z_other[0])
            pl.when(mine != part[1])(copies["zb", 0].start)
        else:
            send(("zb", slot), ysum.at[slot, part[1]], z_sum.at[3], z_other[slot], mine != part[1])
            send(("za", slot), ysum.at[slot, part[1]], z_sum.at[4], z_same[slot], mine == part[1])

    def pair_send(k):
        send(("pair", k), g.at[k, pl.ds(FIRST[(3, 1)[k]], HALF)], pair_in.at[k], (z_in, z_out)[k])

    def pair_add(k):
        recv(("pair", k))

        def add(i, _):
            here = slot16((1, 0)[k], i)
            g[k, here] = (g[k, here].astype(F32) + pair_in[k, rows16(i)].astype(F32)).astype(BF16)
            return 0

        lax.fori_loop(0, HALF // 16, add, 0)

    def back(group):
        t = pl.ds(group * GROUP, GROUP)
        rows = dpre[:, t].T

        def columns(cols):
            part = jnp.dot(rows, w[0, :, cols], preferred_element_type=F32).astype(BF16)
            dn[group, 0, :, cols] = part[:TOK]
            dn[group, 1, :, cols] = part[TOK:]

        def tile(n, _):
            columns(pl.ds(pl.multiple_of(n * 512, 512), 512))
            return 0

        lax.fori_loop(0, 3, tile, 0)
        columns(pl.ds(1536, 128))
        send(("dn", group), dn.at[group, 1 - c], dn_sib.at[group], sib)

    def dn_pass(group, peer):
        recv(("dn", group))

        def add(i, _):
            here = rows16(i)
            dn_st[group - 1, here] = (dn[group, c, here].astype(F32) + dn_sib[group, here].astype(F32)).astype(BF16)
            return 0

        lax.fori_loop(0, TOK // 16, add, 0)
        send(("dx", group), dn_st.at[group - 1], dn_in.at[group - 1], peer)

    pass_w1(0)
    pass_neighbours("u")
    pass_w1(1)
    recv(("u", "s0"), ("n", "s0"))
    forward_one(0, 0)
    pass_w1(2)
    pass_w3(0)
    pass_w1(3)
    pass_neighbours("n")
    pass_w3(1)
    pass_w3(2)
    recv(("u", "s1"), ("n", "s1"))
    forward_one(0, 1)
    pass_w3(3)
    pass_opposite("u")
    recv(("u", "s3"), ("n", "s3"))
    forward_one(0, 3)
    pass_w2(0)
    pass_opposite("n")
    recv(("u", "s2"), ("n", "s2"))
    forward_one(0, 2)
    pass_w2(1)
    grads(0)
    y1(0, 0)
    pass_last()
    all_w(1)
    all_w(3)
    forward_all(1, 2)
    y2(0, 0)
    grads(1, 2)
    pair_send(1)
    pair_send(0)
    y1(3, 1)
    all_w(2)
    forward_all(2)
    grads(2)
    y1(2, None)
    y2(3, 1)
    y3(0, 0)
    back(2)
    back(1)
    dn_pass(2, x_far)
    y2(2, None)
    pair_add(1)
    y1(0, 1)
    back(3)
    dn_pass(1, xr)
    pair_add(0)
    y1(1, 0)
    back(0)
    y3(3, 1)
    dn_pass(3, xl)
    y2(0, 1)
    y3(2, None)
    y2(1, 0)
    y3(0, 1)
    y3(1, 0)

    recv(("dn", 0), ("dx", 1), ("dx", 2), ("dx", 3))

    def finish(i, _):
        here = rows16(i)
        wide = x_ref[here].astype(F32)
        inv = lax.rsqrt(jnp.mean(wide * wide, axis=-1, keepdims=True) + norm_eps)
        unit = wide * inv
        dnormed = dn[0, c, here].astype(F32) + dn_sib[0, here].astype(F32)
        for k in range(3):
            dnormed += dn_in[k, here].astype(F32)
        dunit = dnormed * gain
        project = jnp.mean(dunit * unit, axis=-1, keepdims=True)
        grad_ref[here] = (up_ref[here].astype(F32) + inv * (dunit - unit * project)).astype(BF16)
        return 0

    lax.fori_loop(0, TOK // 16, finish, 0)

    recv(("zb", 0), ("zb", 2), ("za", 2))
    recv(("zb", 1), ("za", 1), when=mine == 0)
    recv(("zb", 3), ("za", 3), when=mine == 1)
    total[:, pl.ds(WIN, 128)] = jnp.zeros((16, 128), F32)

    def split(i, _):
        here = rows16(i)
        rows = ysum[0, mine, here].astype(F32)
        for k in range(5):
            rows += z_sum[k, here].astype(F32)
        total[:, pl.ds(0, WIN)] = rows
        for q in range(4):
            turned = pltpu.roll(total[...], (WIN + 128 - 104 * q) - 32 * y, 1)
            fin_st[q, here] = turned[:, :128].astype(BF16)
        return 0

    lax.fori_loop(0, HALF // 16, split, 0)
    me = 2 * zl + c
    for key, device, to in (("sib", sib, 2 * zl + 1 - c), ("in", z_in, 2 * (1 - zl) + c), ("cross", z_cross, 2 * (1 - zl) + 1 - c)):
        send(("f", key), fin_st.at[to], fin_in.at[me], device)

    def keep(i, _):
        fin_in[me, rows16(i)] = fin_st[me, rows16(i)]
        return 0

    lax.fori_loop(0, HALF // 16, keep, 0)
    recv(("f", "sib"), ("f", "in"), ("f", "cross"))

    for q in range(2):
        rows = (HALF, 400 - HALF)[q]
        up_out[pl.ds(q * HALF, rows), :] = fin_in[q, pl.ds(0, rows)].astype(F32)[:, :104]
        down_out[pl.ds(q * HALF, rows), :] = fin_in[2 + q, pl.ds(0, rows)].astype(F32)[:, :104]
    for key, copy in copies.items():
        if key in only:
            pl.when(only[key])(copy.wait_send)
        else:
            copy.wait_send()


def body(inputs, gain, w_up, w_down, upstream):
    vmem = pl.BlockSpec(memory_space=pltpu.VMEM)
    input_grad, up_grad, down_grad = pl.pallas_call(
        kernel,
        out_shape=(
            jax.ShapeDtypeStruct((TOK, D), BF16),
            jax.ShapeDtypeStruct((400, 104), F32),
            jax.ShapeDtypeStruct((400, 104), F32),
        ),
        in_specs=[vmem] * 5,
        out_specs=(vmem,) * 3,
        scratch_shapes=[
            pltpu.VMEM((T, D), BF16),
            pltpu.VMEM((T, D), BF16),
            pltpu.VMEM((2, HID, D), BF16),
            pltpu.VMEM((HID, T), BF16),
            pltpu.VMEM((HID, T), BF16),
            pltpu.VMEM((2, HID, D), BF16),
            pltpu.VMEM((4, 2, 2, HALF, 256), BF16),
            pltpu.VMEM((4, 2, 2, HALF, 256), BF16),
            pltpu.VMEM((4, 2, 2, HALF, WIN), BF16),
            pltpu.VMEM((4, 2, HALF, WIN), BF16),
            pltpu.VMEM((5, HALF, WIN), BF16),
            pltpu.VMEM((2, HALF, D), BF16),
            pltpu.VMEM((16, WIN + 128), F32),
            pltpu.VMEM((4, HALF, 128), BF16),
            pltpu.VMEM((4, HALF, 128), BF16),
            pltpu.VMEM((4, 2, TOK, D), BF16),
            pltpu.VMEM((4, TOK, D), BF16),
            pltpu.VMEM((3, TOK, D), BF16),
            pltpu.VMEM((3, TOK, D), BF16),
            pltpu.SemaphoreType.DMA((N_SEM,)),
            pltpu.SemaphoreType.DMA((N_SEM,)),
        ],
        compiler_params=pltpu.CompilerParams(
            collective_id=1, has_side_effects=True, vmem_limit_bytes=60 * 2**20
        ),
        name="block_backward",
    )(inputs, upstream, gain, w_up.T, w_down)
    return input_grad, up_grad.T, down_grad


def solution(mesh):
    in_specs = (
        P(("dp", "tensor"), None),
        P(),
        P(None, "tensor"),
        P("tensor", None),
        P(("dp", "tensor"), None),
    )
    out_specs = (P(("dp", "tensor"), None), P("dp", "tensor"), P("tensor", "dp"))
    return jax.shard_map(body, mesh=mesh, in_specs=in_specs, out_specs=out_specs, check_vma=False)
```

```python
import jax
import jax.numpy as jnp
from jax import lax
from jax.experimental import pallas as pl
from jax.experimental.pallas import tpu as pltpu
from jax.sharding import PartitionSpec as P

MESH = pl.DeviceIdType.MESH
PRE = ("outer", "inner", "swap")
F32, BF16 = jnp.float32, jnp.bfloat16

norm_eps = 1e-06
D = 1664
TOK = 128
GROUP = 2 * TOK
T = 4 * GROUP
HALF = 208
HID = 4 * HALF
WIN = 512
CHUNKS = ((0, 64), (112, 48), (64, 48), (160, 48))
N_SEM = 96
RIGHT, LEFT, OPPOSITE = 1, 2, 3
GRAD_SCALE = float(32768) ** (-0.5)

FIRST = (0, HALF, 3 * HALF, 2 * HALF)


def gelu_parts(pre):
    cdf = 0.5 * (1.0 + lax.erf(pre * 0.7071067811865476))
    pdf = jnp.exp(-0.5 * pre * pre) * 0.3989422804014327
    return (pre * cdf, cdf + pre * pdf)


def place(x, y, z, c):
    x, y, z = (x + 8) % 4, (y + 8) % 4, (z + 16) % 8
    return (y * 4 + (z % 2) * 2 + c, x * 4 + z // 2)


def kernel(
    x_hbm, up_hbm, gain_ref, wu_hbm, wd_hbm, grad_ref, up_out, down_out,
    x_ref, tok_n, tok_u, w, hid, dpre, acc, g, yo_in, ya_st, nb_in, ysum, za_in, zb_in, pair_in, total, fin_st, fin_in,
    dn, dn_sib, dn_st, dn_in, local, ss, rs,
):
    dp, tensor = lax.axis_index("dp"), lax.axis_index("tensor")
    y, zl, c = dp // 4, (dp // 2) % 2, dp % 2
    x, z = tensor // 4, (tensor % 4) * 2 + zl
    step_out = 2 * zl - 1
    sib = place(x, y, z, 1 - c)
    xr, xl = place(x + 1, y, z, c), place(x - 1, y, z, c)
    x_far = place(x + 2, y, z, c)
    yr, yl = place(x, y + 1, z, c), place(x, y - 1, z, c)
    z_out, z_in = place(x, y, z + step_out, c), place(x, y, z - step_out, c)
    z_cross = place(x, y, z - step_out, 1 - c)
    z_same = {1: place(x, y, z + 2 * step_out, c), 2: place(x, y, z + 4, c), 3: place(x, y, z - 2 * step_out, c)}
    z_other = {0: z_in, 1: z_out, 2: place(x, y, z + 3 * step_out, c), 3: place(x, y, z - 3 * step_out, c)}
    kind = y % 2
    from_out, from_in = 16 + 96 * zl, 112 - 96 * zl
    mine = zl

    own = pl.ds(pl.multiple_of(c * TOK, 16), TOK)
    load_up = pltpu.make_async_copy(up_hbm, tok_u.at[own], local.at[0])
    load_up.start()
    barrier = pltpu.get_barrier_semaphore()
    peers = [sib, xr, xl, x_far, yr, yl, z_cross, *z_same.values(), *z_other.values()]
    for peer in peers:
        pl.semaphore_signal(barrier, inc=1, device_id=peer, device_id_type=MESH)

    copies, only, summed = {}, {}, {}

    def make(key, src, dst, device):
        i = len(copies)
        copies[key] = pltpu.make_async_remote_copy(
            src_ref=src, dst_ref=dst, send_sem=ss.at[i], recv_sem=rs.at[i], device_id=device, device_id_type=MESH
        )

    def start(key, when=None):
        if when is None:
            copies[key].start()
        else:
            only[key] = when
            pl.when(when)(copies[key].start)

    def send(key, src, dst, device, when=None):
        make(key, src, dst, device)
        start(key, when)

    def recv(*keys, when=None):
        for key in keys:
            if when is None:
                copies[key].wait_recv()
            else:
                pl.when(when)(copies[key].wait_recv)

    def tok_rows(group, core, first=0, rows=TOK):
        return pl.ds(pl.multiple_of(group * GROUP + core * TOK + first, 16), rows)

    load_w = [
        pltpu.make_async_copy(ref.at[pl.ds(pl.multiple_of(c * HALF, 16), 192)], w.at[k, pl.ds(0, 192)], local.at[1 + k])
        for k, ref in enumerate((wu_hbm, wd_hbm))
    ]
    load_rest = [
        pltpu.make_async_copy(ref.at[pl.ds(192, 16)], w.at[k, pl.ds(192, 16)], local.at[3 + k])
        for k, ref in enumerate((wu_hbm, wd_hbm))
    ]
    load_x = pltpu.make_async_copy(x_hbm, x_ref, local.at[5])
    for copy in load_w:
        copy.start()

    @pl.when(c == 0)
    def _():
        for copy in load_rest:
            copy.start()

    @pl.when(c == 1)
    def _():
        w[:, pl.ds(192, 16)] = jnp.zeros((2, 16, D), BF16)

    load_x.start()
    toks = {"u": tok_u, "n": tok_n}

    def send_own(a):
        send((a, "r"), toks[a].at[own], toks[a].at[tok_rows(LEFT, c)], xr)
        send((a, "l"), toks[a].at[own], toks[a].at[tok_rows(RIGHT, c)], xl)
        send((a, "s", 0), toks[a].at[own], toks[a].at[own], sib)

    load_up.wait()
    pl.semaphore_wait(barrier, len(peers))
    send_own("u")
    for copy in load_w:
        copy.wait()

    @pl.when(c == 0)
    def _():
        for copy in load_rest:
            copy.wait()

    def rows_of(slot, first, rows):
        return pl.ds(pl.multiple_of(FIRST[slot] + first, 16), rows)

    def chunk(slot, i):
        return rows_of(slot, *CHUNKS[i])

    for i in range(4):
        send(("w0", i), w.at[kind, chunk(0, i)], w.at[kind, chunk(1, i)], z_out)

    gain = gain_ref[...].astype(F32).reshape(1, D)
    load_x.wait()
    def norm(i, _):
        r = pl.ds(pl.multiple_of(i * 16, 16), 16)
        wide = x_ref[r].astype(F32)
        inv = lax.rsqrt(jnp.mean(wide * wide, axis=-1, keepdims=True) + norm_eps)
        tok_n[tok_rows(0, c, i * 16, 16)] = (wide * inv * gain).astype(BF16)
        return 0

    lax.fori_loop(0, TOK // 16, norm, 0)
    send_own("n")

    def pass_neighbours(a):
        t = toks[a]
        recv((a, "r"))
        send((a, "fr"), t.at[tok_rows(LEFT, c, 0, 64)], t.at[tok_rows(OPPOSITE, c, 0, 64)], xr)
        send((a, "s", LEFT), t.at[tok_rows(LEFT, c)], t.at[tok_rows(LEFT, c)], sib)
        recv((a, "l"))
        send((a, "fl"), t.at[tok_rows(RIGHT, c, 64, 64)], t.at[tok_rows(OPPOSITE, c, 64, 64)], xl)
        send((a, "s", RIGHT), t.at[tok_rows(RIGHT, c)], t.at[tok_rows(RIGHT, c)], sib)

    def pass_opposite(a):
        recv((a, "fr"), (a, "fl"))
        send((a, "s", OPPOSITE), toks[a].at[tok_rows(OPPOSITE, c)], toks[a].at[tok_rows(OPPOSITE, c)], sib)

    def tokens(group):
        recv(("u", "s", group), ("n", "s", group))

    def share(key, rows, peer):
        send(("wy", key), w.at[kind, rows], w.at[kind, rows], peer)

    def pass_w1(i):
        recv(("w0", i))
        send(("w1", i), w.at[kind, chunk(1, i)], w.at[kind, chunk(3, i)], z_in)
        share((1, i), chunk(1, i), (yr, yl, yr, yl)[i])

    def far_out(key, k, i):
        if i == 0:
            send((key, "x"), w.at[k, rows_of(3, 0, 16)], w.at[k, rows_of(2, 0, 16)], z_out, zl == 1)
            for n in range(2):
                here, there = rows_of(3, from_in + 48 * n, 48), rows_of(2, from_in + 48 * n, 48)
                make((key, n), w.at[k, here], w.at[k, there], z_out)
        pl.when(zl == 1 - i % 2)(copies[key, i // 2].start)

    def far_in(key, came, k, n):
        recv((came, n))
        rows = rows_of(2, from_out + 48 * n, 48)
        send((key, n), w.at[k, rows], w.at[k, rows], z_in)
        if n == 1:
            recv((came, "x"), when=zl == 0)
            rows = rows_of(2, 0, 16)
            send((key, "x"), w.at[k, rows], w.at[k, rows], z_in, zl == 0)

    def pass_w3(i):
        recv(("w1", i))
        far_out("w3", kind, i)
        share((3, i), chunk(3, i), (yl, yr, yl, yr)[i])

    def pass_w2(n):
        far_in("w2", "w3", kind, n)

    def pass_v3(i):
        recv(("wy", (3, i)))
        far_out("v3", 1 - kind, i)

    def pass_v2(n):
        far_in("v2", "v3", 1 - kind, n)

    def far_w():
        for key in ("w2", "v2"):
            recv((key, 0), (key, 1))
            recv((key, "x"), when=zl == 1)

    def all_w(slot):
        recv(*[key for key in copies if key[0] == "wy" and key[1][0] == slot])

    def forward(r, t):
        nt = (((1,), (1,)), ((), ()))
        pre = lax.dot_general(w[0, r], tok_n[t], nt, preferred_element_type=F32)
        dhidden = lax.dot_general(w[1, r], tok_u[t], nt, preferred_element_type=F32)
        hidden, slope = gelu_parts(pre)
        hid[r, t] = hidden.astype(BF16)
        dpre[r, t] = (dhidden * slope).astype(BF16)

    def forward_one(slot, group):
        forward(pl.ds(FIRST[slot], HALF), pl.ds(group * GROUP, GROUP))

    def forward_all(slot, slots=1):
        def one(i, _):
            forward(pl.ds(FIRST[slot], slots * HALF), pl.ds(pl.multiple_of(i * 512, 512), 512))
            return 0

        lax.fori_loop(0, 2, one, 0)

    def all_columns(columns):
        def tile(n, _):
            columns(pl.ds(pl.multiple_of(n * 512, 512), 512))
            return 0

        lax.fori_loop(0, 3, tile, 0)
        columns(pl.ds(1536, 128))

    def grads(kind, slot, slots=1):
        r = pl.ds(FIRST[slot], slots * HALF)
        left, right = ((dpre, tok_n), (hid, tok_u))[kind]

        def columns(cols):
            term = jnp.dot(left[r], right[:, cols], preferred_element_type=F32)
            g[kind, r, cols] = (term * GRAD_SCALE).astype(BF16)

        all_columns(columns)

    def grads_first(kind):
        r, t = pl.ds(0, HALF), pl.ds(0, 3 * GROUP)
        left, right = ((dpre, tok_n), (hid, tok_u))[kind]

        def columns(cols):
            acc[kind, :, cols] = jnp.dot(left[r, t], right[t, cols], preferred_element_type=F32)

        all_columns(columns)

    def grads_last(kind):
        r, t = pl.ds(0, HALF), pl.ds(3 * GROUP, GROUP)
        left, right = ((dpre, tok_n), (hid, tok_u))[kind]

        def columns(cols):
            term = acc[kind, :, cols] + jnp.dot(left[r, t], right[t, cols], preferred_element_type=F32)
            g[kind, r, cols] = (term * GRAD_SCALE).astype(BF16)

        all_columns(columns)

    def window(owner, first=0, cols=WIN):
        return pl.ds(pl.multiple_of(((owner + 8) % 4) * 384 + first, 128), cols)

    def rows16(i):
        return pl.ds(pl.multiple_of(i * 16, 16), 16)

    def slot16(slot, i):
        return pl.ds(pl.multiple_of(FIRST[slot] + i * 16, 16), 16)

    def kinds(part):
        return pl.ds(0, 2) if part[1] is None else pl.ds(mine if part[1] == "mine" else part[1], 1)

    def y1(*part):
        r, k = pl.ds(FIRST[part[0]], HALF), kinds(part)
        left, right = pl.ds(0, 256), pl.ds(256, 256)
        send(("yo", part, 0), g.at[k, r, window(y + 2, 0, 256)], yo_in.at[part[0], 0, k], yr)
        send(("yo", part, 1), g.at[k, r, window(y + 2, 256, 256)], yo_in.at[part[0], 1, k], yl)
        send(("yd", part, 0), g.at[k, r, window(y + 1, 256, 256)], nb_in.at[part[0], 0, k, :, right], yr)
        send(("yd", part, 1), g.at[k, r, window(y - 1, 0, 256)], nb_in.at[part[0], 1, k, :, left], yl)

    def y2(*part):
        slot, k = part[0], kinds(part)
        for way, owner, first, peer in ((0, y + 1, 0, yr), (1, y - 1, 256, yl)):
            recv(("yo", part, way))
            cols = window(owner, first, 256)

            def add(i, _):
                here = rows16(i)
                ya_st[slot, way, k, here] = (
                    g[k, slot16(slot, i), cols].astype(F32) + yo_in[slot, way, k, here].astype(F32)
                ).astype(BF16)
                return 0

            lax.fori_loop(0, HALF // 16, add, 0)
            send(("ya", part, way), ya_st.at[slot, way, k], nb_in.at[slot, way, k, :, pl.ds(first, 256)], peer)

    def y3(*part):
        slot, k = part[0], kinds(part)
        recv(("yd", part, 0), ("yd", part, 1), ("ya", part, 0), ("ya", part, 1))
        cols = window(y)

        def add(i, _):
            here = rows16(i)
            ysum[slot, k, here] = (
                g[k, slot16(slot, i), cols].astype(F32)
                + nb_in[slot, 0, k, here].astype(F32)
                + nb_in[slot, 1, k, here].astype(F32)
            ).astype(BF16)
            return 0

        lax.fori_loop(0, HALF // 16, add, 0)
        summed.setdefault(slot, []).append(part[1])
        if part[1] == "mine":
            send(("za", slot), ysum.at[slot, mine], za_in.at[slot - 1], z_same[slot])
            return
        if ("zb", slot) not in copies:
            make(("zb", slot), ysum.at[slot, 1 - mine], zb_in.at[slot], z_other[slot])
            if slot:
                make(("za", slot), ysum.at[slot, mine], za_in.at[slot - 1], z_same[slot])
        for key, when in (("zb", mine != part[1]), ("za", mine == part[1])):
            if (key, slot) in copies:
                if part[1] is None:
                    copies[key, slot].start()
                else:
                    pl.when(when)(copies[key, slot].start)

    def presum_send(key, kind, slot, device):
        send(key, g.at[kind, pl.ds(FIRST[slot], HALF)], pair_in.at[PRE.index(key)], device)

    def presum_add(key, kind, slot):
        recv(key)

        def add(i, _):
            here = slot16(slot, i)
            g[kind, here] = (
                g[kind, here].astype(F32) + pair_in[PRE.index(key), rows16(i)].astype(F32)
            ).astype(BF16)
            return 0

        lax.fori_loop(0, HALF // 16, add, 0)

    def outer_send():
        presum_send("outer", 1, 1, z_out)

    def outer_add():
        presum_add("outer", 1, 0)

    def inner_send():
        presum_send("inner", 0, 3, z_in)

    def inner_add():
        presum_add("inner", 0, 1)

    def swap_send():
        presum_send("swap", 1 - mine, 2, z_in)

    def swap_add():
        presum_add("swap", mine, 2)

    def back(group):
        t = pl.ds(group * GROUP, GROUP)
        rows = dpre[:, t].T

        def columns(cols):
            part = jnp.dot(rows, w[0, :, cols], preferred_element_type=F32).astype(BF16)
            dn[group, 0, :, cols] = part[:TOK]
            dn[group, 1, :, cols] = part[TOK:]

        all_columns(columns)
        send(("dn", group), dn.at[group, 1 - c], dn_sib.at[group], sib)

    def dn_pass(group, peer):
        recv(("dn", group))

        def add(i, _):
            here = rows16(i)
            dn_st[group - 1, here] = (dn[group, c, here].astype(F32) + dn_sib[group, here].astype(F32)).astype(BF16)
            return 0

        lax.fori_loop(0, TOK // 16, add, 0)
        send(("dx", group), dn_st.at[group - 1], dn_in.at[group - 1], peer)

    pass_w1(0)
    pass_neighbours("u")
    pass_w1(1)
    tokens(0)
    forward_one(0, 0)
    pass_w1(2)
    pass_w3(0)
    pass_w1(3)
    pass_w3(1)
    pass_w3(2)
    pass_neighbours("n")
    pass_w3(3)
    pass_v3(0)
    pass_w2(0)
    tokens(RIGHT)
    forward_one(0, RIGHT)
    pass_v3(1)
    tokens(LEFT)
    forward_one(0, LEFT)
    pass_opposite("u")
    pass_v3(2)
    pass_w2(1)
    grads_first(0)
    grads_first(1)
    pass_v3(3)
    pass_v2(0)
    pass_opposite("n")
    all_w(1)
    forward_one(1, 0)
    forward_one(1, RIGHT)
    tokens(OPPOSITE)
    forward_one(0, OPPOSITE)
    grads_last(0)
    y1(0, 0)
    pass_v2(1)
    forward_one(1, LEFT)
    forward_one(1, OPPOSITE)
    forward_all(3)
    y2(0, 0)
    grads(1, 1, 2)
    y1(3, 1)
    outer_send()
    grads(0, 1, 2)
    inner_send()
    far_w()
    forward_all(2)
    y3(0, 0)
    grads(0, 2)
    y2(3, 1)
    grads(1, 2)
    y1(2, None)
    grads_last(1)
    back(OPPOSITE)
    back(RIGHT)
    dn_pass(OPPOSITE, x_far)
    y2(2, None)
    back(LEFT)
    dn_pass(RIGHT, xr)
    y3(3, 1)
    outer_add()
    y1(0, 1)
    inner_add()
    y1(1, 0)
    back(0)
    y3(2, None)
    dn_pass(LEFT, xl)
    y2(0, 1)
    y2(1, 0)
    y3(0, 1)
    y3(1, 0)

    recv(("dn", 0), ("dx", 1), ("dx", 2), ("dx", 3))

    def finish(i, _):
        here = rows16(i)
        wide = x_ref[here].astype(F32)
        inv = lax.rsqrt(jnp.mean(wide * wide, axis=-1, keepdims=True) + norm_eps)
        unit = wide * inv
        dnormed = dn[0, c, here].astype(F32) + dn_sib[0, here].astype(F32)
        for k in range(3):
            dnormed += dn_in[k, here].astype(F32)
        dunit = dnormed * gain
        project = jnp.mean(dunit * unit, axis=-1, keepdims=True)
        grad_ref[here] = (tok_u[tok_rows(0, c, i * 16, 16)].astype(F32) + inv * (dunit - unit * project)).astype(BF16)
        return 0

    lax.fori_loop(0, TOK // 16, finish, 0)

    pieces = []
    for slot, parts in summed.items():
        for key, ref in (("za", za_in.at[slot - 1]), ("zb", zb_in.at[slot])):
            if (key, slot) not in copies:
                continue
            pieces.append(ref)
            if slot and parts in ([0], [1]):
                only[key, slot] = (mine == parts[0]) if key == "za" else (mine != parts[0])
                recv((key, slot), when=mine == parts[0])

                @pl.when(mine != parts[0])
                def _():
                    ref[...] = jnp.zeros((HALF, WIN), BF16)
            else:
                recv((key, slot))
    total[:, pl.ds(WIN, 128)] = jnp.zeros((16, 128), F32)

    def split(i, _):
        here = rows16(i)
        rows = ysum[0, mine, here].astype(F32)
        for piece in pieces:
            rows += piece[here].astype(F32)
        total[:, pl.ds(0, WIN)] = rows
        turned = pltpu.roll(total[...], WIN + 128 - 32 * y, 1)
        for q in range(4):
            fin_st[q, here] = turned[:, 104 * q : 104 * q + 128].astype(BF16)
        return 0

    lax.fori_loop(0, HALF // 16, split, 0)
    me = 2 * zl + c
    for key, device, to in (("sib", sib, 2 * zl + 1 - c), ("in", z_in, 2 * (1 - zl) + c), ("cross", z_cross, 2 * (1 - zl) + 1 - c)):
        send(("f", key), fin_st.at[to], fin_in.at[me], device)

    def keep(i, _):
        fin_in[me, rows16(i)] = fin_st[me, rows16(i)]
        return 0

    lax.fori_loop(0, HALF // 16, keep, 0)
    recv(("f", "sib"), ("f", "in"), ("f", "cross"))

    for q in range(2):
        rows = (HALF, 400 - HALF)[q]
        up_out[pl.ds(q * HALF, rows), :] = fin_in[q, pl.ds(0, rows)].astype(F32)[:, :104]
        down_out[pl.ds(q * HALF, rows), :] = fin_in[2 + q, pl.ds(0, rows)].astype(F32)[:, :104]
    for key, copy in copies.items():
        if key in only:
            pl.when(only[key])(copy.wait_send)
        else:
            copy.wait_send()


def body(inputs, gain, w_up, w_down, upstream):
    vmem = pl.BlockSpec(memory_space=pltpu.VMEM)
    hbm = pl.BlockSpec(memory_space=pl.ANY)
    input_grad, up_grad, down_grad = pl.pallas_call(
        kernel,
        out_shape=(
            jax.ShapeDtypeStruct((TOK, D), BF16),
            jax.ShapeDtypeStruct((400, 104), F32),
            jax.ShapeDtypeStruct((400, 104), F32),
        ),
        in_specs=[hbm, hbm, vmem, hbm, hbm],
        out_specs=(vmem,) * 3,
        scratch_shapes=[
            pltpu.VMEM((TOK, D), BF16),
            pltpu.VMEM((T, D), BF16),
            pltpu.VMEM((T, D), BF16),
            pltpu.VMEM((2, HID, D), BF16),
            pltpu.VMEM((HID, T), BF16),
            pltpu.VMEM((HID, T), BF16),
            pltpu.VMEM((2, HALF, D), F32),
            pltpu.VMEM((2, HID, D), BF16),
            pltpu.VMEM((4, 2, 2, HALF, 256), BF16),
            pltpu.VMEM((4, 2, 2, HALF, 256), BF16),
            pltpu.VMEM((4, 2, 2, HALF, WIN), BF16),
            pltpu.VMEM((4, 2, HALF, WIN), BF16),
            pltpu.VMEM((3, HALF, WIN), BF16),
            pltpu.VMEM((4, HALF, WIN), BF16),
            pltpu.VMEM((3, HALF, D), BF16),
            pltpu.VMEM((16, WIN + 128), F32),
            pltpu.VMEM((4, HALF, 128), BF16),
            pltpu.VMEM((4, HALF, 128), BF16),
            pltpu.VMEM((4, 2, TOK, D), BF16),
            pltpu.VMEM((4, TOK, D), BF16),
            pltpu.VMEM((3, TOK, D), BF16),
            pltpu.VMEM((3, TOK, D), BF16),
            pltpu.SemaphoreType.DMA((6,)),
            pltpu.SemaphoreType.DMA((N_SEM,)),
            pltpu.SemaphoreType.DMA((N_SEM,)),
        ],
        compiler_params=pltpu.CompilerParams(
            collective_id=1, has_side_effects=True, vmem_limit_bytes=60 * 2**20
        ),
        name="block_backward",
    )(inputs, upstream, gain, w_up.T, w_down)
    return input_grad, up_grad.T, down_grad


def solution(mesh):
    in_specs = (
        P(("dp", "tensor"), None),
        P(),
        P(None, "tensor"),
        P("tensor", None),
        P(("dp", "tensor"), None),
    )
    out_specs = (P(("dp", "tensor"), None), P("dp", "tensor"), P("tensor", "dp"))
    return jax.shard_map(body, mesh=mesh, in_specs=in_specs, out_specs=out_specs, check_vma=False)
```

```python
import jax
import jax.numpy as jnp
from jax import lax
from jax.experimental import pallas as pl
from jax.experimental.pallas import tpu as pltpu
from jax.sharding import PartitionSpec as P

MESH = pl.DeviceIdType.MESH
PRE = ("outer", "inner")
F32, BF16 = jnp.float32, jnp.bfloat16

norm_eps = 1e-06
D = 1664
TOK = 128
GROUP = 2 * TOK
T = 4 * GROUP
HALF = 208
HID = 4 * HALF
WIN = 512
CHUNKS = ((0, 64), (112, 48), (64, 48), (160, 48))
N_SEM = 104
RIGHT, LEFT, OPPOSITE = 1, 2, 3
GRAD_SCALE = float(32768) ** (-0.5)

FIRST = (0, HALF, 3 * HALF, 2 * HALF)


def gelu_parts(pre):
    cdf = 0.5 * (1.0 + lax.erf(pre * 0.7071067811865476))
    pdf = jnp.exp(-0.5 * pre * pre) * 0.3989422804014327
    return (pre * cdf, cdf + pre * pdf)


def place(x, y, z, c):
    x, y, z = (x + 8) % 4, (y + 8) % 4, (z + 16) % 8
    return (y * 4 + (z % 2) * 2 + c, x * 4 + z // 2)


def kernel(
    x_hbm, up_hbm, gain_ref, wu_hbm, wd_hbm, grad_ref, up_out, down_out,
    x_ref, tok_n, tok_u, w, hid, dpre, acc, g, yo_in, ya_st, nb_in, ysum, za_in, zb_in, pair_in, total, fin_st, fin_in,
    dn, dn_sib, dn_st, dn_in, local, ss, rs,
):
    dp, tensor = lax.axis_index("dp"), lax.axis_index("tensor")
    y, zl, c = dp // 4, (dp // 2) % 2, dp % 2
    x, z = tensor // 4, (tensor % 4) * 2 + zl
    step_out = 2 * zl - 1
    sib = place(x, y, z, 1 - c)
    xr, xl = place(x + 1, y, z, c), place(x - 1, y, z, c)
    x_far = place(x + 2, y, z, c)
    yr, yl = place(x, y + 1, z, c), place(x, y - 1, z, c)
    z_out, z_in = place(x, y, z + step_out, c), place(x, y, z - step_out, c)
    z_cross = place(x, y, z - step_out, 1 - c)
    z_same = {1: place(x, y, z + 2 * step_out, c), 2: place(x, y, z + 4, c), 3: place(x, y, z - 2 * step_out, c)}
    z_other = {0: z_in, 1: z_out, 2: place(x, y, z + 3 * step_out, c), 3: place(x, y, z - 3 * step_out, c)}
    kind = y % 2
    from_out, from_in = 16 + 96 * zl, 112 - 96 * zl
    mine = zl

    own = pl.ds(pl.multiple_of(c * TOK, 16), TOK)
    load_up = pltpu.make_async_copy(up_hbm, tok_u.at[own], local.at[0])
    load_up.start()
    barrier = pltpu.get_barrier_semaphore()
    peers = [sib, xr, xl, x_far, yr, yl, z_cross, *z_same.values(), *z_other.values()]
    for peer in peers:
        pl.semaphore_signal(barrier, inc=1, device_id=peer, device_id_type=MESH)

    copies, only, summed = {}, {}, {}

    def make(key, src, dst, device):
        i = len(copies)
        copies[key] = pltpu.make_async_remote_copy(
            src_ref=src, dst_ref=dst, send_sem=ss.at[i], recv_sem=rs.at[i], device_id=device, device_id_type=MESH
        )

    def start(key, when=None):
        if when is None:
            copies[key].start()
        else:
            only[key] = when
            pl.when(when)(copies[key].start)

    def send(key, src, dst, device, when=None):
        make(key, src, dst, device)
        start(key, when)

    def recv(*keys, when=None):
        for key in keys:
            if when is None:
                copies[key].wait_recv()
            else:
                pl.when(when)(copies[key].wait_recv)

    def tok_rows(group, core, first=0, rows=TOK):
        return pl.ds(pl.multiple_of(group * GROUP + core * TOK + first, 16), rows)

    load_w = [
        pltpu.make_async_copy(ref.at[pl.ds(pl.multiple_of(c * HALF, 16), 192)], w.at[k, pl.ds(0, 192)], local.at[1 + k])
        for k, ref in enumerate((wu_hbm, wd_hbm))
    ]
    load_rest = [
        pltpu.make_async_copy(ref.at[pl.ds(192, 16)], w.at[k, pl.ds(192, 16)], local.at[3 + k])
        for k, ref in enumerate((wu_hbm, wd_hbm))
    ]
    load_x = pltpu.make_async_copy(x_hbm, x_ref, local.at[5])
    for copy in load_w:
        copy.start()

    @pl.when(c == 0)
    def _():
        for copy in load_rest:
            copy.start()

    @pl.when(c == 1)
    def _():
        w[:, pl.ds(192, 16)] = jnp.zeros((2, 16, D), BF16)

    load_x.start()
    toks = {"u": tok_u, "n": tok_n}

    def send_own(a):
        send((a, "r"), toks[a].at[own], toks[a].at[tok_rows(LEFT, c)], xr)
        send((a, "l"), toks[a].at[own], toks[a].at[tok_rows(RIGHT, c)], xl)
        send((a, "s", 0), toks[a].at[own], toks[a].at[own], sib)

    load_up.wait()
    pl.semaphore_wait(barrier, len(peers))
    send_own("u")
    for copy in load_w:
        copy.wait()

    @pl.when(c == 0)
    def _():
        for copy in load_rest:
            copy.wait()

    def rows_of(slot, first, rows):
        return pl.ds(pl.multiple_of(FIRST[slot] + first, 16), rows)

    def chunk(slot, i):
        return rows_of(slot, *CHUNKS[i])

    for i in range(4):
        send(("w0", i), w.at[kind, chunk(0, i)], w.at[kind, chunk(1, i)], z_out)

    gain = gain_ref[...].astype(F32).reshape(1, D)
    load_x.wait()
    def norm(i, _):
        r = pl.ds(pl.multiple_of(i * 16, 16), 16)
        wide = x_ref[r].astype(F32)
        inv = lax.rsqrt(jnp.mean(wide * wide, axis=-1, keepdims=True) + norm_eps)
        tok_n[tok_rows(0, c, i * 16, 16)] = (wide * inv * gain).astype(BF16)
        return 0

    lax.fori_loop(0, TOK // 16, norm, 0)
    send_own("n")

    def pass_neighbours(a):
        t = toks[a]
        recv((a, "r"))
        send((a, "fr"), t.at[tok_rows(LEFT, c, 0, 64)], t.at[tok_rows(OPPOSITE, c, 0, 64)], xr)
        send((a, "s", LEFT), t.at[tok_rows(LEFT, c)], t.at[tok_rows(LEFT, c)], sib)
        recv((a, "l"))
        send((a, "fl"), t.at[tok_rows(RIGHT, c, 64, 64)], t.at[tok_rows(OPPOSITE, c, 64, 64)], xl)
        send((a, "s", RIGHT), t.at[tok_rows(RIGHT, c)], t.at[tok_rows(RIGHT, c)], sib)

    def pass_opposite(a):
        recv((a, "fr"), (a, "fl"))
        send((a, "s", OPPOSITE), toks[a].at[tok_rows(OPPOSITE, c)], toks[a].at[tok_rows(OPPOSITE, c)], sib)

    def tokens(group):
        recv(("u", "s", group), ("n", "s", group))

    def share(key, rows, peer):
        send(("wy", key), w.at[kind, rows], w.at[kind, rows], peer)

    def pass_w1(i):
        recv(("w0", i))
        send(("w1", i), w.at[kind, chunk(1, i)], w.at[kind, chunk(3, i)], z_in)
        share((1, i), chunk(1, i), (yr, yl, yr, yl)[i])

    def far_out(key, k, i):
        if i == 0:
            send((key, "x"), w.at[k, rows_of(3, 0, 16)], w.at[k, rows_of(2, 0, 16)], z_out, zl == 1)
            for n in range(2):
                here, there = rows_of(3, from_in + 48 * n, 48), rows_of(2, from_in + 48 * n, 48)
                make((key, n), w.at[k, here], w.at[k, there], z_out)
        pl.when(zl == 1 - i % 2)(copies[key, i // 2].start)

    def far_in(key, came, k, n):
        recv((came, n))
        rows = rows_of(2, from_out + 48 * n, 48)
        send((key, n), w.at[k, rows], w.at[k, rows], z_in)
        if n == 1:
            recv((came, "x"), when=zl == 0)
            rows = rows_of(2, 0, 16)
            send((key, "x"), w.at[k, rows], w.at[k, rows], z_in, zl == 0)

    def pass_w3(i):
        recv(("w1", i))
        far_out("w3", kind, i)
        share((3, i), chunk(3, i), (yl, yr, yl, yr)[i])

    def pass_w2(n):
        far_in("w2", "w3", kind, n)

    def pass_v3(i):
        recv(("wy", (3, i)))
        far_out("v3", 1 - kind, i)

    def pass_v2(n):
        far_in("v2", "v3", 1 - kind, n)

    def far_w():
        for key in ("w2", "v2"):
            recv((key, 0), (key, 1))
            recv((key, "x"), when=zl == 1)

    def all_w(slot):
        recv(*[key for key in copies if key[0] == "wy" and key[1][0] == slot])

    def forward(r, t):
        nt = (((1,), (1,)), ((), ()))
        pre = lax.dot_general(w[0, r], tok_n[t], nt, preferred_element_type=F32)
        dhidden = lax.dot_general(w[1, r], tok_u[t], nt, preferred_element_type=F32)
        hidden, slope = gelu_parts(pre)
        hid[r, t] = hidden.astype(BF16)
        dpre[r, t] = (dhidden * slope).astype(BF16)

    def forward_one(slot, group):
        forward(pl.ds(FIRST[slot], HALF), pl.ds(group * GROUP, GROUP))

    def forward_all(slot, slots=1):
        def one(i, _):
            forward(pl.ds(FIRST[slot], slots * HALF), pl.ds(pl.multiple_of(i * 512, 512), 512))
            return 0

        lax.fori_loop(0, 2, one, 0)

    def all_columns(columns):
        def tile(n, _):
            columns(pl.ds(pl.multiple_of(n * 512, 512), 512))
            return 0

        lax.fori_loop(0, 3, tile, 0)
        columns(pl.ds(1536, 128))

    def grads(kind, slot, slots=1):
        r = pl.ds(FIRST[slot], slots * HALF)
        left, right = ((dpre, tok_n), (hid, tok_u))[kind]

        def columns(cols):
            term = jnp.dot(left[r], right[:, cols], preferred_element_type=F32)
            g[kind, r, cols] = (term * GRAD_SCALE).astype(BF16)

        all_columns(columns)

    def grads_first(kind):
        r, t = pl.ds(0, HALF), pl.ds(0, 3 * GROUP)
        left, right = ((dpre, tok_n), (hid, tok_u))[kind]

        def columns(cols):
            acc[:, cols] = jnp.dot(left[r, t], right[t, cols], preferred_element_type=F32)

        all_columns(columns)

    def grads_last(kind):
        r, t = pl.ds(0, HALF), pl.ds(3 * GROUP, GROUP)
        left, right = ((dpre, tok_n), (hid, tok_u))[kind]

        def columns(cols):
            term = acc[:, cols] + jnp.dot(left[r, t], right[t, cols], preferred_element_type=F32)
            g[kind, r, cols] = (term * GRAD_SCALE).astype(BF16)

        all_columns(columns)

    def window(owner, first=0, cols=WIN):
        return pl.ds(pl.multiple_of(((owner + 8) % 4) * 384 + first, 128), cols)

    def rows16(i):
        return pl.ds(pl.multiple_of(i * 16, 16), 16)

    def slot16(slot, i):
        return pl.ds(pl.multiple_of(FIRST[slot] + i * 16, 16), 16)

    def kinds(part):
        return pl.ds(0, 2) if part[1] is None else pl.ds(mine if part[1] == "mine" else part[1], 1)

    def y1(*part):
        r, k = pl.ds(FIRST[part[0]], HALF), kinds(part)
        send(("yo", part, 0), g.at[k, r, window(y + 2, 0, 256)], yo_in.at[part[0], 0, k], yr)
        send(("yo", part, 1), g.at[k, r, window(y + 2, 256, 256)], yo_in.at[part[0], 1, k], yl)

    def yd(*part):
        r, k = pl.ds(FIRST[part[0]], HALF), kinds(part)
        left, right = pl.ds(0, 256), pl.ds(256, 256)
        send(("yd", part, 0), g.at[k, r, window(y + 1, 256, 256)], nb_in.at[part[0], 0, k, :, right], yr)
        send(("yd", part, 1), g.at[k, r, window(y - 1, 0, 256)], nb_in.at[part[0], 1, k, :, left], yl)

    def y2(*part):
        slot, k = part[0], kinds(part)
        for way, owner, first, peer in ((0, y + 1, 0, yr), (1, y - 1, 256, yl)):
            recv(("yo", part, way))
            cols = window(owner, first, 256)

            def add(i, _):
                here = rows16(i)
                ya_st[slot, way, k, here] = (
                    g[k, slot16(slot, i), cols].astype(F32) + yo_in[slot, way, k, here].astype(F32)
                ).astype(BF16)
                return 0

            lax.fori_loop(0, HALF // 16, add, 0)
            send(("ya", part, way), ya_st.at[slot, way, k], nb_in.at[slot, way, k, :, pl.ds(first, 256)], peer)

    def y3(*part):
        slot, k = part[0], kinds(part)
        recv(("yd", part, 0), ("yd", part, 1), ("ya", part, 0), ("ya", part, 1))
        cols = window(y)

        def add(i, _):
            here = rows16(i)
            ysum[slot, k, here] = (
                g[k, slot16(slot, i), cols].astype(F32)
                + nb_in[slot, 0, k, here].astype(F32)
                + nb_in[slot, 1, k, here].astype(F32)
            ).astype(BF16)
            return 0

        lax.fori_loop(0, HALF // 16, add, 0)
        summed.setdefault(slot, []).append(part[1])
        if part[1] == "mine":
            send(("za", slot), ysum.at[slot, mine], za_in.at[slot - 1], z_same[slot])
            return
        if ("zb", slot) not in copies:
            make(("zb", slot), ysum.at[slot, 1 - mine], zb_in.at[slot], z_other[slot])
            if slot:
                make(("za", slot), ysum.at[slot, mine], za_in.at[slot - 1], z_same[slot])
        for key, when in (("zb", mine != part[1]), ("za", mine == part[1])):
            if (key, slot) in copies:
                if part[1] is None:
                    copies[key, slot].start()
                else:
                    pl.when(when)(copies[key, slot].start)

    def presum_send(key, kind, slot, device):
        send(key, g.at[kind, pl.ds(FIRST[slot], HALF)], pair_in.at[PRE.index(key)], device)

    def presum_add(key, kind, slot):
        recv(key)

        def add(i, _):
            here = slot16(slot, i)
            g[kind, here] = (
                g[kind, here].astype(F32) + pair_in[PRE.index(key), rows16(i)].astype(F32)
            ).astype(BF16)
            return 0

        lax.fori_loop(0, HALF // 16, add, 0)

    def outer_send():
        presum_send("outer", 1, 1, z_out)

    def outer_add():
        presum_add("outer", 1, 0)

    def inner_send():
        presum_send("inner", 0, 3, z_in)

    def inner_add():
        presum_add("inner", 0, 1)

    def back(group):
        t = pl.ds(group * GROUP, GROUP)
        rows = dpre[:, t].T

        def columns(cols):
            part = jnp.dot(rows, w[0, :, cols], preferred_element_type=F32).astype(BF16)
            dn[group, 0, :, cols] = part[:TOK]
            dn[group, 1, :, cols] = part[TOK:]

        all_columns(columns)
        send(("dn", group), dn.at[group, 1 - c], dn_sib.at[group], sib)

    def dn_pass(group, peer):
        recv(("dn", group))

        def add(i, _):
            here = rows16(i)
            dn_st[group - 1, here] = (dn[group, c, here].astype(F32) + dn_sib[group, here].astype(F32)).astype(BF16)
            return 0

        lax.fori_loop(0, TOK // 16, add, 0)
        send(("dx", group), dn_st.at[group - 1], dn_in.at[group - 1], peer)

    def input_gradient():
        recv(("dn", 0), ("dx", 1), ("dx", 2), ("dx", 3))

        def finish(i, _):
            here = rows16(i)
            wide = x_ref[here].astype(F32)
            inv = lax.rsqrt(jnp.mean(wide * wide, axis=-1, keepdims=True) + norm_eps)
            unit = wide * inv
            dnormed = dn[0, c, here].astype(F32) + dn_sib[0, here].astype(F32)
            for k in range(3):
                dnormed += dn_in[k, here].astype(F32)
            dunit = dnormed * gain
            project = jnp.mean(dunit * unit, axis=-1, keepdims=True)
            grad_ref[here] = (tok_u[tok_rows(0, c, i * 16, 16)].astype(F32) + inv * (dunit - unit * project)).astype(BF16)
            return 0

        lax.fori_loop(0, TOK // 16, finish, 0)

    pass_w1(0)
    pass_neighbours("u")
    pass_w1(1)
    tokens(0)
    forward_one(0, 0)
    pass_w1(2)
    pass_w3(0)
    pass_w1(3)
    pass_w3(1)
    pass_w3(2)
    pass_neighbours("n")
    pass_w3(3)
    pass_v3(0)
    pass_w2(0)
    tokens(RIGHT)
    forward_one(0, RIGHT)
    pass_v3(1)
    tokens(LEFT)
    forward_one(0, LEFT)
    pass_opposite("u")
    pass_v3(2)
    pass_w2(1)
    grads_first(0)
    pass_opposite("n")
    pass_v3(3)
    tokens(OPPOSITE)
    forward_one(0, OPPOSITE)
    grads_last(0)
    y1(0, 0)
    yd(0, 0)
    pass_v2(0)
    all_w(1)
    forward_all(1, 2)
    pass_v2(1)
    y2(0, 0)
    grads(1, 1, 2)
    y1(3, 1)
    yd(3, 1)
    outer_send()
    grads(0, 1, 2)
    inner_send()
    far_w()
    forward_all(2)
    y2(3, 1)
    grads(0, 2)
    y1(2, 0)
    grads(1, 2)
    y1(2, 1)
    yd(2, 0)
    y3(0, 0)
    grads(1, 0)
    back(OPPOSITE)
    y2(2, 0)
    yd(2, 1)
    back(RIGHT)
    dn_pass(OPPOSITE, x_far)
    y2(2, 1)
    outer_add()
    y1(0, 1)
    dn_pass(RIGHT, xr)
    y3(3, 1)
    back(LEFT)
    y3(2, 0)
    inner_add()
    y1(1, 0)
    yd(0, 1)
    dn_pass(LEFT, xl)
    back(0)
    y3(2, 1)
    y2(0, 1)
    yd(1, 0)
    y2(1, 0)
    y3(0, 1)
    y3(1, 0)
    input_gradient()

    pieces = []
    for slot, parts in summed.items():
        for key, ref in (("za", za_in.at[slot - 1]), ("zb", zb_in.at[slot])):
            if (key, slot) not in copies:
                continue
            pieces.append(ref)
            if slot and parts in ([0], [1]):
                only[key, slot] = (mine == parts[0]) if key == "za" else (mine != parts[0])
                recv((key, slot), when=mine == parts[0])

                @pl.when(mine != parts[0])
                def _():
                    ref[...] = jnp.zeros((HALF, WIN), BF16)
            else:
                recv((key, slot))
    total[:, pl.ds(WIN, 128)] = jnp.zeros((16, 128), F32)

    def split(i, _):
        here = rows16(i)
        rows = ysum[0, mine, here].astype(F32)
        for piece in pieces:
            rows += piece[here].astype(F32)
        total[:, pl.ds(0, WIN)] = rows
        turned = pltpu.roll(total[...], WIN + 128 - 32 * y, 1)
        for q in range(4):
            fin_st[q, here] = turned[:, 104 * q : 104 * q + 128].astype(BF16)
        return 0

    lax.fori_loop(0, HALF // 16, split, 0)
    me = 2 * zl + c
    for key, device, to in (("sib", sib, 2 * zl + 1 - c), ("in", z_in, 2 * (1 - zl) + c), ("cross", z_cross, 2 * (1 - zl) + 1 - c)):
        send(("f", key), fin_st.at[to], fin_in.at[me], device)

    def keep(i, _):
        fin_in[me, rows16(i)] = fin_st[me, rows16(i)]
        return 0

    lax.fori_loop(0, HALF // 16, keep, 0)
    recv(("f", "sib"), ("f", "in"), ("f", "cross"))

    for q in range(2):
        rows = (HALF, 400 - HALF)[q]
        up_out[pl.ds(q * HALF, rows), :] = fin_in[q, pl.ds(0, rows)].astype(F32)[:, :104]
        down_out[pl.ds(q * HALF, rows), :] = fin_in[2 + q, pl.ds(0, rows)].astype(F32)[:, :104]
    for key, copy in copies.items():
        if key in only:
            pl.when(only[key])(copy.wait_send)
        else:
            copy.wait_send()


def body(inputs, gain, w_up, w_down, upstream):
    vmem = pl.BlockSpec(memory_space=pltpu.VMEM)
    hbm = pl.BlockSpec(memory_space=pl.ANY)
    input_grad, up_grad, down_grad = pl.pallas_call(
        kernel,
        out_shape=(
            jax.ShapeDtypeStruct((TOK, D), BF16),
            jax.ShapeDtypeStruct((400, 104), F32),
            jax.ShapeDtypeStruct((400, 104), F32),
        ),
        in_specs=[hbm, hbm, vmem, hbm, hbm],
        out_specs=(vmem,) * 3,
        scratch_shapes=[
            pltpu.VMEM((TOK, D), BF16),
            pltpu.VMEM((T, D), BF16),
            pltpu.VMEM((T, D), BF16),
            pltpu.VMEM((2, HID, D), BF16),
            pltpu.VMEM((HID, T), BF16),
            pltpu.VMEM((HID, T), BF16),
            pltpu.VMEM((HALF, D), F32),
            pltpu.VMEM((2, HID, D), BF16),
            pltpu.VMEM((4, 2, 2, HALF, 256), BF16),
            pltpu.VMEM((4, 2, 2, HALF, 256), BF16),
            pltpu.VMEM((4, 2, 2, HALF, WIN), BF16),
            pltpu.VMEM((4, 2, HALF, WIN), BF16),
            pltpu.VMEM((3, HALF, WIN), BF16),
            pltpu.VMEM((4, HALF, WIN), BF16),
            pltpu.VMEM((2, HALF, D), BF16),
            pltpu.VMEM((16, WIN + 128), F32),
            pltpu.VMEM((4, HALF, 128), BF16),
            pltpu.VMEM((4, HALF, 128), BF16),
            pltpu.VMEM((4, 2, TOK, D), BF16),
            pltpu.VMEM((4, TOK, D), BF16),
            pltpu.VMEM((3, TOK, D), BF16),
            pltpu.VMEM((3, TOK, D), BF16),
            pltpu.SemaphoreType.DMA((6,)),
            pltpu.SemaphoreType.DMA((N_SEM,)),
            pltpu.SemaphoreType.DMA((N_SEM,)),
        ],
        compiler_params=pltpu.CompilerParams(
            collective_id=1, has_side_effects=True, vmem_limit_bytes=53 * 2**20
        ),
        name="block_backward",
    )(inputs, upstream, gain, w_up.T, w_down)
    return input_grad, up_grad.T, down_grad


def solution(mesh):
    in_specs = (
        P(("dp", "tensor"), None),
        P(),
        P(None, "tensor"),
        P("tensor", None),
        P(("dp", "tensor"), None),
    )
    out_specs = (P(("dp", "tensor"), None), P("dp", "tensor"), P("tensor", "dp"))
    return jax.shard_map(body, mesh=mesh, in_specs=in_specs, out_specs=out_specs, check_vma=False)
```

```python
import jax
import jax.numpy as jnp
from jax import lax
from jax.experimental import pallas as pl
from jax.experimental.pallas import tpu as pltpu
from jax.sharding import PartitionSpec as P

MESH = pl.DeviceIdType.MESH
PRE = ("outer", "inner")
F32, BF16 = jnp.float32, jnp.bfloat16

norm_eps = 1e-06
D = 1664
TOK = 128
GROUP = 2 * TOK
T = 4 * GROUP
HALF = 208
HID = 4 * HALF
WIN = 512
CHUNKS = ((0, 64), (112, 48), (64, 48), (160, 48))
N_SEM = 112
RIGHT, LEFT, OPPOSITE = 1, 2, 3
GRAD_SCALE = float(32768) ** (-0.5)

FIRST = (0, HALF, 3 * HALF, 2 * HALF)


def gelu_parts(pre):
    cdf = 0.5 * (1.0 + lax.erf(pre * 0.7071067811865476))
    pdf = jnp.exp(-0.5 * pre * pre) * 0.3989422804014327
    return (pre * cdf, cdf + pre * pdf)


def place(x, y, z, c):
    x, y, z = (x + 8) % 4, (y + 8) % 4, (z + 16) % 8
    return (y * 4 + (z % 2) * 2 + c, x * 4 + z // 2)


def kernel(
    x_hbm, up_hbm, gain_ref, wu_hbm, wd_hbm, grad_ref, up_out, down_out,
    x_ref, tok_n, tok_u, w, hid, dpre, acc, g, yo_in, ya_st, nb_in, ysum, za_in, zb_in, pair_in, total, fin_st, fin_in,
    dn, dn_sib, dn_st, dn_in, local, ss, rs,
):
    dp, tensor = lax.axis_index("dp"), lax.axis_index("tensor")
    y, zl, c = dp // 4, (dp // 2) % 2, dp % 2
    x, z = tensor // 4, (tensor % 4) * 2 + zl
    step_out = 2 * zl - 1
    sib = place(x, y, z, 1 - c)
    xr, xl = place(x + 1, y, z, c), place(x - 1, y, z, c)
    x_far = place(x + 2, y, z, c)
    yr, yl = place(x, y + 1, z, c), place(x, y - 1, z, c)
    z_out, z_in = place(x, y, z + step_out, c), place(x, y, z - step_out, c)
    z_cross = place(x, y, z - step_out, 1 - c)
    z_same = {1: place(x, y, z + 2 * step_out, c), 2: place(x, y, z + 4, c), 3: place(x, y, z - 2 * step_out, c)}
    z_other = {0: z_in, 1: z_out, 2: place(x, y, z + 3 * step_out, c), 3: place(x, y, z - 3 * step_out, c)}
    kind = y % 2
    from_out, from_in = 16 + 96 * zl, 112 - 96 * zl
    mine = zl

    own = pl.ds(pl.multiple_of(c * TOK, 16), TOK)
    load_up = pltpu.make_async_copy(up_hbm, tok_u.at[own], local.at[0])
    load_up.start()
    barrier = pltpu.get_barrier_semaphore()
    peers = [sib, xr, xl, x_far, yr, yl, z_cross, *z_same.values(), *z_other.values()]
    for peer in peers:
        pl.semaphore_signal(barrier, inc=1, device_id=peer, device_id_type=MESH)

    copies, only, summed = {}, {}, {}

    def make(key, src, dst, device):
        i = len(copies)
        copies[key] = pltpu.make_async_remote_copy(
            src_ref=src, dst_ref=dst, send_sem=ss.at[i], recv_sem=rs.at[i], device_id=device, device_id_type=MESH
        )

    def start(key, when=None):
        if when is None:
            copies[key].start()
        else:
            only[key] = when
            pl.when(when)(copies[key].start)

    def send(key, src, dst, device, when=None):
        make(key, src, dst, device)
        start(key, when)

    def recv(*keys, when=None):
        for key in keys:
            if when is None:
                copies[key].wait_recv()
            else:
                pl.when(when)(copies[key].wait_recv)

    def tok_rows(group, core, first=0, rows=TOK):
        return pl.ds(pl.multiple_of(group * GROUP + core * TOK + first, 16), rows)

    load_w = [
        pltpu.make_async_copy(ref.at[pl.ds(pl.multiple_of(c * HALF, 16), 192)], w.at[k, pl.ds(0, 192)], local.at[1 + k])
        for k, ref in enumerate((wu_hbm, wd_hbm))
    ]
    load_rest = [
        pltpu.make_async_copy(ref.at[pl.ds(192, 16)], w.at[k, pl.ds(192, 16)], local.at[3 + k])
        for k, ref in enumerate((wu_hbm, wd_hbm))
    ]
    load_x = pltpu.make_async_copy(x_hbm, x_ref, local.at[5])
    for copy in load_w:
        copy.start()

    @pl.when(c == 0)
    def _():
        for copy in load_rest:
            copy.start()

    @pl.when(c == 1)
    def _():
        w[:, pl.ds(192, 16)] = jnp.zeros((2, 16, D), BF16)

    load_x.start()
    toks = {"u": tok_u, "n": tok_n}

    def send_own(a):
        send((a, "r"), toks[a].at[own], toks[a].at[tok_rows(LEFT, c)], xr)
        send((a, "l"), toks[a].at[own], toks[a].at[tok_rows(RIGHT, c)], xl)
        send((a, "s", 0), toks[a].at[own], toks[a].at[own], sib)

    load_up.wait()
    pl.semaphore_wait(barrier, len(peers))
    send_own("u")
    for copy in load_w:
        copy.wait()

    @pl.when(c == 0)
    def _():
        for copy in load_rest:
            copy.wait()

    def rows_of(slot, first, rows):
        return pl.ds(pl.multiple_of(FIRST[slot] + first, 16), rows)

    def chunk(slot, i):
        return rows_of(slot, *CHUNKS[i])

    for i in range(4):
        send(("w0", i), w.at[kind, chunk(0, i)], w.at[kind, chunk(1, i)], z_out)

    gain = gain_ref[...].astype(F32).reshape(1, D)
    load_x.wait()
    def norm(i, _):
        r = pl.ds(pl.multiple_of(i * 16, 16), 16)
        wide = x_ref[r].astype(F32)
        inv = lax.rsqrt(jnp.mean(wide * wide, axis=-1, keepdims=True) + norm_eps)
        tok_n[tok_rows(0, c, i * 16, 16)] = (wide * inv * gain).astype(BF16)
        return 0

    lax.fori_loop(0, TOK // 16, norm, 0)
    send_own("n")

    def pass_neighbours(a):
        t = toks[a]
        recv((a, "r"))
        send((a, "fr"), t.at[tok_rows(LEFT, c, 0, 64)], t.at[tok_rows(OPPOSITE, c, 0, 64)], xr)
        send((a, "s", LEFT), t.at[tok_rows(LEFT, c)], t.at[tok_rows(LEFT, c)], sib)
        recv((a, "l"))
        send((a, "fl"), t.at[tok_rows(RIGHT, c, 64, 64)], t.at[tok_rows(OPPOSITE, c, 64, 64)], xl)
        send((a, "s", RIGHT), t.at[tok_rows(RIGHT, c)], t.at[tok_rows(RIGHT, c)], sib)

    def pass_opposite(a):
        recv((a, "fr"), (a, "fl"))
        send((a, "s", OPPOSITE), toks[a].at[tok_rows(OPPOSITE, c)], toks[a].at[tok_rows(OPPOSITE, c)], sib)

    def tokens(group):
        recv(("u", "s", group), ("n", "s", group))

    def share(key, rows, peer):
        send(("wy", key), w.at[kind, rows], w.at[kind, rows], peer)

    def pass_w1(i):
        recv(("w0", i))
        send(("w1", i), w.at[kind, chunk(1, i)], w.at[kind, chunk(3, i)], z_in)
        share((1, i), chunk(1, i), (yr, yl, yr, yl)[i])

    def far_out(key, k, i):
        if i == 0:
            send((key, "x"), w.at[k, rows_of(3, 0, 16)], w.at[k, rows_of(2, 0, 16)], z_out, zl == 1)
            for n in range(2):
                here, there = rows_of(3, from_in + 48 * n, 48), rows_of(2, from_in + 48 * n, 48)
                make((key, n), w.at[k, here], w.at[k, there], z_out)
        pl.when(zl == 1 - i % 2)(copies[key, i // 2].start)

    def far_in(key, came, k, n):
        recv((came, n))
        rows = rows_of(2, from_out + 48 * n, 48)
        send((key, n), w.at[k, rows], w.at[k, rows], z_in)
        if n == 1:
            recv((came, "x"), when=zl == 0)
            rows = rows_of(2, 0, 16)
            send((key, "x"), w.at[k, rows], w.at[k, rows], z_in, zl == 0)

    def pass_w3(i):
        recv(("w1", i))
        far_out("w3", kind, i)
        share((3, i), chunk(3, i), (yl, yr, yl, yr)[i])

    def pass_w2(n):
        far_in("w2", "w3", kind, n)

    def pass_v3(i):
        recv(("wy", (3, i)))
        far_out("v3", 1 - kind, i)

    def pass_v2(n):
        far_in("v2", "v3", 1 - kind, n)

    def far_w():
        for key in ("w2", "v2"):
            recv((key, 0), (key, 1))
            recv((key, "x"), when=zl == 1)

    def all_w(slot):
        recv(*[key for key in copies if key[0] == "wy" and key[1][0] == slot])

    def forward(r, t):
        nt = (((1,), (1,)), ((), ()))
        pre = lax.dot_general(w[0, r], tok_n[t], nt, preferred_element_type=F32)
        dhidden = lax.dot_general(w[1, r], tok_u[t], nt, preferred_element_type=F32)
        hidden, slope = gelu_parts(pre)
        hid[r, t] = hidden.astype(BF16)
        dpre[r, t] = (dhidden * slope).astype(BF16)

    def forward_one(slot, group):
        forward(pl.ds(FIRST[slot], HALF), pl.ds(group * GROUP, GROUP))

    def forward_all(slot, slots=1):
        def one(i, _):
            forward(pl.ds(FIRST[slot], slots * HALF), pl.ds(pl.multiple_of(i * 512, 512), 512))
            return 0

        lax.fori_loop(0, 2, one, 0)

    def all_columns(columns):
        def tile(n, _):
            columns(pl.ds(pl.multiple_of(n * 512, 512), 512))
            return 0

        lax.fori_loop(0, 3, tile, 0)
        columns(pl.ds(1536, 128))

    def grads(kind, slot, slots=1):
        r = pl.ds(FIRST[slot], slots * HALF)
        left, right = ((dpre, tok_n), (hid, tok_u))[kind]

        def columns(cols):
            term = jnp.dot(left[r], right[:, cols], preferred_element_type=F32)
            g[kind, r, cols] = (term * GRAD_SCALE).astype(BF16)

        all_columns(columns)

    def grads_first(kind):
        r, t = pl.ds(0, HALF), pl.ds(0, 3 * GROUP)
        left, right = ((dpre, tok_n), (hid, tok_u))[kind]

        def columns(cols):
            acc[:, cols] = jnp.dot(left[r, t], right[t, cols], preferred_element_type=F32)

        all_columns(columns)

    def grads_last(kind):
        r, t = pl.ds(0, HALF), pl.ds(3 * GROUP, GROUP)
        left, right = ((dpre, tok_n), (hid, tok_u))[kind]

        def columns(cols):
            term = acc[:, cols] + jnp.dot(left[r, t], right[t, cols], preferred_element_type=F32)
            g[kind, r, cols] = (term * GRAD_SCALE).astype(BF16)

        all_columns(columns)

    def window(owner, first=0, cols=WIN):
        return pl.ds(pl.multiple_of(((owner + 8) % 4) * 384 + first, 128), cols)

    def rows16(i):
        return pl.ds(pl.multiple_of(i * 16, 16), 16)

    def slot16(slot, i):
        return pl.ds(pl.multiple_of(FIRST[slot] + i * 16, 16), 16)

    def kinds(part):
        return pl.ds(0, 2) if part[1] is None else pl.ds(mine if part[1] == "mine" else part[1], 1)

    def y1(*part):
        r, k = pl.ds(FIRST[part[0]], HALF), kinds(part)
        send(("yo", part, 0), g.at[k, r, window(y + 2, 0, 256)], yo_in.at[part[0], 0, k], yr)
        send(("yo", part, 1), g.at[k, r, window(y + 2, 256, 256)], yo_in.at[part[0], 1, k], yl)

    def yd(*part):
        r, k = pl.ds(FIRST[part[0]], HALF), kinds(part)
        left, right = pl.ds(0, 256), pl.ds(256, 256)
        send(("yd", part, 0), g.at[k, r, window(y + 1, 256, 256)], nb_in.at[part[0], 0, k, :, right], yr)
        send(("yd", part, 1), g.at[k, r, window(y - 1, 0, 256)], nb_in.at[part[0], 1, k, :, left], yl)

    def y2(*part):
        slot, k = part[0], kinds(part)
        for way, owner, first, peer in ((0, y + 1, 0, yr), (1, y - 1, 256, yl)):
            recv(("yo", part, way))
            cols = window(owner, first, 256)

            def add(i, _):
                here = rows16(i)
                ya_st[slot, way, k, here] = (
                    g[k, slot16(slot, i), cols].astype(F32) + yo_in[slot, way, k, here].astype(F32)
                ).astype(BF16)
                return 0

            lax.fori_loop(0, HALF // 16, add, 0)
            send(("ya", part, way), ya_st.at[slot, way, k], nb_in.at[slot, way, k, :, pl.ds(first, 256)], peer)

    def y3(*part):
        slot, k = part[0], kinds(part)
        recv(("yd", part, 0), ("yd", part, 1), ("ya", part, 0), ("ya", part, 1))
        cols = window(y)

        def add(i, _):
            here = rows16(i)
            ysum[slot, k, here] = (
                g[k, slot16(slot, i), cols].astype(F32)
                + nb_in[slot, 0, k, here].astype(F32)
                + nb_in[slot, 1, k, here].astype(F32)
            ).astype(BF16)
            return 0

        lax.fori_loop(0, HALF // 16, add, 0)
        summed.setdefault(slot, []).append(part[1])
        if part[1] == "mine":
            send(("za", slot), ysum.at[slot, mine], za_in.at[slot - 1], z_same[slot])
            return
        if ("zb", slot) not in copies:
            make(("zb", slot), ysum.at[slot, 1 - mine], zb_in.at[slot], z_other[slot])
            if slot:
                make(("za", slot), ysum.at[slot, mine], za_in.at[slot - 1], z_same[slot])
        for key, when in (("zb", mine != part[1]), ("za", mine == part[1])):
            if (key, slot) in copies:
                if part[1] is None:
                    copies[key, slot].start()
                else:
                    pl.when(when)(copies[key, slot].start)

    def presum_send(key, kind, slot, device):
        send(key, g.at[kind, pl.ds(FIRST[slot], HALF)], pair_in.at[PRE.index(key)], device)

    def presum_add(key, kind, slot):
        recv(key)

        def add(i, _):
            here = slot16(slot, i)
            g[kind, here] = (
                g[kind, here].astype(F32) + pair_in[PRE.index(key), rows16(i)].astype(F32)
            ).astype(BF16)
            return 0

        lax.fori_loop(0, HALF // 16, add, 0)

    def outer_send():
        presum_send("outer", 1, 1, z_out)

    def outer_add():
        presum_add("outer", 1, 0)

    def inner_send():
        presum_send("inner", 0, 3, z_in)

    def inner_add():
        presum_add("inner", 0, 1)

    def back(group):
        t = pl.ds(group * GROUP, GROUP)
        rows = dpre[:, t].T

        def columns(cols):
            part = jnp.dot(rows, w[0, :, cols], preferred_element_type=F32).astype(BF16)
            dn[group, 0, :, cols] = part[:TOK]
            dn[group, 1, :, cols] = part[TOK:]

        all_columns(columns)
        send(("dn", group), dn.at[group, 1 - c], dn_sib.at[group], sib)

    def dn_pass(group, peer):
        recv(("dn", group))

        def add(i, _):
            here = rows16(i)
            dn_st[group - 1, here] = (dn[group, c, here].astype(F32) + dn_sib[group, here].astype(F32)).astype(BF16)
            return 0

        lax.fori_loop(0, TOK // 16, add, 0)
        send(("dx", group), dn_st.at[group - 1], dn_in.at[group - 1], peer)

    def input_gradient():
        recv(("dn", 0), ("dx", 1), ("dx", 2), ("dx", 3))

        def finish(i, _):
            here = rows16(i)
            wide = x_ref[here].astype(F32)
            inv = lax.rsqrt(jnp.mean(wide * wide, axis=-1, keepdims=True) + norm_eps)
            unit = wide * inv
            dnormed = dn[0, c, here].astype(F32) + dn_sib[0, here].astype(F32)
            for k in range(3):
                dnormed += dn_in[k, here].astype(F32)
            dunit = dnormed * gain
            project = jnp.mean(dunit * unit, axis=-1, keepdims=True)
            grad_ref[here] = (tok_u[tok_rows(0, c, i * 16, 16)].astype(F32) + inv * (dunit - unit * project)).astype(BF16)
            return 0

        lax.fori_loop(0, TOK // 16, finish, 0)

    pass_w1(0)
    pass_neighbours("u")
    pass_w1(1)
    tokens(0)
    forward_one(0, 0)
    pass_w1(2)
    pass_w3(0)
    pass_w1(3)
    pass_w3(1)
    pass_w3(2)
    pass_neighbours("n")
    pass_w3(3)
    pass_v3(0)
    pass_w2(0)
    tokens(RIGHT)
    forward_one(0, RIGHT)
    pass_v3(1)
    tokens(LEFT)
    forward_one(0, LEFT)
    pass_opposite("u")
    pass_v3(2)
    pass_w2(1)
    grads_first(0)
    pass_opposite("n")
    pass_v3(3)
    tokens(OPPOSITE)
    forward_one(0, OPPOSITE)
    grads_last(0)
    y1(0, 0)
    yd(0, 0)
    pass_v2(0)
    all_w(1)
    forward_all(1, 2)
    pass_v2(1)
    y2(0, 0)
    grads(1, 1, 2)
    y1(3, 1)
    yd(3, 1)
    outer_send()
    grads(0, 1, 2)
    inner_send()
    far_w()
    forward_all(2)
    y2(3, 1)
    grads(0, 2)
    y1(2, 0)
    grads(1, 2)
    y1(2, 1)
    yd(2, 0)
    y3(0, 0)
    grads(1, 0)
    y3(3, 1)
    back(OPPOSITE)
    y2(2, 0)
    yd(2, 1)
    back(RIGHT)
    dn_pass(OPPOSITE, x_far)
    y2(2, 1)
    dn_pass(RIGHT, xr)
    inner_add()
    y1(1, 0)
    y3(2, 0)
    outer_add()
    y1(0, 1)
    back(LEFT)
    y3(2, 1)
    yd(1, 0)
    dn_pass(LEFT, xl)
    y2(1, 0)
    back(0)
    yd(0, 1)
    y2(0, 1)
    y3(1, 0)
    y3(0, 1)
    input_gradient()

    def arrived(slot):
        pieces, parts = [], summed[slot]
        for key, ref in (("za", za_in.at[slot - 1]), ("zb", zb_in.at[slot])):
            if (key, slot) not in copies:
                continue
            pieces.append(ref)
            if slot and parts in ([0], [1]):
                only[key, slot] = (mine == parts[0]) if key == "za" else (mine != parts[0])
                recv((key, slot), when=mine == parts[0])

                @pl.when(mine != parts[0])
                def _():
                    ref[...] = jnp.zeros((HALF, WIN), BF16)
            else:
                recv((key, slot))
        return pieces

    total[:, pl.ds(WIN, 128)] = jnp.zeros((16, 128), F32)
    early = arrived(3) + arrived(2)

    def add_early(i, _):
        here = rows16(i)
        rows = ysum[0, mine, here].astype(F32)
        for piece in early:
            rows += piece[here].astype(F32)
        acc[here, pl.ds(0, WIN)] = rows
        return 0

    lax.fori_loop(0, HALF // 16, add_early, 0)
    late = arrived(0) + arrived(1)

    def split(i, _):
        here = rows16(i)
        rows = acc[here, pl.ds(0, WIN)]
        for piece in late:
            rows += piece[here].astype(F32)
        total[:, pl.ds(0, WIN)] = rows
        turned = pltpu.roll(total[...], WIN + 128 - 32 * y, 1)
        for q in range(4):
            fin_st[q, here] = turned[:, 104 * q : 104 * q + 128].astype(BF16)
        return 0

    me = 2 * zl + c
    others = (("in", z_in, 2 * (1 - zl) + c), ("cross", z_cross, 2 * (1 - zl) + 1 - c), ("sib", sib, 2 * zl + 1 - c))
    for n, (first, rows) in enumerate(((0, 112), (112, 96))):
        lax.fori_loop(first // 16, (first + rows) // 16, split, 0)
        part = pl.ds(first, rows)
        for key, device, to in others:
            send(("f", key, n), fin_st.at[to, part], fin_in.at[me, part], device)

    def keep(i, _):
        fin_in[me, rows16(i)] = fin_st[me, rows16(i)]
        return 0

    lax.fori_loop(0, HALF // 16, keep, 0)
    recv(*[("f", key, n) for n in range(2) for key in ("sib", "in", "cross")])

    for q in range(2):
        rows = (HALF, 400 - HALF)[q]
        up_out[pl.ds(q * HALF, rows), :] = fin_in[q, pl.ds(0, rows)].astype(F32)[:, :104]
        down_out[pl.ds(q * HALF, rows), :] = fin_in[2 + q, pl.ds(0, rows)].astype(F32)[:, :104]
    for key, copy in copies.items():
        if key in only:
            pl.when(only[key])(copy.wait_send)
        else:
            copy.wait_send()


def body(inputs, gain, w_up, w_down, upstream):
    vmem = pl.BlockSpec(memory_space=pltpu.VMEM)
    hbm = pl.BlockSpec(memory_space=pl.ANY)
    input_grad, up_grad, down_grad = pl.pallas_call(
        kernel,
        out_shape=(
            jax.ShapeDtypeStruct((TOK, D), BF16),
            jax.ShapeDtypeStruct((400, 104), F32),
            jax.ShapeDtypeStruct((400, 104), F32),
        ),
        in_specs=[hbm, hbm, vmem, hbm, hbm],
        out_specs=(vmem,) * 3,
        scratch_shapes=[
            pltpu.VMEM((TOK, D), BF16),
            pltpu.VMEM((T, D), BF16),
            pltpu.VMEM((T, D), BF16),
            pltpu.VMEM((2, HID, D), BF16),
            pltpu.VMEM((HID, T), BF16),
            pltpu.VMEM((HID, T), BF16),
            pltpu.VMEM((HALF, D), F32),
            pltpu.VMEM((2, HID, D), BF16),
            pltpu.VMEM((4, 2, 2, HALF, 256), BF16),
            pltpu.VMEM((4, 2, 2, HALF, 256), BF16),
            pltpu.VMEM((4, 2, 2, HALF, WIN), BF16),
            pltpu.VMEM((4, 2, HALF, WIN), BF16),
            pltpu.VMEM((3, HALF, WIN), BF16),
            pltpu.VMEM((4, HALF, WIN), BF16),
            pltpu.VMEM((2, HALF, D), BF16),
            pltpu.VMEM((16, WIN + 128), F32),
            pltpu.VMEM((4, HALF, 128), BF16),
            pltpu.VMEM((4, HALF, 128), BF16),
            pltpu.VMEM((4, 2, TOK, D), BF16),
            pltpu.VMEM((4, TOK, D), BF16),
            pltpu.VMEM((3, TOK, D), BF16),
            pltpu.VMEM((3, TOK, D), BF16),
            pltpu.SemaphoreType.DMA((6,)),
            pltpu.SemaphoreType.DMA((N_SEM,)),
            pltpu.SemaphoreType.DMA((N_SEM,)),
        ],
        compiler_params=pltpu.CompilerParams(
            collective_id=1, has_side_effects=True, vmem_limit_bytes=53 * 2**20
        ),
        name="block_backward",
    )(inputs, upstream, gain, w_up.T, w_down)
    return input_grad, up_grad.T, down_grad


def solution(mesh):
    in_specs = (
        P(("dp", "tensor"), None),
        P(),
        P(None, "tensor"),
        P("tensor", None),
        P(("dp", "tensor"), None),
    )
    out_specs = (P(("dp", "tensor"), None), P("dp", "tensor"), P("tensor", "dp"))
    return jax.shard_map(body, mesh=mesh, in_specs=in_specs, out_specs=out_specs, check_vma=False)
```

```python
import jax
import jax.numpy as jnp
from jax import lax
from jax.experimental import pallas as pl
from jax.experimental.pallas import tpu as pltpu
from jax.sharding import PartitionSpec as P

MESH = pl.DeviceIdType.MESH
PRE = ("outer", "inner")
F32, BF16 = jnp.float32, jnp.bfloat16

norm_eps = 1e-06
D = 1664
TOK = 128
GROUP = 2 * TOK
T = 4 * GROUP
HALF = 208
HID = 4 * HALF
WIN = 512
CHUNKS = ((0, 64), (112, 48), (64, 48), (160, 48))
N_SEM = 112
RIGHT, LEFT, OPPOSITE = 1, 2, 3
GRAD_SCALE = float(32768) ** (-0.5)

FIRST = (0, HALF, 3 * HALF, 2 * HALF)


def gelu_parts(pre):
    cdf = 0.5 * (1.0 + lax.erf(pre * 0.7071067811865476))
    pdf = jnp.exp(-0.5 * pre * pre) * 0.3989422804014327
    return (pre * cdf, cdf + pre * pdf)


def place(x, y, z, c):
    x, y, z = (x + 8) % 4, (y + 8) % 4, (z + 16) % 8
    return (y * 4 + (z % 2) * 2 + c, x * 4 + z // 2)


def kernel(
    x_hbm, up_hbm, gain_ref, wu_hbm, wd_hbm, grad_ref, up_out, down_out,
    x_ref, tok_n, tok_u, w, hid, dpre, acc, g, yo_in, ya_st, nb_in, ysum, za_in, zb_in, pair_in, total, fin_st, fin_in,
    dn, dn_sib, dn_st, dn_in, local, ss, rs,
):
    dp, tensor = lax.axis_index("dp"), lax.axis_index("tensor")
    y, zl, c = dp // 4, (dp // 2) % 2, dp % 2
    x, z = tensor // 4, (tensor % 4) * 2 + zl
    step_out = 2 * zl - 1
    sib = place(x, y, z, 1 - c)
    xr, xl = place(x + 1, y, z, c), place(x - 1, y, z, c)
    x_far = place(x + 2, y, z, c)
    yr, yl = place(x, y + 1, z, c), place(x, y - 1, z, c)
    z_out, z_in = place(x, y, z + step_out, c), place(x, y, z - step_out, c)
    z_cross = place(x, y, z - step_out, 1 - c)
    z_same = {1: place(x, y, z + 2 * step_out, c), 2: place(x, y, z + 4, c), 3: place(x, y, z - 2 * step_out, c)}
    z_other = {0: z_in, 1: z_out, 2: place(x, y, z + 3 * step_out, c), 3: place(x, y, z - 3 * step_out, c)}
    kind = y % 2
    from_out, from_in = 16 + 96 * zl, 112 - 96 * zl
    mine = zl

    own = pl.ds(pl.multiple_of(c * TOK, 16), TOK)
    load_up = pltpu.make_async_copy(up_hbm, tok_u.at[own], local.at[0])
    load_up.start()
    barrier = pltpu.get_barrier_semaphore()
    peers = [sib, xr, xl, x_far, yr, yl, z_cross, *z_same.values(), *z_other.values()]
    for peer in peers:
        pl.semaphore_signal(barrier, inc=1, device_id=peer, device_id_type=MESH)

    copies, only, summed = {}, {}, {}

    def make(key, src, dst, device):
        i = len(copies)
        copies[key] = pltpu.make_async_remote_copy(
            src_ref=src, dst_ref=dst, send_sem=ss.at[i], recv_sem=rs.at[i], device_id=device, device_id_type=MESH
        )

    def start(key, when=None):
        if when is None:
            copies[key].start()
        else:
            only[key] = when
            pl.when(when)(copies[key].start)

    def send(key, src, dst, device, when=None):
        make(key, src, dst, device)
        start(key, when)

    def recv(*keys, when=None):
        for key in keys:
            if when is None:
                copies[key].wait_recv()
            else:
                pl.when(when)(copies[key].wait_recv)

    def tok_rows(group, core, first=0, rows=TOK):
        return pl.ds(pl.multiple_of(group * GROUP + core * TOK + first, 16), rows)

    load_w = [
        pltpu.make_async_copy(ref.at[pl.ds(pl.multiple_of(c * HALF, 16), 192)], w.at[k, pl.ds(0, 192)], local.at[1 + k])
        for k, ref in enumerate((wu_hbm, wd_hbm))
    ]
    load_rest = [
        pltpu.make_async_copy(ref.at[pl.ds(192, 16)], w.at[k, pl.ds(192, 16)], local.at[3 + k])
        for k, ref in enumerate((wu_hbm, wd_hbm))
    ]
    load_x = pltpu.make_async_copy(x_hbm, x_ref, local.at[5])
    for copy in load_w:
        copy.start()

    @pl.when(c == 0)
    def _():
        for copy in load_rest:
            copy.start()

    @pl.when(c == 1)
    def _():
        w[:, pl.ds(192, 16)] = jnp.zeros((2, 16, D), BF16)

    load_x.start()
    toks = {"u": tok_u, "n": tok_n}

    def send_own(a):
        send((a, "r"), toks[a].at[own], toks[a].at[tok_rows(LEFT, c)], xr)
        send((a, "l"), toks[a].at[own], toks[a].at[tok_rows(RIGHT, c)], xl)
        send((a, "s", 0), toks[a].at[own], toks[a].at[own], sib)

    load_up.wait()
    pl.semaphore_wait(barrier, len(peers))
    send_own("u")
    for copy in load_w:
        copy.wait()

    @pl.when(c == 0)
    def _():
        for copy in load_rest:
            copy.wait()

    def rows_of(slot, first, rows):
        return pl.ds(pl.multiple_of(FIRST[slot] + first, 16), rows)

    def chunk(slot, i):
        return rows_of(slot, *CHUNKS[i])

    for i in range(4):
        send(("w0", i), w.at[kind, chunk(0, i)], w.at[kind, chunk(1, i)], z_out)

    gain = gain_ref[...].astype(F32).reshape(1, D)
    load_x.wait()
    def norm(i, _):
        r = pl.ds(pl.multiple_of(i * 16, 16), 16)
        wide = x_ref[r].astype(F32)
        inv = lax.rsqrt(jnp.mean(wide * wide, axis=-1, keepdims=True) + norm_eps)
        tok_n[tok_rows(0, c, i * 16, 16)] = (wide * inv * gain).astype(BF16)
        return 0

    lax.fori_loop(0, TOK // 16, norm, 0, unroll=True)
    send_own("n")

    def pass_neighbours(a):
        t = toks[a]
        recv((a, "r"))
        send((a, "fr"), t.at[tok_rows(LEFT, c, 0, 64)], t.at[tok_rows(OPPOSITE, c, 0, 64)], xr)
        send((a, "s", LEFT), t.at[tok_rows(LEFT, c)], t.at[tok_rows(LEFT, c)], sib)
        recv((a, "l"))
        send((a, "fl"), t.at[tok_rows(RIGHT, c, 64, 64)], t.at[tok_rows(OPPOSITE, c, 64, 64)], xl)
        send((a, "s", RIGHT), t.at[tok_rows(RIGHT, c)], t.at[tok_rows(RIGHT, c)], sib)

    def pass_opposite(a):
        recv((a, "fr"), (a, "fl"))
        send((a, "s", OPPOSITE), toks[a].at[tok_rows(OPPOSITE, c)], toks[a].at[tok_rows(OPPOSITE, c)], sib)

    def tokens(group):
        recv(("u", "s", group), ("n", "s", group))

    def share(key, rows, peer):
        send(("wy", key), w.at[kind, rows], w.at[kind, rows], peer)

    def pass_w1(i):
        recv(("w0", i))
        send(("w1", i), w.at[kind, chunk(1, i)], w.at[kind, chunk(3, i)], z_in)
        share((1, i), chunk(1, i), (yr, yl, yr, yl)[i])

    def far_out(key, k, i):
        if i == 0:
            send((key, "x"), w.at[k, rows_of(3, 0, 16)], w.at[k, rows_of(2, 0, 16)], z_out, zl == 1)
            for n in range(2):
                here, there = rows_of(3, from_in + 48 * n, 48), rows_of(2, from_in + 48 * n, 48)
                make((key, n), w.at[k, here], w.at[k, there], z_out)
        pl.when(zl == 1 - i % 2)(copies[key, i // 2].start)

    def far_in(key, came, k, n):
        recv((came, n))
        rows = rows_of(2, from_out + 48 * n, 48)
        send((key, n), w.at[k, rows], w.at[k, rows], z_in)
        if n == 1:
            recv((came, "x"), when=zl == 0)
            rows = rows_of(2, 0, 16)
            send((key, "x"), w.at[k, rows], w.at[k, rows], z_in, zl == 0)

    def pass_w3(i):
        recv(("w1", i))
        far_out("w3", kind, i)
        share((3, i), chunk(3, i), (yl, yr, yl, yr)[i])

    def pass_w2(n):
        far_in("w2", "w3", kind, n)

    def pass_v3(i):
        recv(("wy", (3, i)))
        far_out("v3", 1 - kind, i)

    def pass_v2(n):
        far_in("v2", "v3", 1 - kind, n)

    def far_w():
        for key in ("w2", "v2"):
            recv((key, 0), (key, 1))
            recv((key, "x"), when=zl == 1)

    def all_w(slot):
        recv(*[key for key in copies if key[0] == "wy" and key[1][0] == slot])

    def forward(r, t):
        nt = (((1,), (1,)), ((), ()))
        pre = lax.dot_general(w[0, r], tok_n[t], nt, preferred_element_type=F32)
        dhidden = lax.dot_general(w[1, r], tok_u[t], nt, preferred_element_type=F32)
        hidden, slope = gelu_parts(pre)
        hid[r, t] = hidden.astype(BF16)
        dpre[r, t] = (dhidden * slope).astype(BF16)

    def forward_one(slot, group):
        forward(pl.ds(FIRST[slot], HALF), pl.ds(group * GROUP, GROUP))

    def forward_all(slot, slots=1):
        def one(i, _):
            forward(pl.ds(FIRST[slot], slots * HALF), pl.ds(pl.multiple_of(i * 512, 512), 512))
            return 0

        lax.fori_loop(0, 2, one, 0)

    def all_columns(columns):
        def tile(n, _):
            columns(pl.ds(pl.multiple_of(n * 512, 512), 512))
            return 0

        lax.fori_loop(0, 3, tile, 0)
        columns(pl.ds(1536, 128))

    def grads(kind, slot, slots=1):
        r = pl.ds(FIRST[slot], slots * HALF)
        left, right = ((dpre, tok_n), (hid, tok_u))[kind]

        def columns(cols):
            term = jnp.dot(left[r], right[:, cols], preferred_element_type=F32)
            g[kind, r, cols] = (term * GRAD_SCALE).astype(BF16)

        all_columns(columns)

    def grads_first(kind):
        r, t = pl.ds(0, HALF), pl.ds(0, 3 * GROUP)
        left, right = ((dpre, tok_n), (hid, tok_u))[kind]

        def columns(cols):
            acc[:, cols] = jnp.dot(left[r, t], right[t, cols], preferred_element_type=F32)

        all_columns(columns)

    def grads_last(kind):
        r, t = pl.ds(0, HALF), pl.ds(3 * GROUP, GROUP)
        left, right = ((dpre, tok_n), (hid, tok_u))[kind]

        def columns(cols):
            term = acc[:, cols] + jnp.dot(left[r, t], right[t, cols], preferred_element_type=F32)
            g[kind, r, cols] = (term * GRAD_SCALE).astype(BF16)

        all_columns(columns)

    def window(owner, first=0, cols=WIN):
        return pl.ds(pl.multiple_of(((owner + 8) % 4) * 384 + first, 128), cols)

    def rows16(i):
        return pl.ds(pl.multiple_of(i * 16, 16), 16)

    def slot16(slot, i):
        return pl.ds(pl.multiple_of(FIRST[slot] + i * 16, 16), 16)

    def kinds(part):
        return pl.ds(0, 2) if part[1] is None else pl.ds(mine if part[1] == "mine" else part[1], 1)

    def y1(*part):
        r, k = pl.ds(FIRST[part[0]], HALF), kinds(part)
        send(("yo", part, 0), g.at[k, r, window(y + 2, 0, 256)], yo_in.at[part[0], 0, k], yr)
        send(("yo", part, 1), g.at[k, r, window(y + 2, 256, 256)], yo_in.at[part[0], 1, k], yl)

    def yd(*part):
        r, k = pl.ds(FIRST[part[0]], HALF), kinds(part)
        left, right = pl.ds(0, 256), pl.ds(256, 256)
        send(("yd", part, 0), g.at[k, r, window(y + 1, 256, 256)], nb_in.at[part[0], 0, k, :, right], yr)
        send(("yd", part, 1), g.at[k, r, window(y - 1, 0, 256)], nb_in.at[part[0], 1, k, :, left], yl)

    def y2(*part):
        slot, k = part[0], kinds(part)
        for way, owner, first, peer in ((0, y + 1, 0, yr), (1, y - 1, 256, yl)):
            recv(("yo", part, way))
            cols = window(owner, first, 256)

            def add(i, _):
                here = rows16(i)
                ya_st[slot, way, k, here] = (
                    g[k, slot16(slot, i), cols].astype(F32) + yo_in[slot, way, k, here].astype(F32)
                ).astype(BF16)
                return 0

            lax.fori_loop(0, HALF // 16, add, 0, unroll=True)
            send(("ya", part, way), ya_st.at[slot, way, k], nb_in.at[slot, way, k, :, pl.ds(first, 256)], peer)

    def y3(*part):
        slot, k = part[0], kinds(part)
        recv(("yd", part, 0), ("yd", part, 1), ("ya", part, 0), ("ya", part, 1))
        cols = window(y)

        def add(i, _):
            here = rows16(i)
            ysum[slot, k, here] = (
                g[k, slot16(slot, i), cols].astype(F32)
                + nb_in[slot, 0, k, here].astype(F32)
                + nb_in[slot, 1, k, here].astype(F32)
            ).astype(BF16)
            return 0

        lax.fori_loop(0, HALF // 16, add, 0, unroll=True)
        summed.setdefault(slot, []).append(part[1])
        if part[1] == "mine":
            send(("za", slot), ysum.at[slot, mine], za_in.at[slot - 1], z_same[slot])
            return
        if ("zb", slot) not in copies:
            make(("zb", slot), ysum.at[slot, 1 - mine], zb_in.at[slot], z_other[slot])
            if slot:
                make(("za", slot), ysum.at[slot, mine], za_in.at[slot - 1], z_same[slot])
        for key, when in (("zb", mine != part[1]), ("za", mine == part[1])):
            if (key, slot) in copies:
                if part[1] is None:
                    copies[key, slot].start()
                else:
                    pl.when(when)(copies[key, slot].start)

    def presum_send(key, kind, slot, device):
        send(key, g.at[kind, pl.ds(FIRST[slot], HALF)], pair_in.at[PRE.index(key)], device)

    def presum_add(key, kind, slot):
        recv(key)

        def add(i, _):
            here = slot16(slot, i)
            g[kind, here] = (
                g[kind, here].astype(F32) + pair_in[PRE.index(key), rows16(i)].astype(F32)
            ).astype(BF16)
            return 0

        lax.fori_loop(0, HALF // 16, add, 0, unroll=True)

    def outer_send():
        presum_send("outer", 1, 1, z_out)

    def outer_add():
        presum_add("outer", 1, 0)

    def inner_send():
        presum_send("inner", 0, 3, z_in)

    def inner_add():
        presum_add("inner", 0, 1)

    def back(group):
        t = pl.ds(group * GROUP, GROUP)
        rows = dpre[:, t].T

        def columns(cols):
            part = jnp.dot(rows, w[0, :, cols], preferred_element_type=F32).astype(BF16)
            dn[group, 0, :, cols] = part[:TOK]
            dn[group, 1, :, cols] = part[TOK:]

        all_columns(columns)
        send(("dn", group), dn.at[group, 1 - c], dn_sib.at[group], sib)

    def dn_pass(group, peer):
        recv(("dn", group))

        def add(i, _):
            here = rows16(i)
            dn_st[group - 1, here] = (dn[group, c, here].astype(F32) + dn_sib[group, here].astype(F32)).astype(BF16)
            return 0

        lax.fori_loop(0, TOK // 16, add, 0, unroll=True)
        send(("dx", group), dn_st.at[group - 1], dn_in.at[group - 1], peer)

    def input_gradient():
        recv(("dn", 0), ("dx", 1), ("dx", 2), ("dx", 3))

        def finish(i, _):
            here = rows16(i)
            wide = x_ref[here].astype(F32)
            inv = lax.rsqrt(jnp.mean(wide * wide, axis=-1, keepdims=True) + norm_eps)
            unit = wide * inv
            dnormed = dn[0, c, here].astype(F32) + dn_sib[0, here].astype(F32)
            for k in range(3):
                dnormed += dn_in[k, here].astype(F32)
            dunit = dnormed * gain
            project = jnp.mean(dunit * unit, axis=-1, keepdims=True)
            grad_ref[here] = (tok_u[tok_rows(0, c, i * 16, 16)].astype(F32) + inv * (dunit - unit * project)).astype(BF16)
            return 0

        lax.fori_loop(0, TOK // 16, finish, 0)

    pass_w1(0)
    pass_neighbours("u")
    pass_w1(1)
    tokens(0)
    forward_one(0, 0)
    pass_w1(2)
    pass_w3(0)
    pass_w1(3)
    pass_w3(1)
    pass_w3(2)
    pass_neighbours("n")
    pass_w3(3)
    pass_v3(0)
    pass_w2(0)
    tokens(RIGHT)
    forward_one(0, RIGHT)
    pass_v3(1)
    tokens(LEFT)
    forward_one(0, LEFT)
    pass_opposite("u")
    pass_v3(2)
    pass_w2(1)
    grads_first(0)
    pass_opposite("n")
    pass_v3(3)
    tokens(OPPOSITE)
    forward_one(0, OPPOSITE)
    grads_last(0)
    y1(0, 0)
    yd(0, 0)
    pass_v2(0)
    all_w(1)
    forward_all(1, 2)
    pass_v2(1)
    y2(0, 0)
    grads(1, 1, 2)
    y1(3, 1)
    yd(3, 1)
    outer_send()
    grads(0, 1, 2)
    inner_send()
    far_w()
    forward_all(2)
    y2(3, 1)
    grads(0, 2)
    y1(2, 0)
    grads(1, 2)
    y1(2, 1)
    yd(2, 0)
    y3(0, 0)
    grads(1, 0)
    y3(3, 1)
    back(OPPOSITE)
    y2(2, 0)
    yd(2, 1)
    back(RIGHT)
    dn_pass(OPPOSITE, x_far)
    y2(2, 1)
    outer_add()
    y1(0, 1)
    dn_pass(RIGHT, xr)
    y3(2, 0)
    inner_add()
    y1(1, 0)
    back(LEFT)
    y3(2, 1)
    yd(0, 1)
    dn_pass(LEFT, xl)
    y2(0, 1)
    back(0)
    yd(1, 0)
    y2(1, 0)
    y3(0, 1)
    y3(1, 0)
    input_gradient()

    def arrived(slot):
        pieces, parts = [], summed[slot]
        for key, ref in (("za", za_in.at[slot - 1]), ("zb", zb_in.at[slot])):
            if (key, slot) not in copies:
                continue
            pieces.append(ref)
            if slot and parts in ([0], [1]):
                only[key, slot] = (mine == parts[0]) if key == "za" else (mine != parts[0])
                recv((key, slot), when=mine == parts[0])

                @pl.when(mine != parts[0])
                def _():
                    ref[...] = jnp.zeros((HALF, WIN), BF16)
            else:
                recv((key, slot))
        return pieces

    total[:, pl.ds(WIN, 128)] = jnp.zeros((16, 128), F32)
    early = arrived(3) + arrived(2)

    def add_early(i, _):
        here = rows16(i)
        rows = ysum[0, mine, here].astype(F32)
        for piece in early:
            rows += piece[here].astype(F32)
        acc[here, pl.ds(0, WIN)] = rows
        return 0

    lax.fori_loop(0, HALF // 16, add_early, 0, unroll=True)
    late = arrived(0) + arrived(1)

    def split(i, _):
        here = rows16(i)
        rows = acc[here, pl.ds(0, WIN)]
        for piece in late:
            rows += piece[here].astype(F32)
        total[:, pl.ds(0, WIN)] = rows
        turned = pltpu.roll(total[...], WIN + 128 - 32 * y, 1)
        for q in range(4):
            fin_st[q, here] = turned[:, 104 * q : 104 * q + 128].astype(BF16)
        return 0

    me = 2 * zl + c
    others = (("in", z_in, 2 * (1 - zl) + c), ("cross", z_cross, 2 * (1 - zl) + 1 - c), ("sib", sib, 2 * zl + 1 - c))
    for n, (first, rows) in enumerate(((0, 112), (112, 96))):
        lax.fori_loop(first // 16, (first + rows) // 16, split, 0, unroll=True)
        part = pl.ds(first, rows)
        for key, device, to in others:
            send(("f", key, n), fin_st.at[to, part], fin_in.at[me, part], device)

    def keep(i, _):
        fin_in[me, rows16(i)] = fin_st[me, rows16(i)]
        return 0

    lax.fori_loop(0, HALF // 16, keep, 0)
    recv(*[("f", key, n) for n in range(2) for key in ("sib", "in", "cross")])

    for q in range(2):
        rows = (HALF, 400 - HALF)[q]
        up_out[pl.ds(q * HALF, rows), :] = fin_in[q, pl.ds(0, rows)].astype(F32)[:, :104]
        down_out[pl.ds(q * HALF, rows), :] = fin_in[2 + q, pl.ds(0, rows)].astype(F32)[:, :104]
    for key, copy in copies.items():
        if key in only:
            pl.when(only[key])(copy.wait_send)
        else:
            copy.wait_send()


def body(inputs, gain, w_up, w_down, upstream):
    vmem = pl.BlockSpec(memory_space=pltpu.VMEM)
    hbm = pl.BlockSpec(memory_space=pl.ANY)
    input_grad, up_grad, down_grad = pl.pallas_call(
        kernel,
        out_shape=(
            jax.ShapeDtypeStruct((TOK, D), BF16),
            jax.ShapeDtypeStruct((400, 104), F32),
            jax.ShapeDtypeStruct((400, 104), F32),
        ),
        in_specs=[hbm, hbm, vmem, hbm, hbm],
        out_specs=(vmem,) * 3,
        scratch_shapes=[
            pltpu.VMEM((TOK, D), BF16),
            pltpu.VMEM((T, D), BF16),
            pltpu.VMEM((T, D), BF16),
            pltpu.VMEM((2, HID, D), BF16),
            pltpu.VMEM((HID, T), BF16),
            pltpu.VMEM((HID, T), BF16),
            pltpu.VMEM((HALF, D), F32),
            pltpu.VMEM((2, HID, D), BF16),
            pltpu.VMEM((4, 2, 2, HALF, 256), BF16),
            pltpu.VMEM((4, 2, 2, HALF, 256), BF16),
            pltpu.VMEM((4, 2, 2, HALF, WIN), BF16),
            pltpu.VMEM((4, 2, HALF, WIN), BF16),
            pltpu.VMEM((3, HALF, WIN), BF16),
            pltpu.VMEM((4, HALF, WIN), BF16),
            pltpu.VMEM((2, HALF, D), BF16),
            pltpu.VMEM((16, WIN + 128), F32),
            pltpu.VMEM((4, HALF, 128), BF16),
            pltpu.VMEM((4, HALF, 128), BF16),
            pltpu.VMEM((4, 2, TOK, D), BF16),
            pltpu.VMEM((4, TOK, D), BF16),
            pltpu.VMEM((3, TOK, D), BF16),
            pltpu.VMEM((3, TOK, D), BF16),
            pltpu.SemaphoreType.DMA((6,)),
            pltpu.SemaphoreType.DMA((N_SEM,)),
            pltpu.SemaphoreType.DMA((N_SEM,)),
        ],
        compiler_params=pltpu.CompilerParams(
            collective_id=1, has_side_effects=True, vmem_limit_bytes=53 * 2**20
        ),
        name="block_backward",
    )(inputs, upstream, gain, w_up.T, w_down)
    return input_grad, up_grad.T, down_grad


def solution(mesh):
    in_specs = (
        P(("dp", "tensor"), None),
        P(),
        P(None, "tensor"),
        P("tensor", None),
        P(("dp", "tensor"), None),
    )
    out_specs = (P(("dp", "tensor"), None), P("dp", "tensor"), P("tensor", "dp"))
    return jax.shard_map(body, mesh=mesh, in_specs=in_specs, out_specs=out_specs, check_vma=False)
```

```python
import jax
import jax.numpy as jnp
from jax import lax
from jax.experimental import pallas as pl
from jax.experimental.pallas import tpu as pltpu
from jax.sharding import PartitionSpec as P

MESH = pl.DeviceIdType.MESH
PRE = ("outer", "inner")
F32, BF16 = jnp.float32, jnp.bfloat16

norm_eps = 1e-06
D = 1664
TOK = 128
GROUP = 2 * TOK
T = 4 * GROUP
HALF = 208
HID = 4 * HALF
WIN = 512
CHUNKS = ((0, 64), (112, 48), (64, 48), (160, 48))
N_SEM = 112
RIGHT, LEFT, OPPOSITE = 1, 2, 3
GRAD_SCALE = float(32768) ** (-0.5)

FIRST = (0, HALF, 3 * HALF, 2 * HALF)


def gelu_parts(pre):
    cdf = 0.5 * (1.0 + lax.erf(pre * 0.7071067811865476))
    pdf = jnp.exp(-0.5 * pre * pre) * 0.3989422804014327
    return (pre * cdf, cdf + pre * pdf)


def place(x, y, z, c):
    x, y, z = (x + 8) % 4, (y + 8) % 4, (z + 16) % 8
    return (y * 4 + (z % 2) * 2 + c, x * 4 + z // 2)


def kernel(
    x_hbm, up_hbm, gain_ref, wu_hbm, wd_hbm, grad_ref, up_out, down_out,
    x_ref, tok_n, tok_u, w, hid, dpre, acc, g, yo_in, ya_st, nb_in, ysum, za_in, zb_in, pair_in, total, fin_st, fin_in,
    dn, dn_sib, dn_st, dn_in, local, ss, rs,
):
    dp, tensor = lax.axis_index("dp"), lax.axis_index("tensor")
    y, zl, c = dp // 4, (dp // 2) % 2, dp % 2
    x, z = tensor // 4, (tensor % 4) * 2 + zl
    step_out = 2 * zl - 1
    sib = place(x, y, z, 1 - c)
    xr, xl = place(x + 1, y, z, c), place(x - 1, y, z, c)
    x_far = place(x + 2, y, z, c)
    yr, yl = place(x, y + 1, z, c), place(x, y - 1, z, c)
    z_out, z_in = place(x, y, z + step_out, c), place(x, y, z - step_out, c)
    z_cross = place(x, y, z - step_out, 1 - c)
    z_same = {1: place(x, y, z + 2 * step_out, c), 2: place(x, y, z + 4, c), 3: place(x, y, z - 2 * step_out, c)}
    z_other = {0: z_in, 1: z_out, 2: place(x, y, z + 3 * step_out, c), 3: place(x, y, z - 3 * step_out, c)}
    kind = y % 2
    from_out, from_in = 16 + 96 * zl, 112 - 96 * zl
    mine = zl

    own = pl.ds(pl.multiple_of(c * TOK, 16), TOK)
    load_up = pltpu.make_async_copy(up_hbm, tok_u.at[own], local.at[0])
    load_up.start()
    barrier = pltpu.get_barrier_semaphore()
    peers = [sib, xr, xl, x_far, yr, yl, z_cross, *z_same.values(), *z_other.values()]
    for peer in peers:
        pl.semaphore_signal(barrier, inc=1, device_id=peer, device_id_type=MESH)

    copies, only, summed = {}, {}, {}

    def make(key, src, dst, device):
        i = len(copies)
        copies[key] = pltpu.make_async_remote_copy(
            src_ref=src, dst_ref=dst, send_sem=ss.at[i], recv_sem=rs.at[i], device_id=device, device_id_type=MESH
        )

    def start(key, when=None):
        if when is None:
            copies[key].start()
        else:
            only[key] = when
            pl.when(when)(copies[key].start)

    def send(key, src, dst, device, when=None):
        make(key, src, dst, device)
        start(key, when)

    def recv(*keys, when=None):
        for key in keys:
            if when is None:
                copies[key].wait_recv()
            else:
                pl.when(when)(copies[key].wait_recv)

    def tok_rows(group, core, first=0, rows=TOK):
        return pl.ds(pl.multiple_of(group * GROUP + core * TOK + first, 16), rows)

    load_w = [
        pltpu.make_async_copy(ref.at[pl.ds(pl.multiple_of(c * HALF, 16), 192)], w.at[k, pl.ds(0, 192)], local.at[1 + k])
        for k, ref in enumerate((wu_hbm, wd_hbm))
    ]
    load_rest = [
        pltpu.make_async_copy(ref.at[pl.ds(192, 16)], w.at[k, pl.ds(192, 16)], local.at[3 + k])
        for k, ref in enumerate((wu_hbm, wd_hbm))
    ]
    load_x = pltpu.make_async_copy(x_hbm, x_ref, local.at[5])
    for copy in load_w:
        copy.start()

    @pl.when(c == 0)
    def _():
        for copy in load_rest:
            copy.start()

    @pl.when(c == 1)
    def _():
        w[:, pl.ds(192, 16)] = jnp.zeros((2, 16, D), BF16)

    load_x.start()
    toks = {"u": tok_u, "n": tok_n}

    def send_own(a):
        send((a, "r"), toks[a].at[own], toks[a].at[tok_rows(LEFT, c)], xr)
        send((a, "l"), toks[a].at[own], toks[a].at[tok_rows(RIGHT, c)], xl)
        send((a, "s", 0), toks[a].at[own], toks[a].at[own], sib)

    load_up.wait()
    pl.semaphore_wait(barrier, len(peers))
    send_own("u")
    for copy in load_w:
        copy.wait()

    @pl.when(c == 0)
    def _():
        for copy in load_rest:
            copy.wait()

    def rows_of(slot, first, rows):
        return pl.ds(pl.multiple_of(FIRST[slot] + first, 16), rows)

    def chunk(slot, i):
        return rows_of(slot, *CHUNKS[i])

    for i in range(4):
        send(("w0", i), w.at[kind, chunk(0, i)], w.at[kind, chunk(1, i)], z_out)

    gain = gain_ref[...].astype(F32).reshape(1, D)
    load_x.wait()
    def norm(i, _):
        r = pl.ds(pl.multiple_of(i * 16, 16), 16)
        wide = x_ref[r].astype(F32)
        inv = lax.rsqrt(jnp.mean(wide * wide, axis=-1, keepdims=True) + norm_eps)
        tok_n[tok_rows(0, c, i * 16, 16)] = (wide * inv * gain).astype(BF16)
        return 0

    lax.fori_loop(0, TOK // 16, norm, 0, unroll=True)
    send_own("n")

    def pass_neighbours(a):
        t = toks[a]
        recv((a, "r"))
        send((a, "fr"), t.at[tok_rows(LEFT, c, 0, 64)], t.at[tok_rows(OPPOSITE, c, 0, 64)], xr)
        send((a, "s", LEFT), t.at[tok_rows(LEFT, c)], t.at[tok_rows(LEFT, c)], sib)
        recv((a, "l"))
        send((a, "fl"), t.at[tok_rows(RIGHT, c, 64, 64)], t.at[tok_rows(OPPOSITE, c, 64, 64)], xl)
        send((a, "s", RIGHT), t.at[tok_rows(RIGHT, c)], t.at[tok_rows(RIGHT, c)], sib)

    def pass_opposite(a):
        recv((a, "fr"), (a, "fl"))
        send((a, "s", OPPOSITE), toks[a].at[tok_rows(OPPOSITE, c)], toks[a].at[tok_rows(OPPOSITE, c)], sib)

    def tokens(group):
        recv(("u", "s", group), ("n", "s", group))

    def share(key, rows, peer):
        send(("wy", key), w.at[kind, rows], w.at[kind, rows], peer)

    def pass_w1(i):
        recv(("w0", i))
        send(("w1", i), w.at[kind, chunk(1, i)], w.at[kind, chunk(3, i)], z_in)
        share((1, i), chunk(1, i), (yr, yl, yr, yl)[i])

    def far_out(key, k, i):
        if i == 0:
            send((key, "x"), w.at[k, rows_of(3, 0, 16)], w.at[k, rows_of(2, 0, 16)], z_out, zl == 1)
            for n in range(2):
                here, there = rows_of(3, from_in + 48 * n, 48), rows_of(2, from_in + 48 * n, 48)
                make((key, n), w.at[k, here], w.at[k, there], z_out)
        pl.when(zl == 1 - i % 2)(copies[key, i // 2].start)

    def far_in(key, came, k, n):
        recv((came, n))
        rows = rows_of(2, from_out + 48 * n, 48)
        send((key, n), w.at[k, rows], w.at[k, rows], z_in)
        if n == 1:
            recv((came, "x"), when=zl == 0)
            rows = rows_of(2, 0, 16)
            send((key, "x"), w.at[k, rows], w.at[k, rows], z_in, zl == 0)

    def pass_w3(i):
        recv(("w1", i))
        far_out("w3", kind, i)
        share((3, i), chunk(3, i), (yl, yr, yl, yr)[i])

    def pass_w2(n):
        far_in("w2", "w3", kind, n)

    def pass_v3(i):
        recv(("wy", (3, i)))
        far_out("v3", 1 - kind, i)

    def pass_v2(n):
        far_in("v2", "v3", 1 - kind, n)

    def far_w():
        for key in ("w2", "v2"):
            recv((key, 0), (key, 1))
            recv((key, "x"), when=zl == 1)

    def all_w(slot):
        recv(*[key for key in copies if key[0] == "wy" and key[1][0] == slot])

    def forward(r, t):
        nt = (((1,), (1,)), ((), ()))
        pre = lax.dot_general(w[0, r], tok_n[t], nt, preferred_element_type=F32)
        dhidden = lax.dot_general(w[1, r], tok_u[t], nt, preferred_element_type=F32)
        hidden, slope = gelu_parts(pre)
        hid[r, t] = hidden.astype(BF16)
        dpre[r, t] = (dhidden * slope).astype(BF16)

    def forward_one(slot, group):
        forward(pl.ds(FIRST[slot], HALF), pl.ds(group * GROUP, GROUP))

    def forward_all(slot, slots=1):
        def one(i, _):
            forward(pl.ds(FIRST[slot], slots * HALF), pl.ds(pl.multiple_of(i * 512, 512), 512))
            return 0

        lax.fori_loop(0, 2, one, 0, unroll=True)

    def all_columns(columns):
        def tile(n, _):
            columns(pl.ds(pl.multiple_of(n * 512, 512), 512))
            return 0

        lax.fori_loop(0, 3, tile, 0, unroll=True)
        columns(pl.ds(1536, 128))

    def grads(kind, slot, slots=1):
        r = pl.ds(FIRST[slot], slots * HALF)
        left, right = ((dpre, tok_n), (hid, tok_u))[kind]

        def columns(cols):
            term = jnp.dot(left[r], right[:, cols], preferred_element_type=F32)
            g[kind, r, cols] = (term * GRAD_SCALE).astype(BF16)

        all_columns(columns)

    def grads_first(kind):
        r, t = pl.ds(0, HALF), pl.ds(0, 3 * GROUP)
        left, right = ((dpre, tok_n), (hid, tok_u))[kind]

        def columns(cols):
            acc[:, cols] = jnp.dot(left[r, t], right[t, cols], preferred_element_type=F32)

        all_columns(columns)

    def grads_last(kind):
        r, t = pl.ds(0, HALF), pl.ds(3 * GROUP, GROUP)
        left, right = ((dpre, tok_n), (hid, tok_u))[kind]

        def columns(cols):
            term = acc[:, cols] + jnp.dot(left[r, t], right[t, cols], preferred_element_type=F32)
            g[kind, r, cols] = (term * GRAD_SCALE).astype(BF16)

        all_columns(columns)

    def window(owner, first=0, cols=WIN):
        return pl.ds(pl.multiple_of(((owner + 8) % 4) * 384 + first, 128), cols)

    def rows16(i):
        return pl.ds(pl.multiple_of(i * 16, 16), 16)

    def slot16(slot, i):
        return pl.ds(pl.multiple_of(FIRST[slot] + i * 16, 16), 16)

    def kinds(part):
        return pl.ds(0, 2) if part[1] is None else pl.ds(mine if part[1] == "mine" else part[1], 1)

    def y1(*part):
        r, k = pl.ds(FIRST[part[0]], HALF), kinds(part)
        send(("yo", part, 0), g.at[k, r, window(y + 2, 0, 256)], yo_in.at[part[0], 0, k], yr)
        send(("yo", part, 1), g.at[k, r, window(y + 2, 256, 256)], yo_in.at[part[0], 1, k], yl)

    def yd(*part):
        r, k = pl.ds(FIRST[part[0]], HALF), kinds(part)
        left, right = pl.ds(0, 256), pl.ds(256, 256)
        send(("yd", part, 0), g.at[k, r, window(y + 1, 256, 256)], nb_in.at[part[0], 0, k, :, right], yr)
        send(("yd", part, 1), g.at[k, r, window(y - 1, 0, 256)], nb_in.at[part[0], 1, k, :, left], yl)

    def y2(*part):
        slot, k = part[0], kinds(part)
        for way, owner, first, peer in ((0, y + 1, 0, yr), (1, y - 1, 256, yl)):
            recv(("yo", part, way))
            cols = window(owner, first, 256)

            def add(i, _):
                here = rows16(i)
                ya_st[slot, way, k, here] = (
                    g[k, slot16(slot, i), cols].astype(F32) + yo_in[slot, way, k, here].astype(F32)
                ).astype(BF16)
                return 0

            lax.fori_loop(0, HALF // 16, add, 0, unroll=True)
            send(("ya", part, way), ya_st.at[slot, way, k], nb_in.at[slot, way, k, :, pl.ds(first, 256)], peer)

    def y3(*part):
        slot, k = part[0], kinds(part)
        recv(("yd", part, 0), ("yd", part, 1), ("ya", part, 0), ("ya", part, 1))
        cols = window(y)

        def add(i, _):
            here = rows16(i)
            ysum[slot, k, here] = (
                g[k, slot16(slot, i), cols].astype(F32)
                + nb_in[slot, 0, k, here].astype(F32)
                + nb_in[slot, 1, k, here].astype(F32)
            ).astype(BF16)
            return 0

        lax.fori_loop(0, HALF // 16, add, 0, unroll=True)
        summed.setdefault(slot, []).append(part[1])
        if part[1] == "mine":
            send(("za", slot), ysum.at[slot, mine], za_in.at[slot - 1], z_same[slot])
            return
        if ("zb", slot) not in copies:
            make(("zb", slot), ysum.at[slot, 1 - mine], zb_in.at[slot], z_other[slot])
            if slot:
                make(("za", slot), ysum.at[slot, mine], za_in.at[slot - 1], z_same[slot])
        for key, when in (("zb", mine != part[1]), ("za", mine == part[1])):
            if (key, slot) in copies:
                if part[1] is None:
                    copies[key, slot].start()
                else:
                    pl.when(when)(copies[key, slot].start)

    def presum_send(key, kind, slot, device):
        send(key, g.at[kind, pl.ds(FIRST[slot], HALF)], pair_in.at[PRE.index(key)], device)

    def presum_add(key, kind, slot):
        recv(key)

        def add(i, _):
            here = slot16(slot, i)
            g[kind, here] = (
                g[kind, here].astype(F32) + pair_in[PRE.index(key), rows16(i)].astype(F32)
            ).astype(BF16)
            return 0

        lax.fori_loop(0, HALF // 16, add, 0, unroll=True)

    def outer_send():
        presum_send("outer", 1, 1, z_out)

    def outer_add():
        presum_add("outer", 1, 0)

    def inner_send():
        presum_send("inner", 0, 3, z_in)

    def inner_add():
        presum_add("inner", 0, 1)

    def back(group):
        t = pl.ds(group * GROUP, GROUP)
        rows = dpre[:, t].T

        def columns(cols):
            part = jnp.dot(rows, w[0, :, cols], preferred_element_type=F32).astype(BF16)
            dn[group, 0, :, cols] = part[:TOK]
            dn[group, 1, :, cols] = part[TOK:]

        all_columns(columns)
        send(("dn", group), dn.at[group, 1 - c], dn_sib.at[group], sib)

    def dn_pass(group, peer):
        recv(("dn", group))

        def add(i, _):
            here = rows16(i)
            dn_st[group - 1, here] = (dn[group, c, here].astype(F32) + dn_sib[group, here].astype(F32)).astype(BF16)
            return 0

        lax.fori_loop(0, TOK // 16, add, 0, unroll=True)
        send(("dx", group), dn_st.at[group - 1], dn_in.at[group - 1], peer)

    def input_gradient():
        recv(("dn", 0), ("dx", 1), ("dx", 2), ("dx", 3))

        def finish(i, _):
            here = rows16(i)
            wide = x_ref[here].astype(F32)
            inv = lax.rsqrt(jnp.mean(wide * wide, axis=-1, keepdims=True) + norm_eps)
            unit = wide * inv
            dnormed = dn[0, c, here].astype(F32) + dn_sib[0, here].astype(F32)
            for k in range(3):
                dnormed += dn_in[k, here].astype(F32)
            dunit = dnormed * gain
            project = jnp.mean(dunit * unit, axis=-1, keepdims=True)
            grad_ref[here] = (tok_u[tok_rows(0, c, i * 16, 16)].astype(F32) + inv * (dunit - unit * project)).astype(BF16)
            return 0

        lax.fori_loop(0, TOK // 16, finish, 0)

    pass_w1(0)
    pass_neighbours("u")
    pass_w1(1)
    tokens(0)
    forward_one(0, 0)
    pass_w1(2)
    pass_w3(0)
    pass_w1(3)
    pass_w3(1)
    pass_w3(2)
    pass_neighbours("n")
    pass_w3(3)
    pass_v3(0)
    pass_w2(0)
    tokens(RIGHT)
    forward_one(0, RIGHT)
    pass_v3(1)
    tokens(LEFT)
    forward_one(0, LEFT)
    pass_opposite("u")
    pass_v3(2)
    pass_w2(1)
    grads_first(0)
    pass_opposite("n")
    pass_v3(3)
    tokens(OPPOSITE)
    forward_one(0, OPPOSITE)
    grads_last(0)
    y1(0, 0)
    yd(0, 0)
    pass_v2(0)
    all_w(1)
    forward_all(1, 2)
    pass_v2(1)
    y2(0, 0)
    grads(1, 1, 2)
    y1(3, 1)
    yd(3, 1)
    outer_send()
    grads(0, 1, 2)
    inner_send()
    far_w()
    forward_all(2)
    y2(3, 1)
    grads(0, 2)
    y1(2, 0)
    grads(1, 2)
    y1(2, 1)
    yd(2, 0)
    y3(0, 0)
    grads(1, 0)
    y3(3, 1)
    back(OPPOSITE)
    y2(2, 0)
    yd(2, 1)
    back(RIGHT)
    dn_pass(OPPOSITE, x_far)
    y2(2, 1)
    outer_add()
    y1(0, 1)
    dn_pass(RIGHT, xr)
    y3(2, 0)
    inner_add()
    y1(1, 0)
    back(LEFT)
    y3(2, 1)
    yd(0, 1)
    dn_pass(LEFT, xl)
    y2(0, 1)
    back(0)
    yd(1, 0)
    y2(1, 0)
    y3(0, 1)
    y3(1, 0)
    input_gradient()

    def arrived(slot):
        pieces, parts = [], summed[slot]
        for key, ref in (("za", za_in.at[slot - 1]), ("zb", zb_in.at[slot])):
            if (key, slot) not in copies:
                continue
            pieces.append(ref)
            if slot and parts in ([0], [1]):
                only[key, slot] = (mine == parts[0]) if key == "za" else (mine != parts[0])
                recv((key, slot), when=mine == parts[0])

                @pl.when(mine != parts[0])
                def _():
                    ref[...] = jnp.zeros((HALF, WIN), BF16)
            else:
                recv((key, slot))
        return pieces

    total[:, pl.ds(WIN, 128)] = jnp.zeros((16, 128), F32)
    early = arrived(3) + arrived(2)

    def add_early(i, _):
        here = rows16(i)
        rows = ysum[0, mine, here].astype(F32)
        for piece in early:
            rows += piece[here].astype(F32)
        acc[here, pl.ds(0, WIN)] = rows
        return 0

    lax.fori_loop(0, HALF // 16, add_early, 0, unroll=True)
    late = arrived(0) + arrived(1)

    def split(i, _):
        here = rows16(i)
        rows = acc[here, pl.ds(0, WIN)]
        for piece in late:
            rows += piece[here].astype(F32)
        total[:, pl.ds(0, WIN)] = rows
        turned = pltpu.roll(total[...], WIN + 128 - 32 * y, 1)
        for q in range(4):
            fin_st[q, here] = turned[:, 104 * q : 104 * q + 128].astype(BF16)
        return 0

    me = 2 * zl + c
    others = (("in", z_in, 2 * (1 - zl) + c), ("cross", z_cross, 2 * (1 - zl) + 1 - c), ("sib", sib, 2 * zl + 1 - c))
    for n, (first, rows) in enumerate(((0, 112), (112, 96))):
        lax.fori_loop(first // 16, (first + rows) // 16, split, 0, unroll=True)
        part = pl.ds(first, rows)
        for key, device, to in others:
            send(("f", key, n), fin_st.at[to, part], fin_in.at[me, part], device)

    def keep(i, _):
        fin_in[me, rows16(i)] = fin_st[me, rows16(i)]
        return 0

    lax.fori_loop(0, HALF // 16, keep, 0)
    recv(*[("f", key, n) for n in range(2) for key in ("sib", "in", "cross")])

    for q in range(2):
        rows = (HALF, 400 - HALF)[q]
        up_out[pl.ds(q * HALF, rows), :] = fin_in[q, pl.ds(0, rows)].astype(F32)[:, :104]
        down_out[pl.ds(q * HALF, rows), :] = fin_in[2 + q, pl.ds(0, rows)].astype(F32)[:, :104]
    for key, copy in copies.items():
        if key in only:
            pl.when(only[key])(copy.wait_send)
        else:
            copy.wait_send()


def body(inputs, gain, w_up, w_down, upstream):
    vmem = pl.BlockSpec(memory_space=pltpu.VMEM)
    hbm = pl.BlockSpec(memory_space=pl.ANY)
    input_grad, up_grad, down_grad = pl.pallas_call(
        kernel,
        out_shape=(
            jax.ShapeDtypeStruct((TOK, D), BF16),
            jax.ShapeDtypeStruct((400, 104), F32),
            jax.ShapeDtypeStruct((400, 104), F32),
        ),
        in_specs=[hbm, hbm, vmem, hbm, hbm],
        out_specs=(vmem,) * 3,
        scratch_shapes=[
            pltpu.VMEM((TOK, D), BF16),
            pltpu.VMEM((T, D), BF16),
            pltpu.VMEM((T, D), BF16),
            pltpu.VMEM((2, HID, D), BF16),
            pltpu.VMEM((HID, T), BF16),
            pltpu.VMEM((HID, T), BF16),
            pltpu.VMEM((HALF, D), F32),
            pltpu.VMEM((2, HID, D), BF16),
            pltpu.VMEM((4, 2, 2, HALF, 256), BF16),
            pltpu.VMEM((4, 2, 2, HALF, 256), BF16),
            pltpu.VMEM((4, 2, 2, HALF, WIN), BF16),
            pltpu.VMEM((4, 2, HALF, WIN), BF16),
            pltpu.VMEM((3, HALF, WIN), BF16),
            pltpu.VMEM((4, HALF, WIN), BF16),
            pltpu.VMEM((2, HALF, D), BF16),
            pltpu.VMEM((16, WIN + 128), F32),
            pltpu.VMEM((4, HALF, 128), BF16),
            pltpu.VMEM((4, HALF, 128), BF16),
            pltpu.VMEM((4, 2, TOK, D), BF16),
            pltpu.VMEM((4, TOK, D), BF16),
            pltpu.VMEM((3, TOK, D), BF16),
            pltpu.VMEM((3, TOK, D), BF16),
            pltpu.SemaphoreType.DMA((6,)),
            pltpu.SemaphoreType.DMA((N_SEM,)),
            pltpu.SemaphoreType.DMA((N_SEM,)),
        ],
        compiler_params=pltpu.CompilerParams(
            collective_id=1, has_side_effects=True, vmem_limit_bytes=53 * 2**20
        ),
        name="block_backward",
    )(inputs, upstream, gain, w_up.T, w_down)
    return input_grad, up_grad.T, down_grad


def solution(mesh):
    in_specs = (
        P(("dp", "tensor"), None),
        P(),
        P(None, "tensor"),
        P("tensor", None),
        P(("dp", "tensor"), None),
    )
    out_specs = (P(("dp", "tensor"), None), P("dp", "tensor"), P("tensor", "dp"))
    return jax.shard_map(body, mesh=mesh, in_specs=in_specs, out_specs=out_specs, check_vma=False)
```
